32 devices in a mesh: groups: 2 (over x), seq: 16 (over z, y, core).
Axes of the slice: x: 2, y: 2, z: 4, core: 2. Of those that a mesh axis runs over, the one named last changes fastest.
Arguments:
- images: bfloat16 [4, 2048, 3072], P('groups', 'seq'), parts along dimension 0, may hold values from -6 to 6
- w_qkv: bfloat16 [3072, 1152], replicated, may hold values from -0.109375 to 0.109375
- b_qkv: float32 [1152], replicated, may hold values from -3 to 3
- q_gain: float32 [128], replicated, may hold values from 0.5 to 2.5
- k_gain: float32 [128], replicated, may hold values from 0.5 to 2.5
- key_basis: float32 [3, 128, 32], replicated, may hold values from -0.5 to 0.5
- value_basis: float32 [3, 128, 32], replicated, may hold values from -0.5 to 0.5
- centers: float32 [4, 2, 3, 128], P('groups'), parts along dimension 0, may hold values from -22 to 22
- refresh: int32 [2, 3], replicated, may hold values 0 or 1
- w_out: bfloat16 [384, 3072], replicated, may hold values from -0.3125 to 0.3125
Outputs:
- mixed: bfloat16 [4, 2048, 3072], P('groups', 'seq'), parts along dimension 0
- new_centers: float32 [4, 2, 3, 128], P('groups'), parts along dimension 0
The draws below stay inside these ranges and needn't reach their ends.
There are 2 independent parts, one for each index of `groups`. The reference program is written for one: setup_inputs(seed, part) draws one part's arguments, and reference() takes and returns one part's arrays. A program takes and returns all parts, laid end to end along the dimension named above; an argument that names none is the same for every part. Nothing has to cross between parts.
All inputs are finite; a program needn't handle non-finite values.
Results may differ from the reference program's by a relative error of at most 0.0051.
Values may be sent and summed in bfloat16 or wider, within the bound.
No kernel may reach another device: no remote copies, remote signals or barrier semaphores. Data moves between devices by JAX's collectives and lax.ppermute only.
A program may use at most 64 MiB of HBM per device.

```python
import math
import jax
import jax.numpy as jnp
from jax import lax

WIDTH = 3072
HEAD_DIM = 128
HEADS_DEV = 3
CODE_RANK = 32
SAMPLES = 2
TOK_DEV = 128
LENGTH = 2048
N_SEQ = 16


def draw_b_qkv(key, part):
    total = 3 * HEADS_DEV * HEAD_DIM
    drawn = 0.5 * jax.random.truncated_normal(jax.random.fold_in(key, 11), -6.0, 6.0, (total,), jnp.float32)
    return drawn


def draw_centers(key, part):
    shape = (SAMPLES, 2, HEADS_DEV, HEAD_DIM)
    return 0.5 * jax.random.truncated_normal(jax.random.fold_in(key, 24), -6.0, 6.0, shape, jnp.float32)


def with_ends(result, key, low, high):
    place = [jax.random.randint(jax.random.fold_in(key, axis), (), 0, length) for axis, length in enumerate(result.shape)]
    main_axis = result.shape.index(max(result.shape))
    next_to = place[:main_axis] + [(place[main_axis] + 1) % result.shape[main_axis]] + place[main_axis + 1:]
    return result.at[tuple(place)].set(low).at[tuple(next_to)].set(high)


def shard_levels(own_key, dims, cuts, low, top_value):
    def one(axis_at, parts):
        steps = jax.random.uniform(jax.random.fold_in(jax.random.fold_in(own_key, 6), axis_at), (parts,), jnp.float32, low / len(cuts), top_value / len(cuts))
        return jnp.repeat(jnp.exp(steps), dims[axis_at] // parts).reshape((-1,) + (1,) * (len(dims) - axis_at - 1))

    level = one(*cuts[0])
    for cut in cuts[1:]:
        level = level * one(*cut)
    return level


def noise(key, dims, spread, most, split=(), kind=jnp.bfloat16):
    array = jax.random.normal(key, dims, jnp.float32) * spread
    if len(split) > 0:
        array = shard_levels(key, dims, split, -0.22, 0.18) * array
    return jnp.clip(array, min=-most, max=most).astype(kind)


def setup_inputs(seed: int = 0, part: int = 0) -> dict:
    splits = jax.random.split(jax.random.key(seed), 11)
    part_keys = jax.random.split(jax.random.fold_in(splits[10], part), 11)
    images = noise(part_keys[0], (SAMPLES, LENGTH, WIDTH), 1.0, 6.0, ((1, 16),))
    w_qkv = noise(splits[1], (WIDTH, 3 * HEADS_DEV * HEAD_DIM), WIDTH ** -0.5, 0.109375)
    b_qkv = draw_b_qkv(jax.random.fold_in(splits[10], 71), part)
    q_gain = jnp.clip(jnp.exp(jax.random.uniform(splits[3], (HEAD_DIM,), jnp.float32, math.log(0.5), math.log(2.5))), 0.5, 2.5)
    k_gain = jnp.clip(jnp.exp(jax.random.uniform(splits[4], (HEAD_DIM,), jnp.float32, math.log(0.5), math.log(2.5))), 0.5, 2.5)
    key_basis = noise(splits[5], (HEADS_DEV, HEAD_DIM, CODE_RANK), HEAD_DIM ** -0.5, 0.5, (), jnp.float32)
    value_basis = noise(splits[6], (HEADS_DEV, HEAD_DIM, CODE_RANK), HEAD_DIM ** -0.5, 0.5, (), jnp.float32)
    centers = draw_centers(jax.random.fold_in(jax.random.fold_in(splits[10], part), 71), part)
    refresh = with_ends((jax.random.randint(splits[8], (2, HEADS_DEV), 0, 2) < 1).astype(jnp.int32), jax.random.fold_in(splits[8], 1), 0, 1)
    w_out = noise(splits[9], (HEADS_DEV * HEAD_DIM, WIDTH), (HEADS_DEV * HEAD_DIM) ** -0.5, 0.3125)
    return {"images": images, "w_qkv": w_qkv, "b_qkv": b_qkv, "q_gain": q_gain, "k_gain": k_gain, "key_basis": key_basis, "value_basis": value_basis, "centers": centers, "refresh": refresh, "w_out": w_out}


epsilon = 1e-06
highest = lax.Precision.HIGHEST

def normalize(values, gain):
    mean_square = lax.optimization_barrier(jnp.mean(values * values, axis=-1, keepdims=True))
    return values * lax.rsqrt(mean_square + epsilon) * gain

def reference(images, w_qkv, b_qkv, q_gain, k_gain, key_basis, value_basis, centers, refresh, w_out):
    sample_count, length, model_width = images.shape
    head_count, head_dim, code_rank = key_basis.shape
    factor = 1.0 / math.sqrt(head_dim)
    flat_images = images.reshape(sample_count * length, model_width)
    projected = jnp.dot(flat_images, w_qkv, preferred_element_type=jnp.float32) + b_qkv
    projected = projected.reshape(sample_count, length, 3, head_count, head_dim)
    query = normalize(projected[:, :, 0], q_gain)
    keys = normalize(projected[:, :, 1], k_gain)
    values = projected[:, :, 2]
    key_center = centers[:, 0]
    value_center = centers[:, 1]
    key_codes = jnp.einsum('blhd,hdr->blhr', keys - key_center[:, None], key_basis, precision=highest).astype(jnp.bfloat16)
    value_codes = jnp.einsum('blhd,hdr->blhr', values - value_center[:, None], value_basis, precision=highest).astype(jnp.bfloat16)
    key_rebuilt = jnp.einsum('blhr,hdr->blhd', key_codes.astype(jnp.float32), key_basis, precision=highest) + key_center[:, None]
    value_rebuilt = jnp.einsum('blhr,hdr->blhd', value_codes.astype(jnp.float32), value_basis, precision=highest) + value_center[:, None]
    fresh_means = jnp.stack([lax.optimization_barrier(jnp.mean(keys, axis=1)), lax.optimization_barrier(jnp.mean(values, axis=1))], axis=1)
    new_centers = jnp.where(refresh[None, :, :, None] == 1, fresh_means, centers)
    columns = jnp.arange(length, dtype=jnp.int32)

    def attend_block(block_index):
        first_row = (block_index * TOK_DEV).astype(jnp.int32)
        query_block = lax.dynamic_slice_in_dim(query, first_row, TOK_DEV, 1)
        key_block = lax.dynamic_slice_in_dim(keys, first_row, TOK_DEV, 1)
        value_block = lax.dynamic_slice_in_dim(values, first_row, TOK_DEV, 1)
        far_scores = jnp.einsum('bqhd,bshd->bhqs', query_block, key_rebuilt, precision=highest) * factor
        owned = (columns >= first_row) & (columns < first_row + TOK_DEV)
        far_scores = jnp.where(owned[None, None, None, :], -jnp.inf, far_scores)
        near_scores = jnp.einsum('bqhd,bshd->bhqs', query_block, key_block, precision=highest) * factor
        row_max = jnp.maximum(lax.optimization_barrier(jnp.max(far_scores, axis=-1)), lax.optimization_barrier(jnp.max(near_scores, axis=-1)))
        far_weights = jnp.exp(far_scores - row_max[..., None])
        near_weights = jnp.exp(near_scores - row_max[..., None])
        row_sum = lax.optimization_barrier(jnp.sum(far_weights, axis=-1)) + lax.optimization_barrier(jnp.sum(near_weights, axis=-1))
        weighted = jnp.einsum('bhqs,bshd->bhqd', far_weights, value_rebuilt, precision=highest)
        weighted = weighted + jnp.einsum('bhqs,bshd->bhqd', near_weights, value_block, precision=highest)
        return weighted / row_sum[..., None]
    blocks = lax.map(attend_block, jnp.arange(N_SEQ, dtype=jnp.int32))
    attended = blocks.transpose(1, 0, 3, 2, 4).reshape(sample_count * length, head_count * head_dim).astype(jnp.bfloat16)
    mixed = jnp.dot(attended, w_out, preferred_element_type=jnp.float32).astype(jnp.bfloat16)
    return (mixed.reshape(sample_count, length, model_width), new_centers)
```

```python
import functools
import math

import jax
import jax.numpy as jnp
from jax import lax
from jax.experimental import pallas as pl
from jax.experimental.pallas import tpu as pltpu
from jax.sharding import PartitionSpec as P

epsilon = 1e-06
f32 = jnp.float32
bf16 = jnp.bfloat16
SUM_ROWS = 16
NT = (((1,), (1,)), ((), ()))
NN = (((1,), (0,)), ((), ()))


def dot(a, b, dims=NN):
    return lax.dot_general(a, b, dims, preferred_element_type=f32)


def split(x):
    high = x.astype(bf16)
    low = (x - high.astype(f32)).astype(bf16)
    return high, low


def dot3(a, b, dims=NN):
    return dot(a[0], b[0], dims) + (dot(a[0], b[1], dims) + dot(a[1], b[0], dims))


def lane_ids(rows, lanes):
    return lax.broadcasted_iota(jnp.int32, (rows, lanes), 1)


def key_lane(sample, head, rank):
    return head * rank if sample == 0 else (head + 1) * rank


def value_lane(sample, head, rank, heads):
    if head == 0:
        return heads * rank if sample == 0 else 0
    return ((heads - 1) * sample + head - 1) * rank


def free_lane(sample, rank):
    return 2 * rank if sample == 0 else rank


def project_kernel(
    images_ref, w_ref, b_ref, qg_ref, kg_ref, kb_ref, vb_ref, centers_ref,
    payload_ref, query_ref, qkv_ref, acc_ref, tiles_h, tiles_l, last_h, last_l, sums_ref,
    *, samples, tokens, heads, dim, rank, log_factor,
):
    step = pl.program_id(0)
    width = heads * dim
    part = dot(images_ref[...], w_ref[...])

    @pl.when(step == 0)
    def _():
        acc_ref[...] = part
        tiles_h[...] = jnp.zeros_like(tiles_h)
        tiles_l[...] = jnp.zeros_like(tiles_l)
        last_h[...] = jnp.zeros_like(last_h)
        last_l[...] = jnp.zeros_like(last_l)
        sums_ref[...] = jnp.zeros_like(sums_ref)
        for h in range(heads):
            kh, kl = split(kb_ref[h])
            vh, vl = split(vb_ref[h])
            for b in range(samples):
                at = key_lane(b, h, rank)
                tiles_h[b, at : at + rank, h * dim : (h + 1) * dim] = kh
                tiles_l[b, at : at + rank, h * dim : (h + 1) * dim] = kl
                at = value_lane(b, h, rank, heads)
                if h == 0:
                    tiles_h[b, at : at + rank, width : width + dim] = vh
                    tiles_l[b, at : at + rank, width : width + dim] = vl
                else:
                    last_h[at : at + rank, (h - 1) * dim : h * dim] = vh
                    last_l[at : at + rank, (h - 1) * dim : h * dim] = vl

    @pl.when(step > 0)
    def _():
        acc_ref[...] += part

    @pl.when(step == pl.num_programs(0) - 1)
    def _():
        def normed(column, gain):
            x = acc_ref[:, column : column + dim] + b_ref[:, column : column + dim]
            mean_square = jnp.mean(x * x, axis=-1, keepdims=True)
            return x * lax.rsqrt(mean_square + epsilon) * gain

        queries, keys, values = [], [], []
        for h in range(heads):
            at = h * dim
            q = normed(at, qg_ref[...])
            k = normed(width + at, kg_ref[...])
            v = acc_ref[:, 2 * width + at : 2 * width + at + dim]
            v = v + b_ref[:, 2 * width + at : 2 * width + at + dim]
            queries.append(q)
            keys.append(k)
            values.append(v)
            for b in range(samples):
                rows = slice(b * tokens, (b + 1) * tokens)
                row = (b * heads + h) * 2
                sums_ref[row : row + 1, :] = jnp.sum(k[rows], axis=0, keepdims=True)
                sums_ref[row + 1 : row + 2, :] = jnp.sum(v[rows], axis=0, keepdims=True)
        rest = sums_ref[...]
        for piece in range(3):
            top = rest.astype(bf16)
            payload_ref[0, tokens : tokens + SUM_ROWS, piece * dim : (piece + 1) * dim] = top
            rest = rest - top.astype(f32)
        lasts = []
        for b in range(samples):
            rows = slice(b * tokens, (b + 1) * tokens)
            shifted = [keys[h][rows] - centers_ref[b, h, 0:1, :] for h in range(heads)]
            shifted += [values[h][rows] - centers_ref[b, h, 1:2, :] for h in range(heads)]
            main = split(jnp.concatenate(shifted[: heads + 1], axis=1))
            code = dot3(main, (tiles_h[b], tiles_l[b]), NT)
            payload_ref[0, :tokens, b * dim : (b + 1) * dim] = code.astype(bf16)
            tail = split(jnp.concatenate(shifted[heads + 1 :], axis=1))
            lasts.append(dot3(tail, (last_h[...], last_l[...]), NT))
            query = split(jnp.concatenate([q[rows] for q in queries], axis=1))
            query_code = dot3(query, (tiles_h[b, :, :width], tiles_l[b, :, :width]), NT)
            high, low = split(query_code * log_factor)
            query_ref[rows, :dim] = high
            query_ref[rows, dim:] = low
        lanes = lane_ids(tokens, dim)
        last = jnp.where(lanes < (heads - 1) * rank, lasts[0], lasts[1])
        payload_ref[0, :tokens, samples * dim :] = last.astype(bf16)
        for h in range(heads):
            qkv_ref[:, h * dim : (h + 1) * dim] = queries[h] * log_factor
            qkv_ref[:, width + h * dim : width + (h + 1) * dim] = keys[h]
            qkv_ref[:, 2 * width + h * dim : 2 * width + (h + 1) * dim] = values[h]


def near_kernel(qkv_ref, centers_ref, acc_ref, stat_ref, *, samples, tokens, heads, dim):
    width = heads * dim
    lanes = lane_ids(tokens, dim)
    for b in range(samples):
        rows = slice(b * tokens, (b + 1) * tokens)
        stats = jnp.zeros((tokens, dim), f32)
        for h in range(heads):
            q = qkv_ref[rows, h * dim : (h + 1) * dim]
            k = split(qkv_ref[rows, width + h * dim : width + (h + 1) * dim])
            v = split(qkv_ref[rows, 2 * width + h * dim : 2 * width + (h + 1) * dim])
            scores = dot3(split(q), k, NT)
            row_max = jnp.max(scores, axis=-1, keepdims=True)
            weights = jnp.exp2(scores - row_max)
            row_sum = jnp.sum(weights, axis=-1, keepdims=True)
            acc_ref[rows, h * dim : (h + 1) * dim] = dot3(split(weights), v)
            center = jnp.sum(q * centers_ref[b, h, 0:1, :], axis=-1, keepdims=True)
            stats = jnp.where(lanes == h, row_max, stats)
            stats = jnp.where(lanes == heads + h, row_sum, stats)
            stats = jnp.where(lanes == 2 * heads + h, center, stats)
        stat_ref[rows, :] = stats


def code_attention(query_ref, tiles, out_ref, *, samples, tokens, heads, dim, rank):
    lanes = lane_ids(tokens, dim)
    for b in range(samples):
        rows = slice(b * tokens, (b + 1) * tokens)
        high = query_ref[rows, :dim]
        low = query_ref[rows, dim:]
        stacked = []
        for h in range(heads):
            at = key_lane(b, h, rank)
            own = (lanes >= at) & (lanes < at + rank)
            zero = jnp.zeros_like(high)
            stacked.append(
                jnp.concatenate([jnp.where(own, high, zero), jnp.where(own, low, zero)], axis=1)
            )
        left = jnp.concatenate(stacked, axis=0)
        scores = []
        for ref, i in tiles:
            code = ref[i, :tokens, b * dim : (b + 1) * dim]
            scores.append(dot(left, jnp.concatenate([code, code], axis=1), NT))
        best = scores[0]
        for part in scores[1:]:
            best = jnp.maximum(best, part)
        row_max = jnp.max(best, axis=-1, keepdims=True)
        total = jnp.zeros_like(best)
        result = jnp.zeros((heads * tokens, 2 * dim), f32)
        for part, (ref, i) in zip(scores, tiles):
            weights = jnp.exp2(part - row_max).astype(bf16)
            total = total + weights.astype(f32)
            values = jnp.concatenate(
                [ref[i, :tokens, b * dim : (b + 1) * dim], ref[i, :tokens, samples * dim :]], axis=1
            )
            result = result + dot(weights, values)
        row_sum = jnp.sum(total, axis=-1, keepdims=True)
        out = jnp.zeros((tokens, dim), f32)
        for h in range(heads):
            head_rows = slice(h * tokens, (h + 1) * tokens)
            at = value_lane(b, h, rank, heads)
            part = result[head_rows, :dim] if h == 0 else result[head_rows, dim:]
            out = jnp.where((lanes >= at) & (lanes < at + rank), part, out)
            spot = free_lane(b, rank)
            out = jnp.where(lanes == spot + h, row_max[head_rows], out)
            out = jnp.where(lanes == spot + heads + h, row_sum[head_rows], out)
        out_ref[rows, :] = out


def tree_sum(parts):
    while len(parts) > 1:
        parts = [parts[i] + parts[i + 1] for i in range(0, len(parts), 2)]
    return parts[0]


def partner_kernel(query_ref, *refs, samples, tokens, heads, dim, rank, order):
    out_ref = refs[-1]
    tiles = [(ref, i) for ref in refs[:-1] for i in range(ref.shape[0])]
    parts = []
    for place in order:
        ref, i = tiles[place]
        rows = slice(tokens, tokens + SUM_ROWS)
        pieces = [ref[i, rows, p * dim : (p + 1) * dim].astype(f32) for p in range(3)]
        parts.append(pieces[0] + (pieces[1] + pieces[2]))
    out_ref[samples * tokens :, :] = tree_sum(parts)
    code_attention(
        query_ref, tiles, out_ref, samples=samples, tokens=tokens, heads=heads, dim=dim, rank=rank
    )


def own_kernel(query_ref, *refs, samples, tokens, heads, dim, rank):
    tiles = [(ref, i) for ref in refs[:-1] for i in range(ref.shape[0])]
    code_attention(
        query_ref, tiles, refs[-1], samples=samples, tokens=tokens, heads=heads, dim=dim, rank=rank
    )


def finish_kernel(
    back_ref, half_ref, own_ref, near_ref, stat_ref, centers_ref, refresh_ref, vb_ref, w_ref,
    mixed_ref, new_ref, attended_ref, basis_h, basis_l,
    *, samples, tokens, heads, dim, rank, length,
):
    @pl.when(pl.program_id(0) == 0)
    def _():
        basis_h[...] = jnp.zeros_like(basis_h)
        basis_l[...] = jnp.zeros_like(basis_l)
        for h in range(heads):
            vh, vl = split(vb_ref[h])
            for b in range(samples):
                at = value_lane(b, h, rank, heads)
                basis_h[b, at : at + rank, h * dim : (h + 1) * dim] = vh
                basis_l[b, at : at + rank, h * dim : (h + 1) * dim] = vl
        lanes = lane_ids(tokens, dim)
        for b in range(samples):
            rows = slice(b * tokens, (b + 1) * tokens)
            stats = stat_ref[rows, :]
            one, two = own_ref[rows, :], back_ref[rows, :]
            spot = free_lane(b, rank)
            scale_one = jnp.zeros((tokens, dim), f32)
            scale_two = jnp.zeros((tokens, dim), f32)
            rest = []
            for h in range(heads):
                center = stats[:, 2 * heads + h : 2 * heads + h + 1]
                near_max = stats[:, h : h + 1]
                max_one = one[:, spot + h : spot + h + 1] + center
                max_two = two[:, spot + h : spot + h + 1] + center
                top = jnp.maximum(near_max, jnp.maximum(max_one, max_two))
                near_scale = jnp.exp2(near_max - top)
                fade_one = jnp.exp2(max_one - top)
                fade_two = jnp.exp2(max_two - top)
                far_sum = fade_one * one[:, spot + heads + h : spot + heads + h + 1]
                far_sum = far_sum + fade_two * two[:, spot + heads + h : spot + heads + h + 1]
                whole = near_scale * stats[:, heads + h : heads + h + 1] + far_sum
                inverse = 1.0 / whole
                at = value_lane(b, h, rank, heads)
                own = (lanes >= at) & (lanes < at + rank)
                scale_one = jnp.where(own, fade_one * inverse, scale_one)
                scale_two = jnp.where(own, fade_two * inverse, scale_two)
                near = near_ref[rows, h * dim : (h + 1) * dim] * (near_scale * inverse)
                rest.append(near + (far_sum * inverse) * centers_ref[b, h, 1:2, :])
            codes = split(one * scale_one + two * scale_two)
            far = dot3(codes, (basis_h[b], basis_l[b]))
            attended_ref[rows, :] = (far + jnp.concatenate(rest, axis=1)).astype(bf16)
            for h in range(heads):
                for j in range(2):
                    row = samples * tokens + (b * heads + h) * 2 + j
                    row_sum = half_ref[row : row + 1, :] + back_ref[row : row + 1, :]
                    fresh = row_sum * (1.0 / length)
                    old = centers_ref[b, h, j : j + 1, :]
                    new_ref[b, h, j : j + 1, :] = jnp.where(refresh_ref[j, h] == 1, fresh, old)

    mixed_ref[...] = dot(attended_ref[...], w_ref[...]).astype(bf16)


VMEM = pl.BlockSpec(memory_space=pltpu.VMEM)


def per_device(
    images, w_qkv, b_qkv, q_gain, k_gain, key_basis, value_basis, centers, refresh, w_out
):
    samples, tokens, model = images.shape
    heads, dim, rank = key_basis.shape
    seq = lax.axis_size("seq")
    rows = samples * tokens
    width = heads * dim
    sizes = dict(samples=samples, tokens=tokens, heads=heads, dim=dim)
    log_factor = math.log2(math.e) / math.sqrt(dim)
    flat = images.reshape(rows, model)
    key_rows = key_basis.transpose(0, 2, 1)
    value_rows = value_basis.transpose(0, 2, 1)
    center_rows = centers.transpose(0, 2, 1, 3)
    depth = 512
    shard = (1, tokens + SUM_ROWS, width)
    whole = lambda *shape: pl.BlockSpec(shape, lambda i: (0,) * len(shape))
    params = lambda mib, **kw: pltpu.CompilerParams(vmem_limit_bytes=mib * 2**20, **kw)

    payload, query, qkv = pl.pallas_call(
        functools.partial(project_kernel, **sizes, rank=rank, log_factor=log_factor),
        grid=(model // depth,),
        in_specs=[
            pl.BlockSpec((rows, depth), lambda i: (0, i)),
            pl.BlockSpec((depth, 3 * width), lambda i: (i, 0)),
            whole(1, 3 * width),
            whole(1, dim),
            whole(1, dim),
            whole(heads, rank, dim),
            whole(heads, rank, dim),
            whole(samples, heads, 2, dim),
        ],
        out_specs=[whole(*shard), whole(rows, 2 * dim), whole(rows, 3 * width)],
        out_shape=[
            jax.ShapeDtypeStruct(shard, bf16),
            jax.ShapeDtypeStruct((rows, 2 * dim), bf16),
            jax.ShapeDtypeStruct((rows, 3 * width), f32),
        ],
        scratch_shapes=[
            pltpu.VMEM((rows, 3 * width), f32),
            pltpu.VMEM((samples, dim, width + dim), bf16),
            pltpu.VMEM((samples, dim, width + dim), bf16),
            pltpu.VMEM((dim, width - dim), bf16),
            pltpu.VMEM((dim, width - dim), bf16),
            pltpu.VMEM((SUM_ROWS, dim), f32),
        ],
        compiler_params=params(24),
        name="project",
    )(
        flat, w_qkv, b_qkv.reshape(1, -1), q_gain.reshape(1, -1), k_gain.reshape(1, -1),
        key_rows, value_rows, center_rows,
    )

    def swap(x, mask):
        return lax.ppermute(x, "seq", [(i, i ^ mask) for i in range(seq)])

    far_mask = seq // 2
    bits = [m for m in (2 ** i for i in range(1, seq.bit_length() - 1)) if m < far_mask]
    query_far = swap(query, far_mask)
    held = [(payload, [0])]
    direct = bits[:2]
    masks = [m for m in range(2, 2 * sum(direct), 2) if m & ~sum(direct) == 0] if direct else []
    for mask in masks:
        held.append((swap(payload, mask), [mask]))
    for bit in bits[2:]:
        block = jnp.concatenate([a for a, _ in held], axis=0)
        names = [m for _, ms in held for m in ms]
        held.append((swap(block, bit), [m ^ bit for m in names]))

    near, stats = pl.pallas_call(
        functools.partial(near_kernel, **sizes),
        in_specs=[VMEM, VMEM],
        out_specs=[VMEM, VMEM],
        out_shape=[
            jax.ShapeDtypeStruct((rows, width), f32),
            jax.ShapeDtypeStruct((rows, dim), f32),
        ],
        compiler_params=params(24),
        cost_estimate=pl.CostEstimate(
            flops=12 * rows * tokens * width, bytes_accessed=5 * rows * width * 4, transcendentals=0
        ),
        name="near",
    )(qkv, center_rows)

    held += [(swap(a, 1), [m ^ 1 for m in ms]) for a, ms in held]
    arrays = [a for a, _ in held]
    names = [m for _, ms in held for m in ms]
    order = tuple(names.index(m) for m in range(len(names)))
    far_flops = 8 * rows * tokens * len(names) * width
    cost = pl.CostEstimate(
        flops=far_flops, bytes_accessed=len(names) * 2 * tokens * width, transcendentals=0
    )
    back = pl.pallas_call(
        functools.partial(partner_kernel, **sizes, rank=rank, order=order),
        in_specs=[VMEM] * (1 + len(arrays)),
        out_specs=VMEM,
        out_shape=jax.ShapeDtypeStruct((rows + SUM_ROWS, dim), f32),
        compiler_params=params(32),
        cost_estimate=cost,
        name="partner",
    )(query_far, *arrays)
    returned = swap(back, far_mask)
    own = pl.pallas_call(
        functools.partial(own_kernel, **sizes, rank=rank),
        in_specs=[VMEM] * len(arrays),
        out_specs=VMEM,
        out_shape=jax.ShapeDtypeStruct((rows, dim), f32),
        compiler_params=params(32),
        cost_estimate=cost,
        name="own",
    )(query, *arrays[1:])

    columns = 1024
    mixed, new_centers = pl.pallas_call(
        functools.partial(finish_kernel, **sizes, rank=rank, length=tokens * seq),
        grid=(model // columns,),
        in_specs=[
            whole(rows + SUM_ROWS, dim),
            whole(rows + SUM_ROWS, dim),
            whole(rows, dim),
            whole(rows, width),
            whole(rows, dim),
            whole(samples, heads, 2, dim),
            pl.BlockSpec(memory_space=pltpu.SMEM),
            whole(heads, rank, dim),
            pl.BlockSpec((width, columns), lambda i: (0, i)),
        ],
        out_specs=[pl.BlockSpec((rows, columns), lambda i: (0, i)), whole(samples, heads, 2, dim)],
        out_shape=[
            jax.ShapeDtypeStruct((rows, model), bf16),
            jax.ShapeDtypeStruct((samples, heads, 2, dim), f32),
        ],
        scratch_shapes=[
            pltpu.VMEM((rows, width), bf16),
            pltpu.VMEM((samples, dim, width), bf16),
            pltpu.VMEM((samples, dim, width), bf16),
        ],
        compiler_params=params(24),
        name="finish",
    )(returned, back, own, near, stats, center_rows, refresh, value_rows, w_out)
    return (mixed.reshape(samples, tokens, model), new_centers.transpose(0, 2, 1, 3))


def solution(mesh):
    return jax.shard_map(
        per_device,
        mesh=mesh,
        in_specs=(
            P("groups", "seq", None),
            P(),
            P(),
            P(),
            P(),
            P(),
            P(),
            P("groups", None, None, None),
            P(),
            P(),
        ),
        out_specs=(P("groups", "seq", None), P("groups", None, None, None)),
        check_vma=False,
    )
```

```python
import functools
import math

import jax
import jax.numpy as jnp
from jax import lax
from jax.experimental import pallas as pl
from jax.experimental.pallas import tpu as pltpu
from jax.sharding import PartitionSpec as P

epsilon = 1e-06
log2_e = math.log2(math.e)
f32 = jnp.float32
bf16 = jnp.bfloat16
SUM_ROWS = 16
NT = (((1,), (1,)), ((), ()))
NN = (((1,), (0,)), ((), ()))


def dot(a, b, dims=NN):
    return lax.dot_general(a, b, dims, preferred_element_type=f32)


def split(x):
    high = x.astype(bf16)
    low = (x - high.astype(f32)).astype(bf16)
    return high, low


def dot3(a, b, dims=NN):
    return dot(a[0], b[0], dims) + (dot(a[0], b[1], dims) + dot(a[1], b[0], dims))


def pieces_of(x, count):
    out = []
    for _ in range(count):
        top = x.astype(bf16)
        out.append(top)
        x = x - top.astype(f32)
    return out


def lane_ids(rows, lanes):
    return lax.broadcasted_iota(jnp.int32, (rows, lanes), 1)


def key_lane(sample, head, rank):
    return head * rank if sample == 0 else (head + 1) * rank


def value_lane(sample, head, rank, heads):
    if head == 0:
        return heads * rank if sample == 0 else 0
    return ((heads - 1) * sample + head - 1) * rank


def free_lane(sample, rank):
    return 2 * rank if sample == 0 else rank


def within(lanes, start, count):
    return (lanes >= start) & (lanes < start + count)


def fill_basis(basis_h, basis_l, vb_ref, samples, heads, dim, rank):
    basis_h[...] = jnp.zeros_like(basis_h)
    basis_l[...] = jnp.zeros_like(basis_l)
    for h in range(heads):
        vh, vl = split(vb_ref[h])
        for b in range(samples):
            at = value_lane(b, h, rank, heads)
            basis_h[b, at : at + rank, h * dim : (h + 1) * dim] = vh
            basis_l[b, at : at + rank, h * dim : (h + 1) * dim] = vl


def project_kernel(
    images_hbm, w_hbm, b_hbm, qg_hbm, kg_hbm, kb_hbm, vb_hbm, centers_hbm,
    payload_ref, query_ref, qkv_ref,
    x_ref, w_ref, b_ref, qg_ref, kg_ref, kb_ref, vb_ref, centers_ref,
    acc_ref, tiles_h, tiles_l, last_h, last_l, sums_ref, big_sem, small_sem,
    *, samples, tokens, heads, dim, rank, log_factor,
):
    chunks, _, depth = x_ref.shape
    width = heads * dim

    def x_copy(c):
        columns = pl.ds(pl.multiple_of(c * depth, depth), depth)
        return pltpu.make_async_copy(images_hbm.at[:, columns], x_ref.at[c], big_sem.at[0, c])

    def w_copy(c):
        some = pl.ds(pl.multiple_of(c * depth, depth), depth)
        return pltpu.make_async_copy(w_hbm.at[some, :], w_ref.at[c], big_sem.at[1, c])

    small = [
        pltpu.make_async_copy(source, target, small_sem.at[i])
        for i, (source, target) in enumerate(
            [
                (kb_hbm, kb_ref), (vb_hbm, vb_ref), (b_hbm, b_ref),
                (qg_hbm, qg_ref), (kg_hbm, kg_ref), (centers_hbm, centers_ref),
            ]
        )
    ]
    for c in range(chunks):
        x_copy(c).start()
        w_copy(c).start()
        if c == 0:
            for copy in small:
                copy.start()
    tiles_h[...] = jnp.zeros_like(tiles_h)
    tiles_l[...] = jnp.zeros_like(tiles_l)
    last_h[...] = jnp.zeros_like(last_h)
    last_l[...] = jnp.zeros_like(last_l)
    sums_ref[...] = jnp.zeros_like(sums_ref)
    for copy in small:
        copy.wait()
    for h in range(heads):
        kh, kl = split(kb_ref[h])
        vh, vl = split(vb_ref[h])
        for b in range(samples):
            at = key_lane(b, h, rank)
            tiles_h[b, at : at + rank, h * dim : (h + 1) * dim] = kh
            tiles_l[b, at : at + rank, h * dim : (h + 1) * dim] = kl
            at = value_lane(b, h, rank, heads)
            if h == 0:
                tiles_h[b, at : at + rank, width : width + dim] = vh
                tiles_l[b, at : at + rank, width : width + dim] = vl
            else:
                last_h[at : at + rank, (h - 1) * dim : h * dim] = vh
                last_l[at : at + rank, (h - 1) * dim : h * dim] = vl
    for c in range(chunks):
        x_copy(c).wait()
        w_copy(c).wait()
        part = dot(x_ref[c], w_ref[c])
        if c == 0:
            acc_ref[...] = part
        else:
            acc_ref[...] += part

    def column(at):
        return acc_ref[:, at * dim : (at + 1) * dim] + b_ref[at : at + 1, :]

    def normed(at, gain):
        x = column(at)
        mean_square = jnp.mean(x * x, axis=-1, keepdims=True)
        return x * lax.rsqrt(mean_square + epsilon) * gain

    queries, keys, values = [], [], []
    for h in range(heads):
        q = normed(h, qg_ref[...])
        k = normed(heads + h, kg_ref[...])
        v = column(2 * heads + h)
        queries.append(q)
        keys.append(k)
        values.append(v)
        for b in range(samples):
            rows = slice(b * tokens, (b + 1) * tokens)
            row = (b * heads + h) * 2
            sums_ref[row : row + 1, :] = jnp.sum(k[rows], axis=0, keepdims=True)
            sums_ref[row + 1 : row + 2, :] = jnp.sum(v[rows], axis=0, keepdims=True)
    for p, piece in enumerate(pieces_of(sums_ref[...], 3)):
        payload_ref[0, tokens : tokens + SUM_ROWS, p * dim : (p + 1) * dim] = piece
    lasts, highs, lows = [], [], []
    for b in range(samples):
        rows = slice(b * tokens, (b + 1) * tokens)
        shifted = [keys[h][rows] - centers_ref[b, h, 0:1, :] for h in range(heads)]
        shifted += [values[h][rows] - centers_ref[b, h, 1:2, :] for h in range(heads)]
        main = split(jnp.concatenate(shifted[: heads + 1], axis=1))
        code = dot3(main, (tiles_h[b], tiles_l[b]), NT)
        payload_ref[0, :tokens, b * dim : (b + 1) * dim] = code.astype(bf16)
        tail = split(jnp.concatenate(shifted[heads + 1 :], axis=1))
        lasts.append(dot3(tail, (last_h[...], last_l[...]), NT))
        query = split(jnp.concatenate([q[rows] for q in queries], axis=1))
        query_code = dot3(query, (tiles_h[b, :, :width], tiles_l[b, :, :width]), NT) * log_factor
        high = query_code.astype(bf16).astype(f32)
        highs.append(high)
        lows.append(query_code - high)
    lanes = lane_ids(tokens, dim)
    last = jnp.where(lanes < (heads - 1) * rank, lasts[0], lasts[1])
    payload_ref[0, :tokens, samples * dim :] = last.astype(bf16)
    turned = pltpu.roll(lows[1], dim // 2, 1)
    query_ref[:, :dim] = jnp.where(lanes < heads * rank, highs[0], turned).astype(bf16)
    query_ref[:, dim : 2 * dim] = jnp.where(lanes < rank, turned, highs[1]).astype(bf16)
    query_ref[:, 2 * dim :] = jnp.where(lanes < heads * rank, lows[0], lows[1]).astype(bf16)
    for h in range(heads):
        qkv_ref[:, h * dim : (h + 1) * dim] = queries[h] * log_factor
        qkv_ref[:, width + h * dim : width + (h + 1) * dim] = keys[h]
        qkv_ref[:, 2 * width + h * dim : 2 * width + (h + 1) * dim] = values[h]


def near_kernel(qkv_ref, centers_ref, near_ref, stat_ref, *, samples, tokens, heads, dim):
    width = heads * dim
    lanes = lane_ids(tokens, dim)
    for b in range(samples):
        rows = slice(b * tokens, (b + 1) * tokens)
        stats = jnp.zeros((tokens, dim), f32)
        for h in range(heads):
            q = qkv_ref[rows, h * dim : (h + 1) * dim]
            k = split(qkv_ref[rows, width + h * dim : width + (h + 1) * dim])
            v = split(qkv_ref[rows, 2 * width + h * dim : 2 * width + (h + 1) * dim])
            scores = dot3(split(q), k, NT)
            row_max = jnp.max(scores, axis=-1, keepdims=True)
            weights = jnp.exp2(scores - row_max)
            row_sum = jnp.sum(weights, axis=-1, keepdims=True)
            near_ref[rows, h * dim : (h + 1) * dim] = dot3(split(weights), v) / row_sum
            center = jnp.sum(q * centers_ref[b, h, 0:1, :], axis=-1, keepdims=True)
            stats = jnp.where(lanes == h, row_max + jnp.log(row_sum) * log2_e, stats)
            stats = jnp.where(lanes == heads + h, center, stats)
        stat_ref[rows, :] = stats


def query_parts(query_ref, sample, heads, dim, rank):
    lanes = lane_ids(query_ref.shape[0], dim)
    if sample == 0:
        return query_ref[:, :dim].astype(f32), query_ref[:, 2 * dim :].astype(f32)
    first, second = query_ref[:, :dim].astype(f32), query_ref[:, dim : 2 * dim].astype(f32)
    turned = pltpu.roll(jnp.where(lanes < rank, second, first), dim // 2, 1)
    return second, jnp.where(lanes < heads * rank, turned, query_ref[:, 2 * dim :].astype(f32))


def code_attention(query_ref, tiles, b, *, samples, tokens, heads, dim, rank):
    lanes = lane_ids(tokens, dim)
    high, low = query_parts(query_ref, b, heads, dim, rank)
    stacked = []
    for h in range(heads):
        own = within(lanes, key_lane(b, h, rank), rank)
        both = [jnp.where(own, part, 0.0).astype(bf16) for part in (high, low)]
        stacked.append(jnp.concatenate(both, axis=1))
    left = jnp.concatenate(stacked, axis=0)
    scores, values = [], []
    for ref, i in tiles:
        code = ref[i, :tokens, b * dim : (b + 1) * dim]
        scores.append(dot(left, jnp.concatenate([code, code], axis=1), NT))
        values.append(jnp.concatenate([code, ref[i, :tokens, samples * dim :]], axis=1))
    best = scores[0]
    for part in scores[1:]:
        best = jnp.maximum(best, part)
    row_max = jnp.max(best, axis=-1, keepdims=True)
    total = jnp.zeros_like(best)
    weights = []
    for part in scores:
        weight = jnp.exp2(part - row_max).astype(bf16)
        total = total + weight.astype(f32)
        weights.append(weight)
    result = dot(jnp.concatenate(weights, axis=1), jnp.concatenate(values, axis=0))
    row_sum = jnp.sum(total, axis=-1, keepdims=True)
    result = result / row_sum
    log_sum = row_max + jnp.log(row_sum) * log2_e
    out = jnp.zeros((tokens, dim), f32)
    logs = []
    for h in range(heads):
        head_rows = slice(h * tokens, (h + 1) * tokens)
        part = result[head_rows, :dim] if h == 0 else result[head_rows, dim:]
        out = jnp.where(within(lanes, value_lane(b, h, rank, heads), rank), part, out)
        logs.append(log_sum[head_rows])
    return out, logs


def tree_sum(parts):
    while len(parts) > 1:
        parts = [parts[i] + parts[i + 1] for i in range(0, len(parts), 2)]
    return parts[0]


def tiles_of(refs):
    return [(ref, i) for ref in refs for i in range(ref.shape[0])]


def partner_kernel(query_ref, *refs, order, samples, tokens, heads, dim, rank):
    out_ref = refs[-1]
    tiles = tiles_of(refs[:-2])
    parts = []
    for place in order:
        ref, i = tiles[place]
        rows = slice(tokens, tokens + SUM_ROWS)
        pieces = [ref[i, rows, p * dim : (p + 1) * dim].astype(f32) for p in range(3)]
        parts.append(pieces[0] + (pieces[1] + pieces[2]))
    first = samples * tokens
    for p, piece in enumerate(pieces_of(tree_sum(parts), 2)):
        out_ref[first + p * SUM_ROWS : first + (p + 1) * SUM_ROWS, :] = piece
    lanes = lane_ids(tokens, dim)
    for b in range(samples):
        out, logs = code_attention(
            query_ref, tiles, b, samples=samples, tokens=tokens, heads=heads, dim=dim, rank=rank
        )
        for h in range(heads):
            for p, piece in enumerate(pieces_of(logs[h], 3)):
                out = jnp.where(lanes == free_lane(b, rank) + 3 * h + p, piece.astype(f32), out)
        out_ref[b * tokens : (b + 1) * tokens, :] = out.astype(bf16)


def own_kernel(
    query_ref, near_ref, stat_ref, centers_ref, vb_ref, *refs, samples, tokens, heads, dim, rank
):
    merged_ref, log_ref, basis_h, basis_l = refs[-4:]
    fill_basis(basis_h, basis_l, vb_ref, samples, heads, dim, rank)
    tiles = tiles_of(refs[:-4])
    lanes = lane_ids(tokens, dim)
    for b in range(samples):
        rows = slice(b * tokens, (b + 1) * tokens)
        out, logs = code_attention(
            query_ref, tiles, b, samples=samples, tokens=tokens, heads=heads, dim=dim, rank=rank
        )
        far = dot3(split(out), (basis_h[b], basis_l[b]))
        stats = stat_ref[rows, :]
        kept = jnp.zeros((tokens, dim), f32)
        for h in range(heads):
            columns = slice(h * dim, (h + 1) * dim)
            near_log = stats[:, h : h + 1]
            center = stats[:, heads + h : heads + h + 1]
            far_log = logs[h] + center
            top = jnp.maximum(near_log, far_log)
            near_part, far_part = jnp.exp2(near_log - top), jnp.exp2(far_log - top)
            whole = near_part + far_part
            merged = near_ref[rows, columns] * (near_part / whole)
            merged = merged + (far[:, columns] + centers_ref[b, h, 1:2, :]) * (far_part / whole)
            merged_ref[rows, columns] = merged
            kept = jnp.where(lanes == h, top + jnp.log(whole) * log2_e, kept)
            kept = jnp.where(lanes == heads + h, center, kept)
        log_ref[rows, :] = kept


def finish_kernel(
    back_ref, half_ref, merged_ref, log_ref, centers_ref, refresh_ref, vb_ref, w_ref,
    mixed_hbm, new_ref, attended_ref, basis_h, basis_l, mixed_ref, sem,
    *, samples, tokens, heads, dim, rank, length,
):
    fill_basis(basis_h, basis_l, vb_ref, samples, heads, dim, rank)
    for b in range(samples):
        rows = slice(b * tokens, (b + 1) * tokens)
        codes = back_ref[rows, :]
        far = dot(codes, basis_h[b]) + dot(codes, basis_l[b])
        extra = codes.astype(f32)
        logs = log_ref[rows, :]
        for h in range(heads):
            columns = slice(h * dim, (h + 1) * dim)
            spot = free_lane(b, rank) + 3 * h
            far_log = extra[:, spot : spot + 1] + (
                extra[:, spot + 1 : spot + 2] + extra[:, spot + 2 : spot + 3]
            )
            far_log = far_log + logs[:, heads + h : heads + h + 1]
            own_log = logs[:, h : h + 1]
            top = jnp.maximum(own_log, far_log)
            own_part, far_part = jnp.exp2(own_log - top), jnp.exp2(far_log - top)
            whole = own_part + far_part
            value = merged_ref[rows, columns] * (own_part / whole)
            value = value + (far[:, columns] + centers_ref[b, h, 1:2, :]) * (far_part / whole)
            attended_ref[rows, columns] = value.astype(bf16)
    chunks, _, columns = mixed_ref.shape
    copies = []
    for c in range(chunks):
        place = slice(c * columns, (c + 1) * columns)
        mixed_ref[c] = dot(attended_ref[...], w_ref[:, place]).astype(bf16)
        copy = pltpu.make_async_copy(mixed_ref.at[c], mixed_hbm.at[:, place], sem.at[c])
        copy.start()
        copies.append(copy)
    first = samples * tokens
    sums = [
        ref[first : first + SUM_ROWS, :].astype(f32)
        + ref[first + SUM_ROWS : first + 2 * SUM_ROWS, :].astype(f32)
        for ref in (half_ref, back_ref)
    ]
    fresh = (sums[0] + sums[1]) * (1.0 / length)
    for b in range(samples):
        for h in range(heads):
            for j in range(2):
                row = (b * heads + h) * 2 + j
                old = centers_ref[b, h, j : j + 1, :]
                new_ref[b, h, j : j + 1, :] = jnp.where(
                    refresh_ref[j, h] == 1, fresh[row : row + 1, :], old
                )
    for copy in copies:
        copy.wait()


VMEM = pl.BlockSpec(memory_space=pltpu.VMEM)
HBM = pl.BlockSpec(memory_space=pltpu.HBM)


def per_device(
    images, w_qkv, b_qkv, q_gain, k_gain, key_basis, value_basis, centers, refresh, w_out
):
    samples, tokens, model = images.shape
    heads, dim, rank = key_basis.shape
    seq = lax.axis_size("seq")
    rows = samples * tokens
    width = heads * dim
    sizes = dict(samples=samples, tokens=tokens, heads=heads, dim=dim)
    log_factor = log2_e / math.sqrt(dim)
    flat = images.reshape(rows, model)
    key_rows = key_basis.transpose(0, 2, 1)
    value_rows = value_basis.transpose(0, 2, 1)
    center_rows = centers.transpose(0, 2, 1, 3)
    chunks = 6
    depth = model // chunks
    shard = (1, tokens + SUM_ROWS, width)
    params = lambda mib: pltpu.CompilerParams(vmem_limit_bytes=mib * 2**20)

    payload, query, qkv = pl.pallas_call(
        functools.partial(project_kernel, **sizes, rank=rank, log_factor=log_factor),
        in_specs=[HBM] * 8,
        out_specs=[VMEM] * 3,
        out_shape=[
            jax.ShapeDtypeStruct(shard, bf16),
            jax.ShapeDtypeStruct((tokens, width), bf16),
            jax.ShapeDtypeStruct((rows, 3 * width), f32),
        ],
        scratch_shapes=[
            pltpu.VMEM((chunks, rows, depth), bf16),
            pltpu.VMEM((chunks, depth, 3 * width), bf16),
            pltpu.VMEM((3 * heads, dim), f32),
            pltpu.VMEM((1, dim), f32),
            pltpu.VMEM((1, dim), f32),
            pltpu.VMEM((heads, rank, dim), f32),
            pltpu.VMEM((heads, rank, dim), f32),
            pltpu.VMEM((samples, heads, 2, dim), f32),
            pltpu.VMEM((rows, 3 * width), f32),
            pltpu.VMEM((samples, dim, width + dim), bf16),
            pltpu.VMEM((samples, dim, width + dim), bf16),
            pltpu.VMEM((dim, width - dim), bf16),
            pltpu.VMEM((dim, width - dim), bf16),
            pltpu.VMEM((SUM_ROWS, dim), f32),
            pltpu.SemaphoreType.DMA((2, chunks)),
            pltpu.SemaphoreType.DMA((6,)),
        ],
        compiler_params=params(32),
        name="project",
    )(
        *(
            pltpu.with_memory_space_constraint(x, pltpu.HBM)
            for x in (
                flat, w_qkv, b_qkv.reshape(3 * heads, dim), q_gain.reshape(1, -1),
                k_gain.reshape(1, -1), key_rows, value_rows, center_rows,
            )
        )
    )

    def swap(x, mask):
        return lax.ppermute(x, "seq", [(i, i ^ mask) for i in range(seq)])

    far_mask = seq // 2
    bits = [m for m in (2**i for i in range(1, seq.bit_length() - 1)) if m < far_mask]
    query_far = swap(query, far_mask)
    held = [(payload, [0])]
    direct = sum(bits[:2])
    for mask in range(2, 2 * direct, 2):
        if mask & ~direct == 0:
            held.append((swap(payload, mask), [mask]))
    for bit in bits[2:]:
        block = jnp.concatenate([a for a, _ in held], axis=0)
        names = [m for _, ms in held for m in ms]
        held.append((swap(block, bit), [m ^ bit for m in names]))

    near, stats = pl.pallas_call(
        functools.partial(near_kernel, **sizes),
        in_specs=[VMEM, VMEM],
        out_specs=[VMEM, VMEM],
        out_shape=[
            jax.ShapeDtypeStruct((rows, width), f32),
            jax.ShapeDtypeStruct((rows, dim), f32),
        ],
        compiler_params=params(24),
        cost_estimate=pl.CostEstimate(
            flops=12 * rows * tokens * width, bytes_accessed=5 * rows * width * 4, transcendentals=0
        ),
        name="near",
    )(qkv, center_rows)

    held += [(swap(a, 1), [m ^ 1 for m in ms]) for a, ms in held]
    arrays = [a for a, _ in held]
    names = [m for _, ms in held for m in ms]
    order = tuple(names.index(m) for m in range(len(names)))
    cost = pl.CostEstimate(
        flops=8 * rows * tokens * len(names) * width,
        bytes_accessed=len(names) * 2 * tokens * width,
        transcendentals=0,
    )
    back = pl.pallas_call(
        functools.partial(partner_kernel, **sizes, rank=rank, order=order),
        in_specs=[VMEM] * (1 + len(arrays)) + [pl.BlockSpec(memory_space=pl.ANY)],
        out_specs=VMEM,
        out_shape=jax.ShapeDtypeStruct((rows + 2 * SUM_ROWS, dim), bf16),
        compiler_params=params(32),
        cost_estimate=cost,
        name="partner",
    )(query_far, *arrays, stats)
    returned = swap(back, far_mask)
    merged, logs = pl.pallas_call(
        functools.partial(own_kernel, **sizes, rank=rank),
        in_specs=[VMEM] * (4 + len(arrays)),
        out_specs=[VMEM, VMEM],
        out_shape=[
            jax.ShapeDtypeStruct((rows, width), f32),
            jax.ShapeDtypeStruct((rows, dim), f32),
        ],
        scratch_shapes=[
            pltpu.VMEM((samples, dim, width), bf16),
            pltpu.VMEM((samples, dim, width), bf16),
        ],
        compiler_params=params(32),
        cost_estimate=cost,
        name="own",
    )(query, near, stats, center_rows, value_rows, *arrays[1:])

    columns = 512
    mixed, new_centers = pl.pallas_call(
        functools.partial(finish_kernel, **sizes, rank=rank, length=tokens * seq),
        in_specs=[VMEM] * 5 + [pl.BlockSpec(memory_space=pltpu.SMEM), VMEM, VMEM],
        out_specs=[HBM, VMEM],
        out_shape=[
            jax.ShapeDtypeStruct((rows, model), bf16),
            jax.ShapeDtypeStruct((samples, heads, 2, dim), f32),
        ],
        scratch_shapes=[
            pltpu.VMEM((rows, width), bf16),
            pltpu.VMEM((samples, dim, width), bf16),
            pltpu.VMEM((samples, dim, width), bf16),
            pltpu.VMEM((model // columns, rows, columns), bf16),
            pltpu.SemaphoreType.DMA((model // columns,)),
        ],
        compiler_params=params(24),
        name="finish",
    )(returned, back, merged, logs, center_rows, refresh, value_rows, w_out)
    return (mixed.reshape(samples, tokens, model), new_centers.transpose(0, 2, 1, 3))


def solution(mesh):
    return jax.shard_map(
        per_device,
        mesh=mesh,
        in_specs=(
            P("groups", "seq", None),
            P(),
            P(),
            P(),
            P(),
            P(),
            P(),
            P("groups", None, None, None),
            P(),
            P(),
        ),
        out_specs=(P("groups", "seq", None), P("groups", None, None, None)),
        check_vma=False,
    )
```

```python
import functools
import math

import jax
import jax.numpy as jnp
from jax import lax
from jax.experimental import pallas as pl
from jax.experimental.pallas import tpu as pltpu
from jax.sharding import PartitionSpec as P

epsilon = 1e-06
log2_e = math.log2(math.e)
f32 = jnp.float32
bf16 = jnp.bfloat16
SUM_ROWS = 16
NT = (((1,), (1,)), ((), ()))
NN = (((1,), (0,)), ((), ()))


def dot(a, b, dims=NN):
    return lax.dot_general(a, b, dims, preferred_element_type=f32)


def split(x):
    high = x.astype(bf16)
    low = (x - high.astype(f32)).astype(bf16)
    return high, low


def dot3(a, b, dims=NN):
    return dot(a[0], b[0], dims) + (dot(a[0], b[1], dims) + dot(a[1], b[0], dims))


def pieces_of(x, count):
    out = []
    for _ in range(count):
        top = x.astype(bf16)
        out.append(top)
        x = x - top.astype(f32)
    return out


def lane_ids(rows, lanes):
    return lax.broadcasted_iota(jnp.int32, (rows, lanes), 1)


def key_lane(sample, head, rank):
    return head * rank if sample == 0 else (head + 1) * rank


def value_lane(sample, head, rank, heads):
    if head == 0:
        return heads * rank if sample == 0 else 0
    return ((heads - 1) * sample + head - 1) * rank


def free_lane(sample, rank):
    return 2 * rank if sample == 0 else rank


def within(lanes, start, count):
    return (lanes >= start) & (lanes < start + count)


def fill_basis(basis_h, basis_l, vb_ref, samples, heads, dim, rank):
    basis_h[...] = jnp.zeros_like(basis_h)
    basis_l[...] = jnp.zeros_like(basis_l)
    for h in range(heads):
        vh, vl = split(vb_ref[h])
        for b in range(samples):
            at = value_lane(b, h, rank, heads)
            basis_h[b, at : at + rank, h * dim : (h + 1) * dim] = vh
            basis_l[b, at : at + rank, h * dim : (h + 1) * dim] = vl


def project_kernel(
    images_hbm, w_hbm, b_hbm, qg_hbm, kg_hbm, kb_hbm, vb_hbm, centers_hbm,
    payload_ref, query_ref, qkv_ref,
    x_ref, w_ref, b_ref, qg_ref, kg_ref, kb_ref, vb_ref, centers_ref,
    acc_ref, tiles_h, tiles_l, last_h, last_l, sums_ref, big_sem, small_sem,
    *, samples, tokens, heads, dim, rank, log_factor,
):
    chunks, _, depth = x_ref.shape
    width = heads * dim

    def x_copy(c):
        columns = pl.ds(pl.multiple_of(c * depth, depth), depth)
        return pltpu.make_async_copy(images_hbm.at[:, columns], x_ref.at[c], big_sem.at[0, c])

    def w_copy(c):
        some = pl.ds(pl.multiple_of(c * depth, depth), depth)
        return pltpu.make_async_copy(w_hbm.at[some, :], w_ref.at[c], big_sem.at[1, c])

    small = [
        pltpu.make_async_copy(source, target, small_sem.at[i])
        for i, (source, target) in enumerate(
            [
                (kb_hbm, kb_ref), (vb_hbm, vb_ref), (b_hbm, b_ref),
                (qg_hbm, qg_ref), (kg_hbm, kg_ref), (centers_hbm, centers_ref),
            ]
        )
    ]
    for c in range(chunks):
        x_copy(c).start()
        w_copy(c).start()
        if c == 0:
            for copy in small:
                copy.start()
    tiles_h[...] = jnp.zeros_like(tiles_h)
    tiles_l[...] = jnp.zeros_like(tiles_l)
    last_h[...] = jnp.zeros_like(last_h)
    last_l[...] = jnp.zeros_like(last_l)
    sums_ref[...] = jnp.zeros_like(sums_ref)
    for copy in small:
        copy.wait()
    for h in range(heads):
        kh, kl = split(kb_ref[h])
        vh, vl = split(vb_ref[h])
        for b in range(samples):
            at = key_lane(b, h, rank)
            tiles_h[b, at : at + rank, h * dim : (h + 1) * dim] = kh
            tiles_l[b, at : at + rank, h * dim : (h + 1) * dim] = kl
            at = value_lane(b, h, rank, heads)
            if h == 0:
                tiles_h[b, at : at + rank, width : width + dim] = vh
                tiles_l[b, at : at + rank, width : width + dim] = vl
            else:
                last_h[at : at + rank, (h - 1) * dim : h * dim] = vh
                last_l[at : at + rank, (h - 1) * dim : h * dim] = vl
    for c in range(chunks):
        x_copy(c).wait()
        w_copy(c).wait()
        part = dot(x_ref[c], w_ref[c])
        if c == 0:
            acc_ref[...] = part
        else:
            acc_ref[...] += part

    def column(at):
        return acc_ref[:, at * dim : (at + 1) * dim] + b_ref[at : at + 1, :]

    def normed(at, gain):
        x = column(at)
        mean_square = jnp.mean(x * x, axis=-1, keepdims=True)
        return x * lax.rsqrt(mean_square + epsilon) * gain

    queries, keys, values = [], [], []
    for h in range(heads):
        q = normed(h, qg_ref[...])
        k = normed(heads + h, kg_ref[...])
        v = column(2 * heads + h)
        queries.append(q)
        keys.append(k)
        values.append(v)
        for b in range(samples):
            rows = slice(b * tokens, (b + 1) * tokens)
            row = (b * heads + h) * 2
            sums_ref[row : row + 1, :] = jnp.sum(k[rows], axis=0, keepdims=True)
            sums_ref[row + 1 : row + 2, :] = jnp.sum(v[rows], axis=0, keepdims=True)
    for p, piece in enumerate(pieces_of(sums_ref[...], 3)):
        payload_ref[0, tokens : tokens + SUM_ROWS, p * dim : (p + 1) * dim] = piece
    lasts, highs, lows = [], [], []
    for b in range(samples):
        rows = slice(b * tokens, (b + 1) * tokens)
        shifted = [keys[h][rows] - centers_ref[b, h, 0:1, :] for h in range(heads)]
        shifted += [values[h][rows] - centers_ref[b, h, 1:2, :] for h in range(heads)]
        main = split(jnp.concatenate(shifted[: heads + 1], axis=1))
        code = dot3(main, (tiles_h[b], tiles_l[b]), NT)
        payload_ref[0, :tokens, b * dim : (b + 1) * dim] = code.astype(bf16)
        tail = split(jnp.concatenate(shifted[heads + 1 :], axis=1))
        lasts.append(dot3(tail, (last_h[...], last_l[...]), NT))
        query = split(jnp.concatenate([q[rows] for q in queries], axis=1))
        query_code = dot3(query, (tiles_h[b, :, :width], tiles_l[b, :, :width]), NT) * log_factor
        high = query_code.astype(bf16).astype(f32)
        highs.append(high)
        lows.append(query_code - high)
    lanes = lane_ids(tokens, dim)
    last = jnp.where(lanes < (heads - 1) * rank, lasts[0], lasts[1])
    payload_ref[0, :tokens, samples * dim :] = last.astype(bf16)
    turned = pltpu.roll(lows[1], dim // 2, 1)
    query_ref[:, :dim] = jnp.where(lanes < heads * rank, highs[0], turned).astype(bf16)
    query_ref[:, dim : 2 * dim] = jnp.where(lanes < rank, turned, highs[1]).astype(bf16)
    query_ref[:, 2 * dim :] = jnp.where(lanes < heads * rank, lows[0], lows[1]).astype(bf16)
    for h in range(heads):
        qkv_ref[:, h * dim : (h + 1) * dim] = queries[h] * log_factor
        qkv_ref[:, width + h * dim : width + (h + 1) * dim] = keys[h]
        qkv_ref[:, 2 * width + h * dim : 2 * width + (h + 1) * dim] = values[h]


def near_kernel(qkv_ref, centers_ref, near_ref, stat_ref, *, samples, tokens, heads, dim):
    width = heads * dim
    lanes = lane_ids(tokens, dim)
    for b in range(samples):
        rows = slice(b * tokens, (b + 1) * tokens)
        stats = jnp.zeros((tokens, dim), f32)
        for h in range(heads):
            q = qkv_ref[rows, h * dim : (h + 1) * dim]
            k = split(qkv_ref[rows, width + h * dim : width + (h + 1) * dim])
            v = split(qkv_ref[rows, 2 * width + h * dim : 2 * width + (h + 1) * dim])
            scores = dot3(split(q), k, NT)
            row_max = jnp.max(scores, axis=-1, keepdims=True)
            weights = jnp.exp2(scores - row_max)
            row_sum = jnp.sum(weights, axis=-1, keepdims=True)
            near_ref[rows, h * dim : (h + 1) * dim] = dot3(split(weights), v) / row_sum
            center = jnp.sum(q * centers_ref[b, h, 0:1, :], axis=-1, keepdims=True)
            stats = jnp.where(lanes == h, row_max + jnp.log(row_sum) * log2_e, stats)
            stats = jnp.where(lanes == heads + h, center, stats)
        stat_ref[rows, :] = stats


def query_parts(query_ref, sample, heads, dim, rank):
    lanes = lane_ids(query_ref.shape[0], dim)
    if sample == 0:
        return query_ref[:, :dim].astype(f32), query_ref[:, 2 * dim :].astype(f32)
    first, second = query_ref[:, :dim].astype(f32), query_ref[:, dim : 2 * dim].astype(f32)
    turned = pltpu.roll(jnp.where(lanes < rank, second, first), dim // 2, 1)
    return second, jnp.where(lanes < heads * rank, turned, query_ref[:, 2 * dim :].astype(f32))


def code_attention(query_ref, tiles, b, *, samples, tokens, heads, dim, rank):
    lanes = lane_ids(tokens, dim)
    high, low = query_parts(query_ref, b, heads, dim, rank)
    stacked = []
    for h in range(heads):
        own = within(lanes, key_lane(b, h, rank), rank)
        both = [jnp.where(own, part, 0.0).astype(bf16) for part in (high, low)]
        stacked.append(jnp.concatenate(both, axis=1))
    left = jnp.concatenate(stacked, axis=0)
    scores, values = [], []
    for ref, i in tiles:
        code = ref[i, :tokens, b * dim : (b + 1) * dim]
        scores.append(dot(left, jnp.concatenate([code, code], axis=1), NT))
        values.append(jnp.concatenate([code, ref[i, :tokens, samples * dim :]], axis=1))
    best = scores[0]
    for part in scores[1:]:
        best = jnp.maximum(best, part)
    row_max = jnp.max(best, axis=-1, keepdims=True)
    total = jnp.zeros_like(best)
    weights = []
    for part in scores:
        weight = jnp.exp2(part - row_max).astype(bf16)
        total = total + weight.astype(f32)
        weights.append(weight)
    result = dot(jnp.concatenate(weights, axis=1), jnp.concatenate(values, axis=0))
    row_sum = jnp.sum(total, axis=-1, keepdims=True)
    result = result / row_sum
    log_sum = row_max + jnp.log(row_sum) * log2_e
    out = jnp.zeros((tokens, dim), f32)
    logs = []
    for h in range(heads):
        head_rows = slice(h * tokens, (h + 1) * tokens)
        part = result[head_rows, :dim] if h == 0 else result[head_rows, dim:]
        out = jnp.where(within(lanes, value_lane(b, h, rank, heads), rank), part, out)
        logs.append(log_sum[head_rows])
    return out, logs


def tree_sum(parts):
    while len(parts) > 1:
        parts = [parts[i] + parts[i + 1] for i in range(0, len(parts), 2)]
    return parts[0]


def tiles_of(refs):
    return [(ref, i) for ref in refs for i in range(ref.shape[0])]


def partner_kernel(query_ref, *refs, order, samples, tokens, heads, dim, rank):
    out_ref = refs[-1]
    tiles = tiles_of(refs[:-2])
    parts = []
    for place in order:
        ref, i = tiles[place]
        rows = slice(tokens, tokens + SUM_ROWS)
        pieces = [ref[i, rows, p * dim : (p + 1) * dim].astype(f32) for p in range(3)]
        parts.append(pieces[0] + (pieces[1] + pieces[2]))
    first = samples * tokens
    for p, piece in enumerate(pieces_of(tree_sum(parts), 2)):
        out_ref[first + p * SUM_ROWS : first + (p + 1) * SUM_ROWS, :] = piece
    lanes = lane_ids(tokens, dim)
    for b in range(samples):
        out, logs = code_attention(
            query_ref, tiles, b, samples=samples, tokens=tokens, heads=heads, dim=dim, rank=rank
        )
        for h in range(heads):
            for p, piece in enumerate(pieces_of(logs[h], 3)):
                out = jnp.where(lanes == free_lane(b, rank) + 3 * h + p, piece.astype(f32), out)
        out_ref[b * tokens : (b + 1) * tokens, :] = out.astype(bf16)


def own_kernel(
    query_ref, near_ref, stat_ref, centers_ref, vb_ref, *refs, samples, tokens, heads, dim, rank
):
    merged_ref, log_ref, basis_h, basis_l = refs[-4:]
    fill_basis(basis_h, basis_l, vb_ref, samples, heads, dim, rank)
    tiles = tiles_of(refs[:-4])
    lanes = lane_ids(tokens, dim)
    for b in range(samples):
        rows = slice(b * tokens, (b + 1) * tokens)
        out, logs = code_attention(
            query_ref, tiles, b, samples=samples, tokens=tokens, heads=heads, dim=dim, rank=rank
        )
        far = dot3(split(out), (basis_h[b], basis_l[b]))
        stats = stat_ref[rows, :]
        kept = jnp.zeros((tokens, dim), f32)
        for h in range(heads):
            columns = slice(h * dim, (h + 1) * dim)
            near_log = stats[:, h : h + 1]
            center = stats[:, heads + h : heads + h + 1]
            far_log = logs[h] + center
            top = jnp.maximum(near_log, far_log)
            near_part, far_part = jnp.exp2(near_log - top), jnp.exp2(far_log - top)
            whole = near_part + far_part
            merged = near_ref[rows, columns] * (near_part / whole)
            merged = merged + (far[:, columns] + centers_ref[b, h, 1:2, :]) * (far_part / whole)
            merged_ref[rows, columns] = merged
            kept = jnp.where(lanes == h, top + jnp.log(whole) * log2_e, kept)
            kept = jnp.where(lanes == heads + h, center, kept)
        log_ref[rows, :] = kept


def finish_kernel(
    back_ref, half_ref, merged_ref, log_ref, centers_ref, refresh_ref, vb_ref, w_ref,
    mixed_hbm, new_ref, attended_ref, basis_h, basis_l, mixed_ref, sem,
    *, samples, tokens, heads, dim, rank, length,
):
    fill_basis(basis_h, basis_l, vb_ref, samples, heads, dim, rank)
    for b in range(samples):
        rows = slice(b * tokens, (b + 1) * tokens)
        codes = back_ref[rows, :]
        far = dot(codes, basis_h[b]) + dot(codes, basis_l[b])
        extra = codes.astype(f32)
        logs = log_ref[rows, :]
        for h in range(heads):
            columns = slice(h * dim, (h + 1) * dim)
            spot = free_lane(b, rank) + 3 * h
            far_log = extra[:, spot : spot + 1] + (
                extra[:, spot + 1 : spot + 2] + extra[:, spot + 2 : spot + 3]
            )
            far_log = far_log + logs[:, heads + h : heads + h + 1]
            own_log = logs[:, h : h + 1]
            top = jnp.maximum(own_log, far_log)
            own_part, far_part = jnp.exp2(own_log - top), jnp.exp2(far_log - top)
            whole = own_part + far_part
            value = merged_ref[rows, columns] * (own_part / whole)
            value = value + (far[:, columns] + centers_ref[b, h, 1:2, :]) * (far_part / whole)
            attended_ref[rows, columns] = value.astype(bf16)
    chunks, _, columns = mixed_ref.shape
    copies = []
    for c in range(chunks):
        place = slice(c * columns, (c + 1) * columns)
        mixed_ref[c] = dot(attended_ref[...], w_ref[:, place]).astype(bf16)
        copy = pltpu.make_async_copy(mixed_ref.at[c], mixed_hbm.at[:, place], sem.at[c])
        copy.start()
        copies.append(copy)
    first = samples * tokens
    sums = [
        ref[first : first + SUM_ROWS, :].astype(f32)
        + ref[first + SUM_ROWS : first + 2 * SUM_ROWS, :].astype(f32)
        for ref in (half_ref, back_ref)
    ]
    fresh = (sums[0] + sums[1]) * (1.0 / length)
    for b in range(samples):
        for h in range(heads):
            for j in range(2):
                row = (b * heads + h) * 2 + j
                old = centers_ref[b, h, j : j + 1, :]
                new_ref[b, h, j : j + 1, :] = jnp.where(
                    refresh_ref[j, h] == 1, fresh[row : row + 1, :], old
                )
    for copy in copies:
        copy.wait()


VMEM = pl.BlockSpec(memory_space=pltpu.VMEM)
HBM = pl.BlockSpec(memory_space=pltpu.HBM)


def per_device(
    images, w_qkv, b_qkv, q_gain, k_gain, key_basis, value_basis, centers, refresh, w_out
):
    samples, tokens, model = images.shape
    heads, dim, rank = key_basis.shape
    seq = lax.axis_size("seq")
    rows = samples * tokens
    width = heads * dim
    sizes = dict(samples=samples, tokens=tokens, heads=heads, dim=dim)
    log_factor = log2_e / math.sqrt(dim)
    flat = images.reshape(rows, model)
    key_rows = key_basis.transpose(0, 2, 1)
    value_rows = value_basis.transpose(0, 2, 1)
    center_rows = centers.transpose(0, 2, 1, 3)
    chunks = 6
    depth = model // chunks
    shard = (1, tokens + SUM_ROWS, width)
    params = lambda mib: pltpu.CompilerParams(vmem_limit_bytes=mib * 2**20)

    payload, query, qkv = pl.pallas_call(
        functools.partial(project_kernel, **sizes, rank=rank, log_factor=log_factor),
        in_specs=[HBM] * 8,
        out_specs=[VMEM] * 3,
        out_shape=[
            jax.ShapeDtypeStruct(shard, bf16),
            jax.ShapeDtypeStruct((tokens, width), bf16),
            jax.ShapeDtypeStruct((rows, 3 * width), f32),
        ],
        scratch_shapes=[
            pltpu.VMEM((chunks, rows, depth), bf16),
            pltpu.VMEM((chunks, depth, 3 * width), bf16),
            pltpu.VMEM((3 * heads, dim), f32),
            pltpu.VMEM((1, dim), f32),
            pltpu.VMEM((1, dim), f32),
            pltpu.VMEM((heads, rank, dim), f32),
            pltpu.VMEM((heads, rank, dim), f32),
            pltpu.VMEM((samples, heads, 2, dim), f32),
            pltpu.VMEM((rows, 3 * width), f32),
            pltpu.VMEM((samples, dim, width + dim), bf16),
            pltpu.VMEM((samples, dim, width + dim), bf16),
            pltpu.VMEM((dim, width - dim), bf16),
            pltpu.VMEM((dim, width - dim), bf16),
            pltpu.VMEM((SUM_ROWS, dim), f32),
            pltpu.SemaphoreType.DMA((2, chunks)),
            pltpu.SemaphoreType.DMA((6,)),
        ],
        compiler_params=params(32),
        name="project",
    )(
        *(
            pltpu.with_memory_space_constraint(x, pltpu.HBM)
            for x in (
                flat, w_qkv, b_qkv.reshape(3 * heads, dim), q_gain.reshape(1, -1),
                k_gain.reshape(1, -1), key_rows, value_rows, center_rows,
            )
        )
    )

    def swap(x, mask):
        return lax.ppermute(x, "seq", [(i, i ^ mask) for i in range(seq)])

    far_mask = seq // 2
    bits = [m for m in (2**i for i in range(1, seq.bit_length() - 1)) if m < far_mask]
    held = [(payload, [0])]
    direct = sum(bits[:2])
    for mask in range(2, 2 * direct, 2):
        if mask & ~direct == 0:
            held.append((swap(payload, mask), [mask]))
    for bit in bits[2:]:
        block = jnp.concatenate([a for a, _ in held], axis=0)
        names = [m for _, ms in held for m in ms]
        held.append((swap(block, bit), [m ^ bit for m in names]))

    query_far = swap(query, far_mask)

    near, stats = pl.pallas_call(
        functools.partial(near_kernel, **sizes),
        in_specs=[VMEM, VMEM],
        out_specs=[VMEM, VMEM],
        out_shape=[
            jax.ShapeDtypeStruct((rows, width), f32),
            jax.ShapeDtypeStruct((rows, dim), f32),
        ],
        compiler_params=params(24),
        cost_estimate=pl.CostEstimate(
            flops=1200 * rows * tokens * width, bytes_accessed=50 * rows * width * 4, transcendentals=0
        ),
        name="near",
    )(qkv, center_rows)

    for i in range(1, len(held)):
        x, _, _ = lax.optimization_barrier((held[i][0], stats, query_far))
        held[i] = (x, held[i][1])
    held += [(swap(a, 1), [m ^ 1 for m in ms]) for a, ms in held]
    arrays = [a for a, _ in held]
    names = [m for _, ms in held for m in ms]
    order = tuple(names.index(m) for m in range(len(names)))
    cost = pl.CostEstimate(
        flops=8 * rows * tokens * len(names) * width,
        bytes_accessed=len(names) * 2 * tokens * width,
        transcendentals=0,
    )
    back = pl.pallas_call(
        functools.partial(partner_kernel, **sizes, rank=rank, order=order),
        in_specs=[VMEM] * (1 + len(arrays)) + [pl.BlockSpec(memory_space=pl.ANY)],
        out_specs=VMEM,
        out_shape=jax.ShapeDtypeStruct((rows + 2 * SUM_ROWS, dim), bf16),
        compiler_params=params(32),
        cost_estimate=cost,
        name="partner",
    )(query_far, *arrays, stats)
    returned = swap(back, far_mask)
    merged, logs = pl.pallas_call(
        functools.partial(own_kernel, **sizes, rank=rank),
        in_specs=[VMEM] * (4 + len(arrays)),
        out_specs=[VMEM, VMEM],
        out_shape=[
            jax.ShapeDtypeStruct((rows, width), f32),
            jax.ShapeDtypeStruct((rows, dim), f32),
        ],
        scratch_shapes=[
            pltpu.VMEM((samples, dim, width), bf16),
            pltpu.VMEM((samples, dim, width), bf16),
        ],
        compiler_params=params(32),
        cost_estimate=cost,
        name="own",
    )(query, near, stats, center_rows, value_rows, *arrays[1:])

    columns = 512
    mixed, new_centers = pl.pallas_call(
        functools.partial(finish_kernel, **sizes, rank=rank, length=tokens * seq),
        in_specs=[VMEM] * 5 + [pl.BlockSpec(memory_space=pltpu.SMEM), VMEM, VMEM],
        out_specs=[HBM, VMEM],
        out_shape=[
            jax.ShapeDtypeStruct((rows, model), bf16),
            jax.ShapeDtypeStruct((samples, heads, 2, dim), f32),
        ],
        scratch_shapes=[
            pltpu.VMEM((rows, width), bf16),
            pltpu.VMEM((samples, dim, width), bf16),
            pltpu.VMEM((samples, dim, width), bf16),
            pltpu.VMEM((model // columns, rows, columns), bf16),
            pltpu.SemaphoreType.DMA((model // columns,)),
        ],
        compiler_params=params(24),
        name="finish",
    )(returned, back, merged, logs, center_rows, refresh, value_rows, w_out)
    return (mixed.reshape(samples, tokens, model), new_centers.transpose(0, 2, 1, 3))


def solution(mesh):
    return jax.shard_map(
        per_device,
        mesh=mesh,
        in_specs=(
            P("groups", "seq", None),
            P(),
            P(),
            P(),
            P(),
            P(),
            P(),
            P("groups", None, None, None),
            P(),
            P(),
        ),
        out_specs=(P("groups", "seq", None), P("groups", None, None, None)),
        check_vma=False,
    )
```

```python
import functools
import math

import jax
import jax.numpy as jnp
from jax import lax
from jax.experimental import pallas as pl
from jax.experimental.pallas import tpu as pltpu
from jax.sharding import PartitionSpec as P

epsilon = 1e-06
log2_e = math.log2(math.e)
f32 = jnp.float32
bf16 = jnp.bfloat16
SUM_ROWS = 16
NT = (((1,), (1,)), ((), ()))
NN = (((1,), (0,)), ((), ()))


def dot(a, b, dims=NN):
    return lax.dot_general(a, b, dims, preferred_element_type=f32)


def split(x):
    high = x.astype(bf16)
    low = (x - high.astype(f32)).astype(bf16)
    return high, low


def dot3(a, b, dims=NN):
    return dot(a[0], b[0], dims) + (dot(a[0], b[1], dims) + dot(a[1], b[0], dims))


def pieces_of(x, count):
    out = []
    for _ in range(count):
        top = x.astype(bf16)
        out.append(top)
        x = x - top.astype(f32)
    return out


def lane_ids(rows, lanes):
    return lax.broadcasted_iota(jnp.int32, (rows, lanes), 1)


def key_lane(sample, head, rank):
    return head * rank if sample == 0 else (head + 1) * rank


def value_lane(sample, head, rank, heads):
    if head == 0:
        return heads * rank if sample == 0 else 0
    return ((heads - 1) * sample + head - 1) * rank


def free_lane(sample, rank):
    return 2 * rank if sample == 0 else rank


def within(lanes, start, count):
    return (lanes >= start) & (lanes < start + count)


def fill_basis(basis_h, basis_l, vb_ref, samples, heads, dim, rank):
    basis_h[...] = jnp.zeros_like(basis_h)
    basis_l[...] = jnp.zeros_like(basis_l)
    for h in range(heads):
        vh, vl = split(vb_ref[h])
        for b in range(samples):
            at = value_lane(b, h, rank, heads)
            basis_h[b, at : at + rank, h * dim : (h + 1) * dim] = vh
            basis_l[b, at : at + rank, h * dim : (h + 1) * dim] = vl


def project_kernel(
    images_hbm, w_hbm, b_hbm, qg_hbm, kg_hbm, kb_hbm, vb_hbm, centers_hbm,
    payload_ref, query_ref, qkv_ref,
    x_ref, w_ref, b_ref, qg_ref, kg_ref, kb_ref, vb_ref, centers_ref,
    acc_ref, main_ref, tail_ref, sums_ref, big_sem, small_sem,
    *, samples, tokens, heads, dim, rank, log_factor,
):
    chunks, _, depth = x_ref.shape
    width = heads * dim

    def x_copy(c):
        columns = pl.ds(pl.multiple_of(c * depth, depth), depth)
        return pltpu.make_async_copy(images_hbm.at[:, columns], x_ref.at[c], big_sem.at[0, c])

    def w_copy(c):
        some = pl.ds(pl.multiple_of(c * depth, depth), depth)
        return pltpu.make_async_copy(w_hbm.at[some, :], w_ref.at[c], big_sem.at[1, c])

    small = [
        pltpu.make_async_copy(source, target, small_sem.at[i])
        for i, (source, target) in enumerate(
            [
                (kb_hbm, kb_ref), (vb_hbm, vb_ref), (b_hbm, b_ref),
                (qg_hbm, qg_ref), (kg_hbm, kg_ref), (centers_hbm, centers_ref),
            ]
        )
    ]
    for c in range(chunks):
        x_copy(c).start()
        w_copy(c).start()
    for copy in small:
        copy.start()
    main_ref[...] = jnp.zeros_like(main_ref)
    tail_ref[...] = jnp.zeros_like(tail_ref)
    sums_ref[...] = jnp.zeros_like(sums_ref)
    for c in range(chunks):
        x_copy(c).wait()
        w_copy(c).wait()
        part = dot(x_ref[c], w_ref[c])
        if c == 0:
            acc_ref[...] = part
        else:
            acc_ref[...] += part

    for copy in small:
        copy.wait()
    half = dim // 2
    for h in range(heads):
        for p, (k, v) in enumerate(zip(split(kb_ref[h]), split(vb_ref[h]))):
            at = p * dim + key_lane(0, h, rank)
            main_ref[at : at + rank, h * dim : (h + 1) * dim] = k
            at = value_lane(0, h, rank, heads)
            if h == 0:
                main_ref[p * dim + at : p * dim + at + rank, width:] = v
            else:
                at = p * half + at
                tail_ref[at : at + rank, (h - 1) * dim : h * dim] = v
    def column(at):
        return acc_ref[:, at * dim : (at + 1) * dim] + b_ref[at : at + 1, :]

    def normed(at, gain):
        x = column(at)
        mean_square = jnp.mean(x * x, axis=-1, keepdims=True)
        return x * lax.rsqrt(mean_square + epsilon) * gain

    queries, keys, values = [], [], []
    for h in range(heads):
        q = normed(h, qg_ref[...])
        k = normed(heads + h, kg_ref[...])
        v = column(2 * heads + h)
        queries.append(q)
        keys.append(k)
        values.append(v)
        for b in range(samples):
            rows = slice(b * tokens, (b + 1) * tokens)
            row = (b * heads + h) * 2
            sums_ref[row : row + 1, :] = jnp.sum(k[rows], axis=0, keepdims=True)
            sums_ref[row + 1 : row + 2, :] = jnp.sum(v[rows], axis=0, keepdims=True)
    for p, piece in enumerate(pieces_of(sums_ref[...], 3)):
        payload_ref[0, tokens : tokens + SUM_ROWS, p * dim : (p + 1) * dim] = piece
    def by_sample(j):
        rows = [centers_ref[b, h, j : j + 1, :] for b in range(samples) for h in range(heads)]
        return [
            jnp.concatenate(
                [jnp.broadcast_to(rows[b * heads + h], (tokens, dim)) for b in range(samples)], axis=0
            )
            for h in range(heads)
        ]

    key_centers, value_centers = by_sample(0), by_sample(1)
    shifted = [keys[h] - key_centers[h] for h in range(heads)]
    shifted += [values[h] - value_centers[h] for h in range(heads)]

    def coded(x, columns):
        high, low = split(x)
        both = dot(high, main_ref[:, columns], NT)
        return both[:, :dim] + (both[:, dim:] + dot(low, main_ref[:dim, columns], NT))

    code = coded(jnp.concatenate(shifted[: heads + 1], axis=1), slice(0, width + dim))
    query_code = coded(jnp.concatenate(queries, axis=1), slice(0, width)) * log_factor
    high, low = split(jnp.concatenate(shifted[heads + 1 :], axis=1))
    both = dot(high, tail_ref[...], NT)
    tail = both + pltpu.roll(both, half, 1) + dot(low, tail_ref[...], NT)
    payload_ref[0, :tokens, :dim] = code[:tokens].astype(bf16)
    payload_ref[0, :tokens, dim : 2 * dim] = pltpu.roll(code[tokens:], rank, 1).astype(bf16)
    lanes = lane_ids(tokens, dim)
    last = jnp.where(lanes < half, tail[:tokens], pltpu.roll(tail[tokens:], half, 1))
    payload_ref[0, :tokens, samples * dim :] = last.astype(bf16)
    high_0 = query_code[:tokens].astype(bf16).astype(f32)
    low_0 = query_code[:tokens] - high_0
    query_1 = pltpu.roll(query_code[tokens:], rank, 1)
    high_1 = query_1.astype(bf16).astype(f32)
    low_1 = query_1 - high_1
    turned = pltpu.roll(low_1, half, 1)
    query_ref[:, :dim] = jnp.where(lanes < heads * rank, high_0, turned).astype(bf16)
    query_ref[:, dim : 2 * dim] = jnp.where(lanes < rank, turned, high_1).astype(bf16)
    query_ref[:, 2 * dim :] = jnp.where(lanes < heads * rank, low_0, low_1).astype(bf16)
    for h in range(heads):
        qkv_ref[:, h * dim : (h + 1) * dim] = queries[h] * log_factor
        qkv_ref[:, width + h * dim : width + (h + 1) * dim] = keys[h]
        qkv_ref[:, 2 * width + h * dim : 2 * width + (h + 1) * dim] = values[h]


def near_kernel(
    qkv_ref, centers_ref, refresh_ref, vb_ref, near_ref, stat_ref, basis_h, basis_l, old_ref,
    *, samples, tokens, heads, dim, rank,
):
    width = heads * dim
    fill_basis(basis_h, basis_l, vb_ref, samples, heads, dim, rank)
    old_ref[...] = jnp.zeros_like(old_ref)
    for b in range(samples):
        for h in range(heads):
            for j in range(2):
                row = (b * heads + h) * 2 + j
                keep = jnp.where(refresh_ref[j, h] == 1, 0.0, 1.0)
                old_ref[row : row + 1, :] = centers_ref[b, h, j : j + 1, :]
                old_ref[SUM_ROWS + row : SUM_ROWS + row + 1, :] = jnp.full((1, dim), keep, f32)
    lanes = lane_ids(tokens, dim)
    for b in range(samples):
        rows = slice(b * tokens, (b + 1) * tokens)
        stats = jnp.zeros((tokens, dim), f32)
        for h in range(heads):
            q = qkv_ref[rows, h * dim : (h + 1) * dim]
            k = split(qkv_ref[rows, width + h * dim : width + (h + 1) * dim])
            v = split(qkv_ref[rows, 2 * width + h * dim : 2 * width + (h + 1) * dim])
            scores = dot3(split(q), k, NT)
            row_max = jnp.max(scores, axis=-1, keepdims=True)
            weights = jnp.exp2(scores - row_max)
            row_sum = jnp.sum(weights, axis=-1, keepdims=True)
            near_ref[rows, h * dim : (h + 1) * dim] = dot3(split(weights), v) / row_sum
            center = jnp.sum(q * centers_ref[b, h, 0:1, :], axis=-1, keepdims=True)
            stats = jnp.where(lanes == h, row_max + jnp.log(row_sum) * log2_e, stats)
            stats = jnp.where(lanes == heads + h, center, stats)
        stat_ref[rows, :] = stats


def query_parts(query_ref, sample, heads, dim, rank):
    lanes = lane_ids(query_ref.shape[0], dim)
    if sample == 0:
        return query_ref[:, :dim].astype(f32), query_ref[:, 2 * dim :].astype(f32)
    first, second = query_ref[:, :dim].astype(f32), query_ref[:, dim : 2 * dim].astype(f32)
    turned = pltpu.roll(jnp.where(lanes < rank, second, first), dim // 2, 1)
    return second, jnp.where(lanes < heads * rank, turned, query_ref[:, 2 * dim :].astype(f32))


def code_attention(query_ref, tiles, b, *, samples, tokens, heads, dim, rank):
    lanes = lane_ids(tokens, dim)
    high, low = query_parts(query_ref, b, heads, dim, rank)
    stacked = []
    for h in range(heads):
        own = within(lanes, key_lane(b, h, rank), rank)
        both = [jnp.where(own, part, 0.0).astype(bf16) for part in (high, low)]
        stacked.append(jnp.concatenate(both, axis=1))
    left = jnp.concatenate(stacked, axis=0)
    scores, values = [], []
    for ref, i in tiles:
        code = ref[i, :tokens, b * dim : (b + 1) * dim]
        scores.append(dot(left, jnp.concatenate([code, code], axis=1), NT))
        values.append(jnp.concatenate([code, ref[i, :tokens, samples * dim :]], axis=1))
    best = scores[0]
    for part in scores[1:]:
        best = jnp.maximum(best, part)
    row_max = jnp.max(best, axis=-1, keepdims=True)
    total = jnp.zeros_like(best)
    weights = []
    for part in scores:
        weight = jnp.exp2(part - row_max).astype(bf16)
        total = total + weight.astype(f32)
        weights.append(weight)
    result = dot(jnp.concatenate(weights, axis=1), jnp.concatenate(values, axis=0))
    row_sum = jnp.sum(total, axis=-1, keepdims=True)
    result = result / row_sum
    log_sum = row_max + jnp.log(row_sum) * log2_e
    out = jnp.zeros((tokens, dim), f32)
    logs = []
    for h in range(heads):
        head_rows = slice(h * tokens, (h + 1) * tokens)
        part = result[head_rows, :dim] if h == 0 else result[head_rows, dim:]
        out = jnp.where(within(lanes, value_lane(b, h, rank, heads), rank), part, out)
        logs.append(log_sum[head_rows])
    return out, logs


def tree_sum(parts):
    while len(parts) > 1:
        parts = [parts[i] + parts[i + 1] for i in range(0, len(parts), 2)]
    return parts[0]


def tiles_of(refs):
    return [(ref, i) for ref in refs for i in range(ref.shape[0])]


def partner_kernel(query_ref, *refs, order, samples, tokens, heads, dim, rank):
    out_ref = refs[-1]
    tiles = tiles_of(refs[:-2])
    parts = []
    for place in order:
        ref, i = tiles[place]
        rows = slice(tokens, tokens + SUM_ROWS)
        pieces = [ref[i, rows, p * dim : (p + 1) * dim].astype(f32) for p in range(3)]
        parts.append(pieces[0] + (pieces[1] + pieces[2]))
    first = samples * tokens
    for p, piece in enumerate(pieces_of(tree_sum(parts), 2)):
        out_ref[first + p * SUM_ROWS : first + (p + 1) * SUM_ROWS, :] = piece
    lanes = lane_ids(tokens, dim)
    for b in range(samples):
        out, logs = code_attention(
            query_ref, tiles, b, samples=samples, tokens=tokens, heads=heads, dim=dim, rank=rank
        )
        for h in range(heads):
            for p, piece in enumerate(pieces_of(logs[h], 3)):
                out = jnp.where(lanes == free_lane(b, rank) + 3 * h + p, piece.astype(f32), out)
        out_ref[b * tokens : (b + 1) * tokens, :] = out.astype(bf16)


def own_kernel(
    query_ref, near_ref, stat_ref, old_ref, basis_h, basis_l, *refs,
    samples, tokens, heads, dim, rank,
):
    merged_ref, log_ref = refs[-2:]
    tiles = tiles_of(refs[:-2])
    lanes = lane_ids(tokens, dim)
    for b in range(samples):
        rows = slice(b * tokens, (b + 1) * tokens)
        out, logs = code_attention(
            query_ref, tiles, b, samples=samples, tokens=tokens, heads=heads, dim=dim, rank=rank
        )
        far = dot3(split(out), (basis_h[b], basis_l[b]))
        stats = stat_ref[rows, :]
        kept = jnp.zeros((tokens, dim), f32)
        for h in range(heads):
            columns = slice(h * dim, (h + 1) * dim)
            near_log = stats[:, h : h + 1]
            center = stats[:, heads + h : heads + h + 1]
            far_log = logs[h] + center
            top = jnp.maximum(near_log, far_log)
            near_part, far_part = jnp.exp2(near_log - top), jnp.exp2(far_log - top)
            whole = near_part + far_part
            merged = near_ref[rows, columns] * (near_part / whole)
            row = (b * heads + h) * 2 + 1
            merged = merged + (far[:, columns] + old_ref[row : row + 1, :]) * (far_part / whole)
            merged_ref[rows, columns] = merged
            kept = jnp.where(lanes == h, top + jnp.log(whole) * log2_e, kept)
            kept = jnp.where(lanes == heads + h, center, kept)
        log_ref[rows, :] = kept


def finish_kernel(
    back_ref, half_ref, merged_ref, log_ref, old_ref, basis_h, basis_l, w_ref,
    mixed_hbm, new_hbm, attended_ref, mixed_ref, new_ref, sem, new_sem,
    *, samples, tokens, heads, dim, rank, length,
):
    first = samples * tokens
    sums = [
        ref[first : first + SUM_ROWS, :].astype(f32)
        + ref[first + SUM_ROWS : first + 2 * SUM_ROWS, :].astype(f32)
        for ref in (half_ref, back_ref)
    ]
    fresh = (sums[0] + sums[1]) * (1.0 / length)
    fresh = jnp.where(old_ref[SUM_ROWS:, :] > 0.5, old_ref[:SUM_ROWS, :], fresh)
    for b in range(samples):
        for h in range(heads):
            row = (b * heads + h) * 2
            new_ref[b, h] = fresh[row : row + 2, :]
    new_copy = pltpu.make_async_copy(new_ref, new_hbm, new_sem.at[0])
    new_copy.start()
    chunks, columns = mixed_ref.shape[1], mixed_ref.shape[3]
    copies = []
    for b in range(samples):
        rows = slice(b * tokens, (b + 1) * tokens)
        codes = back_ref[rows, :]
        far = dot(codes, basis_h[b]) + dot(codes, basis_l[b])
        extra = codes.astype(f32)
        logs = log_ref[rows, :]
        for h in range(heads):
            head = slice(h * dim, (h + 1) * dim)
            spot = free_lane(b, rank) + 3 * h
            far_log = extra[:, spot : spot + 1] + (
                extra[:, spot + 1 : spot + 2] + extra[:, spot + 2 : spot + 3]
            )
            far_log = far_log + logs[:, heads + h : heads + h + 1]
            own_log = logs[:, h : h + 1]
            top = jnp.maximum(own_log, far_log)
            own_part, far_part = jnp.exp2(own_log - top), jnp.exp2(far_log - top)
            whole = own_part + far_part
            row = (b * heads + h) * 2 + 1
            value = merged_ref[rows, head] * (own_part / whole)
            value = value + (far[:, head] + old_ref[row : row + 1, :]) * (far_part / whole)
            attended_ref[rows, head] = value.astype(bf16)
        for c in range(chunks):
            place = slice(c * columns, (c + 1) * columns)
            mixed_ref[b, c] = dot(attended_ref[rows, :], w_ref[:, place]).astype(bf16)
            copy = pltpu.make_async_copy(
                mixed_ref.at[b, c], mixed_hbm.at[rows, place], sem.at[b, c]
            )
            copy.start()
            copies.append(copy)
    for copy in copies + [new_copy]:
        copy.wait()


VMEM = pl.BlockSpec(memory_space=pltpu.VMEM)
HBM = pl.BlockSpec(memory_space=pltpu.HBM)


def per_device(
    images, w_qkv, b_qkv, q_gain, k_gain, key_basis, value_basis, centers, refresh, w_out
):
    samples, tokens, model = images.shape
    heads, dim, rank = key_basis.shape
    seq = lax.axis_size("seq")
    rows = samples * tokens
    width = heads * dim
    sizes = dict(samples=samples, tokens=tokens, heads=heads, dim=dim)
    log_factor = log2_e / math.sqrt(dim)
    flat = images.reshape(rows, model)
    key_rows = key_basis.transpose(0, 2, 1)
    value_rows = value_basis.transpose(0, 2, 1)
    center_rows = centers.transpose(0, 2, 1, 3)
    chunks = 3
    depth = model // chunks
    shard = (1, tokens + SUM_ROWS, width)
    params = lambda mib: pltpu.CompilerParams(vmem_limit_bytes=mib * 2**20)

    payload, query, qkv = pl.pallas_call(
        functools.partial(project_kernel, **sizes, rank=rank, log_factor=log_factor),
        in_specs=[HBM] * 8,
        out_specs=[VMEM] * 3,
        out_shape=[
            jax.ShapeDtypeStruct(shard, bf16),
            jax.ShapeDtypeStruct((tokens, width), bf16),
            jax.ShapeDtypeStruct((rows, 3 * width), f32),
        ],
        scratch_shapes=[
            pltpu.VMEM((chunks, rows, depth), bf16),
            pltpu.VMEM((chunks, depth, 3 * width), bf16),
            pltpu.VMEM((3 * heads, dim), f32),
            pltpu.VMEM((1, dim), f32),
            pltpu.VMEM((1, dim), f32),
            pltpu.VMEM((heads, rank, dim), f32),
            pltpu.VMEM((heads, rank, dim), f32),
            pltpu.VMEM((samples, heads, 2, dim), f32),
            pltpu.VMEM((rows, 3 * width), f32),
            pltpu.VMEM((2 * dim, width + dim), bf16),
            pltpu.VMEM((dim, width - dim), bf16),
            pltpu.VMEM((SUM_ROWS, dim), f32),
            pltpu.SemaphoreType.DMA((2, chunks)),
            pltpu.SemaphoreType.DMA((6,)),
        ],
        compiler_params=params(32),
        name="project",
    )(
        *(
            pltpu.with_memory_space_constraint(x, pltpu.HBM)
            for x in (
                flat, w_qkv, b_qkv.reshape(3 * heads, dim), q_gain.reshape(1, -1),
                k_gain.reshape(1, -1), key_rows, value_rows, center_rows,
            )
        )
    )

    def swap(x, mask):
        return lax.ppermute(x, "seq", [(i, i ^ mask) for i in range(seq)])

    far_mask = seq // 2
    bits = [m for m in (2**i for i in range(1, seq.bit_length() - 1)) if m < far_mask]
    held = [(payload, [0])]
    direct = sum(bits[:2])
    for mask in range(2, 2 * direct, 2):
        if mask & ~direct == 0:
            held.append((swap(payload, mask), [mask]))
    for bit in bits[2:]:
        block = jnp.concatenate([a for a, _ in held], axis=0)
        names = [m for _, ms in held for m in ms]
        held.append((swap(block, bit), [m ^ bit for m in names]))

    query_far = swap(query, far_mask)

    near, stats, basis_high, basis_low, old = pl.pallas_call(
        functools.partial(near_kernel, **sizes, rank=rank),
        in_specs=[VMEM, VMEM, pl.BlockSpec(memory_space=pltpu.SMEM), VMEM],
        out_specs=[VMEM] * 5,
        out_shape=[
            jax.ShapeDtypeStruct((rows, width), f32),
            jax.ShapeDtypeStruct((rows, dim), f32),
            jax.ShapeDtypeStruct((samples, dim, width), bf16),
            jax.ShapeDtypeStruct((samples, dim, width), bf16),
            jax.ShapeDtypeStruct((2 * SUM_ROWS, dim), f32),
        ],
        compiler_params=params(24),
        cost_estimate=pl.CostEstimate(
            flops=1200 * rows * tokens * width, bytes_accessed=50 * rows * width * 4, transcendentals=0
        ),
        name="near",
    )(qkv, center_rows, refresh, value_rows)

    for i in range(1, len(held)):
        x, _, _ = lax.optimization_barrier((held[i][0], stats, query_far if i == 1 else stats))
        held[i] = (x, held[i][1])
    held += [(swap(a, 1), [m ^ 1 for m in ms]) for a, ms in held]
    arrays = [a for a, _ in held]
    names = [m for _, ms in held for m in ms]
    order = tuple(names.index(m) for m in range(len(names)))
    cost = pl.CostEstimate(
        flops=8 * rows * tokens * len(names) * width,
        bytes_accessed=len(names) * 2 * tokens * width,
        transcendentals=0,
    )
    back = pl.pallas_call(
        functools.partial(partner_kernel, **sizes, rank=rank, order=order),
        in_specs=[VMEM] * (1 + len(arrays)) + [pl.BlockSpec(memory_space=pl.ANY)],
        out_specs=VMEM,
        out_shape=jax.ShapeDtypeStruct((rows + 2 * SUM_ROWS, dim), bf16),
        compiler_params=params(32),
        cost_estimate=cost,
        name="partner",
    )(query_far, *arrays, stats)
    returned = swap(back, far_mask)
    merged, logs = pl.pallas_call(
        functools.partial(own_kernel, **sizes, rank=rank),
        in_specs=[VMEM] * (5 + len(arrays)),
        out_specs=[VMEM] * 2,
        out_shape=[
            jax.ShapeDtypeStruct((rows, width), f32),
            jax.ShapeDtypeStruct((rows, dim), f32),
        ],
        compiler_params=params(32),
        cost_estimate=cost,
        name="own",
    )(query, near, stats, old, basis_high, basis_low, *arrays[1:])

    columns = 768
    mixed, new_centers = pl.pallas_call(
        functools.partial(finish_kernel, **sizes, rank=rank, length=tokens * seq),
        in_specs=[VMEM] * 8,
        out_specs=[HBM, HBM],
        out_shape=[
            jax.ShapeDtypeStruct((rows, model), bf16),
            jax.ShapeDtypeStruct((samples, heads, 2, dim), f32),
        ],
        scratch_shapes=[
            pltpu.VMEM((rows, width), bf16),
            pltpu.VMEM((samples, model // columns, tokens, columns), bf16),
            pltpu.VMEM((samples, heads, 2, dim), f32),
            pltpu.SemaphoreType.DMA((samples, model // columns)),
            pltpu.SemaphoreType.DMA((1,)),
        ],
        compiler_params=params(24),
        name="finish",
    )(returned, back, merged, logs, old, basis_high, basis_low, w_out)
    return (mixed.reshape(samples, tokens, model), new_centers.transpose(0, 2, 1, 3))


def solution(mesh):
    return jax.shard_map(
        per_device,
        mesh=mesh,
        in_specs=(
            P("groups", "seq", None),
            P(),
            P(),
            P(),
            P(),
            P(),
            P(),
            P("groups", None, None, None),
            P(),
            P(),
        ),
        out_specs=(P("groups", "seq", None), P("groups", None, None, None)),
        check_vma=False,
    )
```

```python
import functools
import math

import jax
import jax.numpy as jnp
from jax import lax
from jax.experimental import pallas as pl
from jax.experimental.pallas import tpu as pltpu
from jax.sharding import PartitionSpec as P

epsilon = 1e-06
log2_e = math.log2(math.e)
f32 = jnp.float32
bf16 = jnp.bfloat16
SUM_ROWS = 16
NT = (((1,), (1,)), ((), ()))
NN = (((1,), (0,)), ((), ()))


def dot(a, b, dims=NN):
    return lax.dot_general(a, b, dims, preferred_element_type=f32)


def split(x):
    high = x.astype(bf16)
    low = (x - high.astype(f32)).astype(bf16)
    return high, low


def dot3(a, b, dims=NN):
    return dot(a[0], b[0], dims) + (dot(a[0], b[1], dims) + dot(a[1], b[0], dims))


def pieces_of(x, count):
    out = []
    for _ in range(count):
        top = x.astype(bf16)
        out.append(top)
        x = x - top.astype(f32)
    return out


def lane_ids(rows, lanes):
    return lax.broadcasted_iota(jnp.int32, (rows, lanes), 1)


def key_lane(sample, head, rank):
    return head * rank if sample == 0 else (head + 1) * rank


def value_lane(sample, head, rank, heads):
    if head == 0:
        return heads * rank if sample == 0 else 0
    return ((heads - 1) * sample + head - 1) * rank


def free_lane(sample, rank):
    return 2 * rank if sample == 0 else rank


def log_lane(sample, head, piece, rank):
    return free_lane(sample, rank) + 8 * piece + head


def sum_lane(sample, rank):
    return free_lane(sample, rank) + 20


def within(lanes, start, count):
    return (lanes >= start) & (lanes < start + count)


def fill_basis(basis_h, basis_l, vb_ref, samples, heads, dim, rank):
    basis_h[...] = jnp.zeros_like(basis_h)
    basis_l[...] = jnp.zeros_like(basis_l)
    for h in range(heads):
        vh, vl = split(vb_ref[h])
        for b in range(samples):
            at = value_lane(b, h, rank, heads)
            basis_h[b, at : at + rank, h * dim : (h + 1) * dim] = vh
            basis_l[b, at : at + rank, h * dim : (h + 1) * dim] = vl


def project_kernel(
    images_hbm, w_hbm, b_hbm, qg_hbm, kg_hbm, kb_hbm, vb_hbm, centers_hbm,
    payload_ref, query_ref, qkv_ref,
    x_ref, w_ref, b_ref, qg_ref, kg_ref, kb_ref, vb_ref, centers_ref,
    acc_ref, main_ref, tail_ref, sums_ref, big_sem, small_sem,
    *, samples, tokens, heads, dim, rank, log_factor, cuts,
):
    width = heads * dim
    places = [slice(first, last) for first, last in zip(cuts[:-1], cuts[1:])]

    def x_copy(c):
        p = places[c]
        return pltpu.make_async_copy(images_hbm.at[:, p], x_ref.at[:, p], big_sem.at[0, c])

    def w_copy(c):
        p = places[c]
        return pltpu.make_async_copy(w_hbm.at[p, :], w_ref.at[p, :], big_sem.at[1, c])

    small = [
        pltpu.make_async_copy(source, target, small_sem.at[i])
        for i, (source, target) in enumerate(
            [
                (kb_hbm, kb_ref), (vb_hbm, vb_ref), (b_hbm, b_ref),
                (qg_hbm, qg_ref), (kg_hbm, kg_ref), (centers_hbm, centers_ref),
            ]
        )
    ]
    for copy in small:
        copy.start()
    for c in range(len(places)):
        x_copy(c).start()
        w_copy(c).start()
    main_ref[...] = jnp.zeros_like(main_ref)
    tail_ref[...] = jnp.zeros_like(tail_ref)
    sums_ref[...] = jnp.zeros_like(sums_ref)
    half = dim // 2

    def build():
        for copy in small:
            copy.wait()
        for h in range(heads):
            for p, (k, v) in enumerate(zip(split(kb_ref[h]), split(vb_ref[h]))):
                at = p * dim + key_lane(0, h, rank)
                main_ref[at : at + rank, h * dim : (h + 1) * dim] = k
                at = value_lane(0, h, rank, heads)
                if h == 0:
                    main_ref[p * dim + at : p * dim + at + rank, width:] = v
                else:
                    at = p * half + at
                    tail_ref[at : at + rank, (h - 1) * dim : h * dim] = v

    for c, place in enumerate(places):
        if c == len(places) - 1:
            build()
        x_copy(c).wait()
        w_copy(c).wait()
        part = dot(x_ref[:, place], w_ref[place, :])
        if c == 0:
            acc_ref[...] = part
        else:
            acc_ref[...] += part

    def column(at):
        return acc_ref[:, at * dim : (at + 1) * dim] + b_ref[at : at + 1, :]

    def normed(at, gain):
        x = column(at)
        mean_square = jnp.mean(x * x, axis=-1, keepdims=True)
        return x * lax.rsqrt(mean_square + epsilon) * gain

    queries, keys, values = [], [], []
    for h in range(heads):
        q = normed(h, qg_ref[...])
        k = normed(heads + h, kg_ref[...])
        v = column(2 * heads + h)
        queries.append(q)
        keys.append(k)
        values.append(v)
        for b in range(samples):
            rows = slice(b * tokens, (b + 1) * tokens)
            row = (b * heads + h) * 2
            sums_ref[row : row + 1, :] = jnp.sum(k[rows], axis=0, keepdims=True)
            sums_ref[row + 1 : row + 2, :] = jnp.sum(v[rows], axis=0, keepdims=True)
    for p, piece in enumerate(pieces_of(sums_ref[...], 3)):
        payload_ref[0, tokens : tokens + SUM_ROWS, p * dim : (p + 1) * dim] = piece
    def by_sample(j):
        rows = [centers_ref[b, h, j : j + 1, :] for b in range(samples) for h in range(heads)]
        return [
            jnp.concatenate(
                [jnp.broadcast_to(rows[b * heads + h], (tokens, dim)) for b in range(samples)], axis=0
            )
            for h in range(heads)
        ]

    key_centers, value_centers = by_sample(0), by_sample(1)
    shifted = [keys[h] - key_centers[h] for h in range(heads)]
    shifted += [values[h] - value_centers[h] for h in range(heads)]

    def coded(x, columns):
        high, low = split(x)
        both = dot(high, main_ref[:, columns], NT)
        return both[:, :dim] + (both[:, dim:] + dot(low, main_ref[:dim, columns], NT))

    code = coded(jnp.concatenate(shifted[: heads + 1], axis=1), slice(0, width + dim))
    query_code = coded(jnp.concatenate(queries, axis=1), slice(0, width)) * log_factor
    high, low = split(jnp.concatenate(shifted[heads + 1 :], axis=1))
    both = dot(high, tail_ref[...], NT)
    tail = both + pltpu.roll(both, half, 1) + dot(low, tail_ref[...], NT)
    payload_ref[0, :tokens, :dim] = code[:tokens].astype(bf16)
    payload_ref[0, :tokens, dim : 2 * dim] = pltpu.roll(code[tokens:], rank, 1).astype(bf16)
    lanes = lane_ids(tokens, dim)
    last = jnp.where(lanes < half, tail[:tokens], pltpu.roll(tail[tokens:], half, 1))
    payload_ref[0, :tokens, samples * dim :] = last.astype(bf16)
    high_0 = query_code[:tokens].astype(bf16).astype(f32)
    low_0 = query_code[:tokens] - high_0
    query_1 = pltpu.roll(query_code[tokens:], rank, 1)
    high_1 = query_1.astype(bf16).astype(f32)
    low_1 = query_1 - high_1
    turned = pltpu.roll(low_1, half, 1)
    query_ref[:, :dim] = jnp.where(lanes < heads * rank, high_0, turned).astype(bf16)
    query_ref[:, dim : 2 * dim] = jnp.where(lanes < rank, turned, high_1).astype(bf16)
    query_ref[:, 2 * dim :] = jnp.where(lanes < heads * rank, low_0, low_1).astype(bf16)
    for h in range(heads):
        qkv_ref[:, h * dim : (h + 1) * dim] = queries[h] * log_factor
        qkv_ref[:, width + h * dim : width + (h + 1) * dim] = keys[h]
        qkv_ref[:, 2 * width + h * dim : 2 * width + (h + 1) * dim] = values[h]


def near_kernel(
    qkv_ref, centers_ref, refresh_ref, vb_ref, near_ref, stat_ref, basis_h, basis_l, old_ref,
    *, samples, tokens, heads, dim, rank,
):
    width = heads * dim
    fill_basis(basis_h, basis_l, vb_ref, samples, heads, dim, rank)
    old_ref[...] = jnp.zeros_like(old_ref)
    for b in range(samples):
        for h in range(heads):
            for j in range(2):
                row = (b * heads + h) * 2 + j
                keep = jnp.where(refresh_ref[j, h] == 1, 0.0, 1.0)
                old_ref[row : row + 1, :] = centers_ref[b, h, j : j + 1, :]
                old_ref[SUM_ROWS + row : SUM_ROWS + row + 1, :] = jnp.full((1, dim), keep, f32)
    lanes = lane_ids(tokens, dim)
    for b in range(samples):
        rows = slice(b * tokens, (b + 1) * tokens)
        stats = jnp.zeros((tokens, dim), f32)
        for h in range(heads):
            q = qkv_ref[rows, h * dim : (h + 1) * dim]
            k = split(qkv_ref[rows, width + h * dim : width + (h + 1) * dim])
            v = split(qkv_ref[rows, 2 * width + h * dim : 2 * width + (h + 1) * dim])
            scores = dot3(split(q), k, NT)
            row_max = jnp.max(scores, axis=-1, keepdims=True)
            weights = jnp.exp2(scores - row_max)
            row_sum = jnp.sum(weights, axis=-1, keepdims=True)
            near_ref[rows, h * dim : (h + 1) * dim] = dot3(split(weights), v) / row_sum
            center = jnp.sum(q * centers_ref[b, h, 0:1, :], axis=-1, keepdims=True)
            stats = jnp.where(lanes == h, row_max + jnp.log(row_sum) * log2_e, stats)
            stats = jnp.where(lanes == heads + h, center, stats)
        stat_ref[rows, :] = stats


def query_parts(query_ref, sample, heads, dim, rank):
    lanes = lane_ids(query_ref.shape[0], dim)
    if sample == 0:
        return query_ref[:, :dim].astype(f32), query_ref[:, 2 * dim :].astype(f32)
    first, second = query_ref[:, :dim].astype(f32), query_ref[:, dim : 2 * dim].astype(f32)
    turned = pltpu.roll(jnp.where(lanes < rank, second, first), dim // 2, 1)
    return second, jnp.where(lanes < heads * rank, turned, query_ref[:, 2 * dim :].astype(f32))


def code_attention(query_ref, tiles, b, *, samples, tokens, heads, dim, rank):
    lanes = lane_ids(tokens, dim)
    high, low = query_parts(query_ref, b, heads, dim, rank)
    stacked = []
    for h in range(heads):
        own = within(lanes, key_lane(b, h, rank), rank)
        both = [jnp.where(own, part, 0.0).astype(bf16) for part in (high, low)]
        stacked.append(jnp.concatenate(both, axis=1))
    left = jnp.concatenate(stacked, axis=0)
    scores, values, codes = [], [], []
    for ref, i in tiles:
        code = ref[i, :tokens, b * dim : (b + 1) * dim]
        codes.append(jnp.concatenate([code, code], axis=1))
        values.append(jnp.concatenate([code, ref[i, :tokens, samples * dim :]], axis=1))
    for i in range(0, len(codes), 2):
        some = codes[i : i + 2]
        both = dot(left, jnp.concatenate(some, axis=0), NT)
        scores += [both[:, j * tokens : (j + 1) * tokens] for j in range(len(some))]
    best = scores[0]
    for part in scores[1:]:
        best = jnp.maximum(best, part)
    row_max = jnp.max(best, axis=-1, keepdims=True)
    total = jnp.zeros_like(best)
    weights = []
    for part in scores:
        weight = jnp.exp2(part - row_max).astype(bf16)
        total = total + weight.astype(f32)
        weights.append(weight)
    result = dot(jnp.concatenate(weights, axis=1), jnp.concatenate(values, axis=0))
    row_sum = jnp.sum(total, axis=-1, keepdims=True)
    result = result / row_sum
    log_sum = row_max + jnp.log(row_sum) * log2_e
    out = jnp.zeros((tokens, dim), f32)
    logs = []
    for h in range(heads):
        head_rows = slice(h * tokens, (h + 1) * tokens)
        part = result[head_rows, :dim] if h == 0 else result[head_rows, dim:]
        out = jnp.where(within(lanes, value_lane(b, h, rank, heads), rank), part, out)
        logs.append(log_sum[head_rows])
    return out, logs


def tree_sum(parts):
    while len(parts) > 1:
        parts = [parts[i] + parts[i + 1] for i in range(0, len(parts), 2)]
    return parts[0]


def tiles_of(refs):
    return [(ref, i) for ref in refs for i in range(ref.shape[0])]


def early_kernel(query_ref, *refs, samples, tokens, heads, dim, rank):
    out_ref, log_ref = refs[-2:]
    tiles = tiles_of(refs[:-2])
    lanes = lane_ids(tokens, dim)
    for b in range(samples):
        rows = slice(b * tokens, (b + 1) * tokens)
        out, logs = code_attention(
            query_ref, tiles, b, samples=samples, tokens=tokens, heads=heads, dim=dim, rank=rank
        )
        kept = jnp.zeros((tokens, dim), f32)
        for h in range(heads):
            kept = jnp.where(lanes == h, logs[h], kept)
        out_ref[rows, :] = out
        log_ref[rows, :] = kept


def partner_kernel(
    query_ref, part_ref, part_log_ref, *refs, order, late, samples, tokens, heads, dim, rank
):
    out_ref, half_ref = refs[-2:]
    tiles = tiles_of(refs[:-2])
    parts = []
    for place in order:
        ref, i = tiles[place]
        rows = slice(tokens, tokens + SUM_ROWS)
        pieces = [ref[i, rows, p * dim : (p + 1) * dim].astype(f32) for p in range(3)]
        parts.append(pieces[0] + (pieces[1] + pieces[2]))
    pieces = [piece.astype(f32) for piece in pieces_of(tree_sum(parts), 2)]
    half_ref[...] = pieces[0] + pieces[1]
    empty = jnp.zeros((tokens - SUM_ROWS, dim), f32)
    turned = [jnp.concatenate([piece, empty], axis=0).T for piece in pieces]
    lanes = lane_ids(tokens, dim)
    for b in range(samples):
        rows = slice(b * tokens, (b + 1) * tokens)
        out, logs = code_attention(
            query_ref, tiles[-late:], b,
            samples=samples, tokens=tokens, heads=heads, dim=dim, rank=rank,
        )
        before, before_logs = part_ref[rows, :], part_log_ref[rows, :]
        scale = jnp.zeros((tokens, dim), f32)
        for h in range(heads):
            before_log = before_logs[:, h : h + 1]
            top = jnp.maximum(logs[h], before_log)
            new, old = jnp.exp2(logs[h] - top), jnp.exp2(before_log - top)
            whole = new + old
            scale = jnp.where(within(lanes, value_lane(b, h, rank, heads), rank), new / whole, scale)
            logs[h] = top + jnp.log(whole) * log2_e
        out = before + (out - before) * scale
        for h in range(heads):
            for p, piece in enumerate(pieces_of(logs[h], 3)):
                out = jnp.where(lanes == log_lane(b, h, p, rank), piece.astype(f32), out)
        at = sum_lane(b, rank)
        out = jnp.where(within(lanes, at, 2 * samples * heads), pltpu.roll(turned[b], at, 1), out)
        out_ref[rows, :] = out.astype(bf16)


def own_kernel(
    query_ref, near_ref, stat_ref, old_ref, basis_h, basis_l, *refs,
    samples, tokens, heads, dim, rank,
):
    merged_ref, log_ref = refs[-2:]
    tiles = tiles_of(refs[:-2])
    lanes = lane_ids(tokens, dim)
    for b in range(samples):
        rows = slice(b * tokens, (b + 1) * tokens)
        out, logs = code_attention(
            query_ref, tiles, b, samples=samples, tokens=tokens, heads=heads, dim=dim, rank=rank
        )
        far = dot3(split(out), (basis_h[b], basis_l[b]))
        stats = stat_ref[rows, :]
        kept = jnp.zeros((tokens, dim), f32)
        for h in range(heads):
            columns = slice(h * dim, (h + 1) * dim)
            near_log = stats[:, h : h + 1]
            center = stats[:, heads + h : heads + h + 1]
            far_log = logs[h] + center
            top = jnp.maximum(near_log, far_log)
            near_part, far_part = jnp.exp2(near_log - top), jnp.exp2(far_log - top)
            whole = near_part + far_part
            merged = near_ref[rows, columns] * (near_part / whole)
            row = (b * heads + h) * 2 + 1
            merged = merged + (far[:, columns] + old_ref[row : row + 1, :]) * (far_part / whole)
            merged_ref[rows, columns] = merged
            log = top + jnp.log(whole) * log2_e - center
            kept = jnp.where(lanes == log_lane(b, h, 0, rank), log, kept)
        log_ref[rows, :] = kept


def finish_kernel(
    back_ref, half_ref, merged_ref, log_ref, old_ref, basis_h, basis_l, w_ref,
    mixed_hbm, new_hbm, attended_ref, mixed_ref, new_ref, sem, new_sem,
    *, samples, tokens, heads, dim, rank, length,
):
    chunks, columns = mixed_ref.shape[1], mixed_ref.shape[3]
    copies = []
    sums = jnp.zeros((tokens, dim), f32)
    for b in range(samples):
        rows = slice(b * tokens, (b + 1) * tokens)
        codes = back_ref[rows, :]
        extra = codes.astype(f32)
        sums = sums + pltpu.roll(extra, dim - sum_lane(b, rank), 1)
        far_log = extra + (pltpu.roll(extra, dim - 8, 1) + pltpu.roll(extra, dim - 16, 1))
        share = 1.0 / (1.0 + jnp.exp2(log_ref[rows, :] - far_log))
        far = dot(codes, basis_h[b]) + dot(codes, basis_l[b])
        for h in range(heads):
            head = slice(h * dim, (h + 1) * dim)
            at = log_lane(b, h, 0, rank)
            row = (b * heads + h) * 2 + 1
            near = merged_ref[rows, head]
            value = far[:, head] + old_ref[row : row + 1, :] - near
            attended_ref[rows, head] = (near + value * share[:, at : at + 1]).astype(bf16)
        for c in range(chunks):
            place = slice(c * columns, (c + 1) * columns)
            mixed_ref[b, c] = dot(attended_ref[rows, :], w_ref[:, place]).astype(bf16)
            copy = pltpu.make_async_copy(
                mixed_ref.at[b, c], mixed_hbm.at[rows, place], sem.at[b, c]
            )
            copy.start()
            copies.append(copy)
    fresh = (half_ref[...] + sums.T[:SUM_ROWS, :]) * (1.0 / length)
    fresh = jnp.where(old_ref[SUM_ROWS:, :] > 0.5, old_ref[:SUM_ROWS, :], fresh)
    for b in range(samples):
        for h in range(heads):
            row = (b * heads + h) * 2
            new_ref[b, h] = fresh[row : row + 2, :]
    copies.append(pltpu.make_async_copy(new_ref, new_hbm, new_sem.at[0]))
    copies[-1].start()
    for copy in copies:
        copy.wait()


VMEM = pl.BlockSpec(memory_space=pltpu.VMEM)
HBM = pl.BlockSpec(memory_space=pltpu.HBM)


def per_device(
    images, w_qkv, b_qkv, q_gain, k_gain, key_basis, value_basis, centers, refresh, w_out
):
    samples, tokens, model = images.shape
    heads, dim, rank = key_basis.shape
    seq = lax.axis_size("seq")
    rows = samples * tokens
    width = heads * dim
    sizes = dict(samples=samples, tokens=tokens, heads=heads, dim=dim)
    log_factor = log2_e / math.sqrt(dim)
    flat = images.reshape(rows, model)
    key_rows = key_basis.transpose(0, 2, 1)
    value_rows = value_basis.transpose(0, 2, 1)
    center_rows = centers.transpose(0, 2, 1, 3)
    cuts = tuple(model * i // 3 for i in range(4))
    shard = (1, tokens + SUM_ROWS, width)
    params = lambda mib: pltpu.CompilerParams(vmem_limit_bytes=mib * 2**20)

    payload, query, qkv = pl.pallas_call(
        functools.partial(project_kernel, **sizes, rank=rank, log_factor=log_factor, cuts=cuts),
        in_specs=[HBM] * 8,
        out_specs=[VMEM] * 3,
        out_shape=[
            jax.ShapeDtypeStruct(shard, bf16),
            jax.ShapeDtypeStruct((tokens, width), bf16),
            jax.ShapeDtypeStruct((rows, 3 * width), f32),
        ],
        scratch_shapes=[
            pltpu.VMEM((rows, model), bf16),
            pltpu.VMEM((model, 3 * width), bf16),
            pltpu.VMEM((3 * heads, dim), f32),
            pltpu.VMEM((1, dim), f32),
            pltpu.VMEM((1, dim), f32),
            pltpu.VMEM((heads, rank, dim), f32),
            pltpu.VMEM((heads, rank, dim), f32),
            pltpu.VMEM((samples, heads, 2, dim), f32),
            pltpu.VMEM((rows, 3 * width), f32),
            pltpu.VMEM((2 * dim, width + dim), bf16),
            pltpu.VMEM((dim, width - dim), bf16),
            pltpu.VMEM((SUM_ROWS, dim), f32),
            pltpu.SemaphoreType.DMA((2, len(cuts) - 1)),
            pltpu.SemaphoreType.DMA((6,)),
        ],
        compiler_params=params(32),
        name="project",
    )(
        *(
            pltpu.with_memory_space_constraint(x, pltpu.HBM)
            for x in (
                flat, w_qkv, b_qkv.reshape(3 * heads, dim), q_gain.reshape(1, -1),
                k_gain.reshape(1, -1), key_rows, value_rows, center_rows,
            )
        )
    )

    def swap(x, mask):
        return lax.ppermute(x, "seq", [(i, i ^ mask) for i in range(seq)])

    far_mask = seq // 2
    bits = [m for m in (2**i for i in range(1, seq.bit_length() - 1)) if m < far_mask]
    held = [(payload, [0])]
    direct = sum(bits[:2])
    for mask in range(2, 2 * direct, 2):
        if mask & ~direct == 0:
            held.append((swap(payload, mask), [mask]))
    for bit in bits[2:]:
        block = jnp.concatenate([a for a, _ in held], axis=0)
        names = [m for _, ms in held for m in ms]
        held.append((swap(block, bit), [m ^ bit for m in names]))

    query_far = swap(query, far_mask)

    near, stats, basis_high, basis_low, old = pl.pallas_call(
        functools.partial(near_kernel, **sizes, rank=rank),
        in_specs=[VMEM, VMEM, pl.BlockSpec(memory_space=pltpu.SMEM), VMEM],
        out_specs=[VMEM] * 5,
        out_shape=[
            jax.ShapeDtypeStruct((rows, width), f32),
            jax.ShapeDtypeStruct((rows, dim), f32),
            jax.ShapeDtypeStruct((samples, dim, width), bf16),
            jax.ShapeDtypeStruct((samples, dim, width), bf16),
            jax.ShapeDtypeStruct((2 * SUM_ROWS, dim), f32),
        ],
        compiler_params=params(24),
        cost_estimate=pl.CostEstimate(
            flops=1200 * rows * tokens * width, bytes_accessed=50 * rows * width * 4, transcendentals=0
        ),
        name="near",
    )(qkv, center_rows, refresh, value_rows)

    for i in range(1, len(held)):
        x, _ = lax.optimization_barrier((held[i][0], stats))
        held[i] = (x, held[i][1])
    held.insert(1, (swap(payload, 1), [1]))
    early = [a for a, _ in held]
    held += [(swap(a, 1), [m ^ 1 for m in ms]) for a, ms in held[2:]]
    arrays = [a for a, _ in held]
    names = [m for _, ms in held for m in ms]
    order = tuple(names.index(m) for m in range(len(names)))
    count_early = sum(a.shape[0] for a in early)

    def cost(shards):
        return pl.CostEstimate(
            flops=8 * rows * tokens * shards * width,
            bytes_accessed=shards * 2 * tokens * width,
            transcendentals=0,
        )

    part, part_log = pl.pallas_call(
        functools.partial(early_kernel, **sizes, rank=rank),
        in_specs=[VMEM] * (1 + len(early)),
        out_specs=[VMEM] * 2,
        out_shape=[jax.ShapeDtypeStruct((rows, dim), f32)] * 2,
        compiler_params=params(32),
        cost_estimate=cost(count_early),
        name="early",
    )(query_far, *early)
    back, half = pl.pallas_call(
        functools.partial(
            partner_kernel, **sizes, rank=rank, order=order, late=len(names) - count_early
        ),
        in_specs=[VMEM] * (3 + len(arrays)),
        out_specs=[VMEM] * 2,
        out_shape=[
            jax.ShapeDtypeStruct((rows, dim), bf16),
            jax.ShapeDtypeStruct((SUM_ROWS, dim), f32),
        ],
        compiler_params=params(32),
        cost_estimate=cost(len(names)),
        name="partner",
    )(query_far, part, part_log, *arrays)
    returned = swap(back, far_mask)
    merged, logs = pl.pallas_call(
        functools.partial(own_kernel, **sizes, rank=rank),
        in_specs=[VMEM] * (5 + len(arrays)),
        out_specs=[VMEM] * 2,
        out_shape=[
            jax.ShapeDtypeStruct((rows, width), f32),
            jax.ShapeDtypeStruct((rows, dim), f32),
        ],
        compiler_params=params(32),
        cost_estimate=cost(len(names)),
        name="own",
    )(query, near, stats, old, basis_high, basis_low, *arrays[1:])

    columns = 768
    mixed, new_centers = pl.pallas_call(
        functools.partial(finish_kernel, **sizes, rank=rank, length=tokens * seq),
        in_specs=[VMEM] * 8,
        out_specs=[HBM, HBM],
        out_shape=[
            jax.ShapeDtypeStruct((rows, model), bf16),
            jax.ShapeDtypeStruct((samples, heads, 2, dim), f32),
        ],
        scratch_shapes=[
            pltpu.VMEM((rows, width), bf16),
            pltpu.VMEM((samples, model // columns, tokens, columns), bf16),
            pltpu.VMEM((samples, heads, 2, dim), f32),
            pltpu.SemaphoreType.DMA((samples, model // columns)),
            pltpu.SemaphoreType.DMA((1,)),
        ],
        compiler_params=params(24),
        name="finish",
    )(returned, half, merged, logs, old, basis_high, basis_low, w_out)
    return (mixed.reshape(samples, tokens, model), new_centers.transpose(0, 2, 1, 3))


def solution(mesh):
    return jax.shard_map(
        per_device,
        mesh=mesh,
        in_specs=(
            P("groups", "seq", None),
            P(),
            P(),
            P(),
            P(),
            P(),
            P(),
            P("groups", None, None, None),
            P(),
            P(),
        ),
        out_specs=(P("groups", "seq", None), P("groups", None, None, None)),
        check_vma=False,
    )
```

```python
import functools
import math

import jax
import jax.numpy as jnp
from jax import lax
from jax.experimental import pallas as pl
from jax.experimental.pallas import tpu as pltpu
from jax.sharding import PartitionSpec as P

epsilon = 1e-06
log2_e = math.log2(math.e)
f32 = jnp.float32
bf16 = jnp.bfloat16
SUM_ROWS = 16
NT = (((1,), (1,)), ((), ()))
NN = (((1,), (0,)), ((), ()))


def dot(a, b, dims=NN):
    return lax.dot_general(a, b, dims, preferred_element_type=f32)


def split(x):
    high = x.astype(bf16)
    low = (x - high.astype(f32)).astype(bf16)
    return high, low


def dot3(a, b, dims=NN):
    return dot(a[0], b[0], dims) + (dot(a[0], b[1], dims) + dot(a[1], b[0], dims))


def pieces_of(x, count):
    out = []
    for _ in range(count):
        top = x.astype(bf16)
        out.append(top)
        x = x - top.astype(f32)
    return out


def lane_ids(rows, lanes):
    return lax.broadcasted_iota(jnp.int32, (rows, lanes), 1)


def key_lane(sample, head, rank):
    return head * rank if sample == 0 else (head + 1) * rank


def value_lane(sample, head, rank, heads):
    if head == 0:
        return heads * rank if sample == 0 else 0
    return ((heads - 1) * sample + head - 1) * rank


def free_lane(sample, rank):
    return 2 * rank if sample == 0 else rank


def log_lane(sample, head, piece, rank):
    return free_lane(sample, rank) + 8 * piece + head


def sum_lane(sample, rank):
    return free_lane(sample, rank) + 20


def within(lanes, start, count):
    return (lanes >= start) & (lanes < start + count)


def fill_basis(basis_h, basis_l, vb_ref, samples, heads, dim, rank):
    basis_h[...] = jnp.zeros_like(basis_h)
    basis_l[...] = jnp.zeros_like(basis_l)
    for h in range(heads):
        vh, vl = split(vb_ref[h])
        for b in range(samples):
            at = value_lane(b, h, rank, heads)
            basis_h[b, at : at + rank, h * dim : (h + 1) * dim] = vh
            basis_l[b, at : at + rank, h * dim : (h + 1) * dim] = vl


def project_kernel(
    images_hbm, w_hbm, b_hbm, qg_hbm, kg_hbm, kb_hbm, vb_hbm, centers_hbm,
    payload_ref, query_ref, qkv_ref,
    x_ref, w_ref, b_ref, qg_ref, kg_ref, kb_ref, vb_ref, centers_ref,
    acc_ref, main_ref, tail_ref, sums_ref, big_sem, small_sem,
    *, samples, tokens, heads, dim, rank, log_factor, cuts,
):
    width = heads * dim
    places = [slice(first, last) for first, last in zip(cuts[:-1], cuts[1:])]

    def x_copy(c):
        p = places[c]
        return pltpu.make_async_copy(images_hbm.at[:, p], x_ref.at[:, p], big_sem.at[0, c])

    def w_copy(c):
        p = places[c]
        return pltpu.make_async_copy(w_hbm.at[p, :], w_ref.at[p, :], big_sem.at[1, c])

    small = [
        pltpu.make_async_copy(source, target, small_sem.at[i])
        for i, (source, target) in enumerate(
            [
                (kb_hbm, kb_ref), (vb_hbm, vb_ref), (b_hbm, b_ref),
                (qg_hbm, qg_ref), (kg_hbm, kg_ref), (centers_hbm, centers_ref),
            ]
        )
    ]
    for copy in small:
        copy.start()
    for c in range(len(places)):
        x_copy(c).start()
        w_copy(c).start()
    main_ref[...] = jnp.zeros_like(main_ref)
    tail_ref[...] = jnp.zeros_like(tail_ref)
    sums_ref[...] = jnp.zeros_like(sums_ref)
    half = dim // 2

    def build():
        for copy in small:
            copy.wait()
        for h in range(heads):
            for p, (k, v) in enumerate(zip(split(kb_ref[h]), split(vb_ref[h]))):
                at = p * dim + key_lane(0, h, rank)
                main_ref[at : at + rank, h * dim : (h + 1) * dim] = k
                at = value_lane(0, h, rank, heads)
                if h == 0:
                    main_ref[p * dim + at : p * dim + at + rank, width:] = v
                else:
                    at = p * half + at
                    tail_ref[at : at + rank, (h - 1) * dim : h * dim] = v

    for c, place in enumerate(places):
        if c == len(places) - 1:
            build()
        x_copy(c).wait()
        w_copy(c).wait()
        part = dot(x_ref[:, place], w_ref[place, :])
        if c == 0:
            acc_ref[...] = part
        else:
            acc_ref[...] += part

    def column(at):
        return acc_ref[:, at * dim : (at + 1) * dim] + b_ref[at : at + 1, :]

    def normed(at, gain):
        x = column(at)
        mean_square = jnp.mean(x * x, axis=-1, keepdims=True)
        return x * lax.rsqrt(mean_square + epsilon) * gain

    queries, keys, values = [], [], []
    for h in range(heads):
        q = normed(h, qg_ref[...])
        k = normed(heads + h, kg_ref[...])
        v = column(2 * heads + h)
        queries.append(q)
        keys.append(k)
        values.append(v)
        for b in range(samples):
            rows = slice(b * tokens, (b + 1) * tokens)
            row = (b * heads + h) * 2
            sums_ref[row : row + 1, :] = jnp.sum(k[rows], axis=0, keepdims=True)
            sums_ref[row + 1 : row + 2, :] = jnp.sum(v[rows], axis=0, keepdims=True)
    for p, piece in enumerate(pieces_of(sums_ref[...], 3)):
        payload_ref[0, tokens : tokens + SUM_ROWS, p * dim : (p + 1) * dim] = piece
    def by_sample(j):
        rows = [centers_ref[b, h, j : j + 1, :] for b in range(samples) for h in range(heads)]
        return [
            jnp.concatenate(
                [jnp.broadcast_to(rows[b * heads + h], (tokens, dim)) for b in range(samples)], axis=0
            )
            for h in range(heads)
        ]

    key_centers, value_centers = by_sample(0), by_sample(1)
    shifted = [keys[h] - key_centers[h] for h in range(heads)]
    shifted += [values[h] - value_centers[h] for h in range(heads)]

    def coded(x, columns):
        high, low = split(x)
        both = dot(high, main_ref[:, columns], NT)
        return both[:, :dim] + (both[:, dim:] + dot(low, main_ref[:dim, columns], NT))

    code = coded(jnp.concatenate(shifted[: heads + 1], axis=1), slice(0, width + dim))
    query_code = coded(jnp.concatenate(queries, axis=1), slice(0, width)) * log_factor
    high, low = split(jnp.concatenate(shifted[heads + 1 :], axis=1))
    both = dot(high, tail_ref[...], NT)
    tail = both + pltpu.roll(both, half, 1) + dot(low, tail_ref[...], NT)
    payload_ref[0, :tokens, :dim] = code[:tokens].astype(bf16)
    payload_ref[0, :tokens, dim : 2 * dim] = pltpu.roll(code[tokens:], rank, 1).astype(bf16)
    lanes = lane_ids(tokens, dim)
    last = jnp.where(lanes < half, tail[:tokens], pltpu.roll(tail[tokens:], half, 1))
    payload_ref[0, :tokens, samples * dim :] = last.astype(bf16)
    high_0 = query_code[:tokens].astype(bf16).astype(f32)
    low_0 = query_code[:tokens] - high_0
    query_1 = pltpu.roll(query_code[tokens:], rank, 1)
    high_1 = query_1.astype(bf16).astype(f32)
    low_1 = query_1 - high_1
    turned = pltpu.roll(low_1, half, 1)
    query_ref[:, :dim] = jnp.where(lanes < heads * rank, high_0, turned).astype(bf16)
    query_ref[:, dim : 2 * dim] = jnp.where(lanes < rank, turned, high_1).astype(bf16)
    query_ref[:, 2 * dim :] = jnp.where(lanes < heads * rank, low_0, low_1).astype(bf16)
    for h in range(heads):
        qkv_ref[:, h * dim : (h + 1) * dim] = queries[h] * log_factor
        qkv_ref[:, width + h * dim : width + (h + 1) * dim] = keys[h]
        qkv_ref[:, 2 * width + h * dim : 2 * width + (h + 1) * dim] = values[h]


def near_kernel(
    qkv_ref, centers_ref, refresh_ref, vb_ref, near_ref, rel_ref, basis_h, basis_l, old_ref,
    *, samples, tokens, heads, dim, rank,
):
    width = heads * dim
    fill_basis(basis_h, basis_l, vb_ref, samples, heads, dim, rank)
    old_ref[...] = jnp.zeros_like(old_ref)
    for b in range(samples):
        for h in range(heads):
            for j in range(2):
                row = (b * heads + h) * 2 + j
                keep = jnp.where(refresh_ref[j, h] == 1, 0.0, 1.0)
                old_ref[row : row + 1, :] = centers_ref[b, h, j : j + 1, :]
                old_ref[SUM_ROWS + row : SUM_ROWS + row + 1, :] = jnp.full((1, dim), keep, f32)
    for b in range(samples):
        rows = slice(b * tokens, (b + 1) * tokens)
        for h in range(heads):
            head = slice(h * dim, (h + 1) * dim)
            q = qkv_ref[rows, head]
            k = split(qkv_ref[rows, width + h * dim : width + (h + 1) * dim])
            v = split(qkv_ref[rows, 2 * width + h * dim : 2 * width + (h + 1) * dim])
            scores = dot3(split(q), k, NT)
            row_max = jnp.max(scores, axis=-1, keepdims=True)
            weights = jnp.exp2(scores - row_max)
            row_sum = jnp.sum(weights, axis=-1, keepdims=True)
            near_ref[rows, head] = dot3(split(weights), v) / row_sum
            center = jnp.sum(q * centers_ref[b, h, 0:1, :], axis=-1, keepdims=True)
            rel = row_max + jnp.log(row_sum) * log2_e - center
            rel_ref[rows, head] = jnp.broadcast_to(rel, (tokens, dim))


def query_parts(query_ref, sample, heads, dim, rank):
    lanes = lane_ids(query_ref.shape[0], dim)
    if sample == 0:
        return query_ref[:, :dim].astype(f32), query_ref[:, 2 * dim :].astype(f32)
    first, second = query_ref[:, :dim].astype(f32), query_ref[:, dim : 2 * dim].astype(f32)
    turned = pltpu.roll(jnp.where(lanes < rank, second, first), dim // 2, 1)
    return second, jnp.where(lanes < heads * rank, turned, query_ref[:, 2 * dim :].astype(f32))


def code_attention(query_ref, tiles, *, samples, tokens, heads, dim, rank):
    lanes = lane_ids(tokens, dim)
    scores, values = [], []
    for b in range(samples):
        high, low = query_parts(query_ref, b, heads, dim, rank)
        stacked = []
        for h in range(heads):
            own = within(lanes, key_lane(b, h, rank), rank)
            both = [jnp.where(own, part, 0.0).astype(bf16) for part in (high, low)]
            stacked.append(jnp.concatenate(both, axis=1))
        left = jnp.concatenate(stacked, axis=0)
        codes = [ref[i, :tokens, b * dim : (b + 1) * dim] for ref, i in tiles]
        values.append(jnp.concatenate(codes, axis=0))
        parts = []
        for i in range(0, len(codes), 2):
            some = jnp.concatenate(codes[i : i + 2], axis=0)
            both = dot(left, jnp.concatenate([some, some], axis=1), NT)
            parts += [both[:, j * tokens : (j + 1) * tokens] for j in range(len(codes[i : i + 2]))]
        scores.append(parts)
    rest = jnp.concatenate([ref[i, :tokens, samples * dim :] for ref, i in tiles], axis=0)
    weights, scales, logs = [], [], []
    for b in range(samples):
        best = scores[b][0]
        for part in scores[b][1:]:
            best = jnp.maximum(best, part)
        row_max = jnp.max(best, axis=-1, keepdims=True)
        total = jnp.zeros_like(best)
        parts = []
        for part in scores[b]:
            weight = jnp.exp2(part - row_max).astype(bf16)
            total = total + weight.astype(f32)
            parts.append(weight)
        row_sum = jnp.sum(total, axis=-1, keepdims=True)
        weights.append(jnp.concatenate(parts, axis=1))
        scales.append(1.0 / row_sum)
        log = row_max + jnp.log(row_sum) * log2_e
        logs.append([log[h * tokens : (h + 1) * tokens] for h in range(heads)])
    outs = []
    for b in range(samples):
        results = [dot(weights[b][:tokens], values[b])]
        others = dot(weights[b][tokens:], rest)
        results += [others[h * tokens : (h + 1) * tokens] for h in range(heads - 1)]
        out = jnp.zeros((tokens, dim), f32)
        for h in range(heads):
            part = results[h] * scales[b][h * tokens : (h + 1) * tokens]
            out = jnp.where(within(lanes, value_lane(b, h, rank, heads), rank), part, out)
        outs.append(out)
    return outs, logs


def spread(b, logs, tokens, heads, dim, rank):
    lanes = lane_ids(tokens, dim)
    out = jnp.zeros((tokens, dim), f32)
    for h in range(heads):
        place = within(lanes, value_lane(b, h, rank, heads), rank)
        for p in range(3):
            place = place | (lanes == log_lane(b, h, p, rank))
        out = jnp.where(place, logs[h], out)
    return out


def tree_sum(parts):
    while len(parts) > 1:
        parts = [parts[i] + parts[i + 1] for i in range(0, len(parts), 2)]
    return parts[0]


def tiles_of(refs):
    return [(ref, i) for ref in refs for i in range(ref.shape[0])]


def early_kernel(query_ref, *refs, samples, tokens, heads, dim, rank):
    out_ref, log_ref = refs[-2:]
    tiles = tiles_of(refs[:-2])
    lanes = lane_ids(tokens, dim)
    outs, all_logs = code_attention(
        query_ref, tiles, samples=samples, tokens=tokens, heads=heads, dim=dim, rank=rank
    )
    for b in range(samples):
        rows = slice(b * tokens, (b + 1) * tokens)
        out, logs = outs[b], all_logs[b]
        out_ref[rows, :] = out
        log_ref[rows, :] = spread(b, logs, tokens, heads, dim, rank)


def partner_kernel(
    query_ref, part_ref, part_log_ref, *refs, order, late, samples, tokens, heads, dim, rank
):
    out_ref, half_ref = refs[-2:]
    tiles = tiles_of(refs[:-2])
    parts = []
    for place in order:
        ref, i = tiles[place]
        rows = slice(tokens, tokens + SUM_ROWS)
        pieces = [ref[i, rows, p * dim : (p + 1) * dim].astype(f32) for p in range(3)]
        parts.append(pieces[0] + (pieces[1] + pieces[2]))
    pieces = [piece.astype(f32) for piece in pieces_of(tree_sum(parts), 2)]
    half_ref[...] = pieces[0] + pieces[1]
    empty = jnp.zeros((tokens - SUM_ROWS, dim), f32)
    turned = [jnp.concatenate([piece, empty], axis=0).T for piece in pieces]
    lanes = lane_ids(tokens, dim)
    outs, all_logs = code_attention(
        query_ref, tiles[-late:], samples=samples, tokens=tokens, heads=heads, dim=dim, rank=rank
    )
    for b in range(samples):
        rows = slice(b * tokens, (b + 1) * tokens)
        out, logs = outs[b], all_logs[b]
        before, before_log = part_ref[rows, :], part_log_ref[rows, :]
        log = spread(b, logs, tokens, heads, dim, rank)
        top = jnp.maximum(log, before_log)
        new = jnp.exp2(log - top)
        whole = new + jnp.exp2(before_log - top)
        out = before + (out - before) * (new / whole)
        log = top + jnp.log(whole) * log2_e
        for p, piece in enumerate(pieces_of(log, 3)):
            place = within(lanes, log_lane(b, 0, p, rank), heads)
            out = jnp.where(place, piece.astype(f32), out)
        at = sum_lane(b, rank)
        out = jnp.where(within(lanes, at, 2 * samples * heads), pltpu.roll(turned[b], at, 1), out)
        out_ref[rows, :] = out.astype(bf16)


def own_kernel(
    query_ref, near_ref, rel_ref, old_ref, basis_h, basis_l, *refs,
    samples, tokens, heads, dim, rank,
):
    merged_ref, log_ref = refs[-2:]
    tiles = tiles_of(refs[:-2])
    lanes = lane_ids(tokens, dim)
    outs, all_logs = code_attention(
        query_ref, tiles, samples=samples, tokens=tokens, heads=heads, dim=dim, rank=rank
    )
    for b in range(samples):
        rows = slice(b * tokens, (b + 1) * tokens)
        out, logs = outs[b], all_logs[b]
        far = dot3(split(out), (basis_h[b], basis_l[b]))
        kept = jnp.zeros((tokens, dim), f32)
        for h in range(heads):
            columns = slice(h * dim, (h + 1) * dim)
            near, rel = near_ref[rows, columns], rel_ref[rows, columns]
            top = jnp.maximum(rel, logs[h])
            far_part = jnp.exp2(logs[h] - top)
            whole = jnp.exp2(rel - top) + far_part
            row = (b * heads + h) * 2 + 1
            value = far[:, columns] + old_ref[row : row + 1, :] - near
            merged_ref[rows, columns] = near + value * (far_part / whole)
            log = top + jnp.log(whole) * log2_e
            kept = jnp.where(lanes == log_lane(b, h, 0, rank), log, kept)
        log_ref[rows, :] = kept


def finish_kernel(
    back_ref, half_ref, merged_ref, log_ref, old_ref, basis_h, basis_l, w_ref,
    mixed_hbm, new_hbm, attended_ref, mixed_ref, new_ref, sem, new_sem,
    *, samples, tokens, heads, dim, rank, length,
):
    chunks, columns = mixed_ref.shape[1], mixed_ref.shape[3]
    copies = []
    sums = jnp.zeros((tokens, dim), f32)
    for b in range(samples):
        rows = slice(b * tokens, (b + 1) * tokens)
        codes = back_ref[rows, :]
        extra = codes.astype(f32)
        sums = sums + pltpu.roll(extra, dim - sum_lane(b, rank), 1)
        far_log = extra + (pltpu.roll(extra, dim - 8, 1) + pltpu.roll(extra, dim - 16, 1))
        share = 1.0 / (1.0 + jnp.exp2(log_ref[rows, :] - far_log))
        far = dot(codes, basis_h[b]) + dot(codes, basis_l[b])
        for h in range(heads):
            head = slice(h * dim, (h + 1) * dim)
            at = log_lane(b, h, 0, rank)
            row = (b * heads + h) * 2 + 1
            near = merged_ref[rows, head]
            value = far[:, head] + old_ref[row : row + 1, :] - near
            attended_ref[rows, head] = (near + value * share[:, at : at + 1]).astype(bf16)
        for c in range(chunks):
            place = slice(c * columns, (c + 1) * columns)
            mixed_ref[b, c] = dot(attended_ref[rows, :], w_ref[:, place]).astype(bf16)
            copy = pltpu.make_async_copy(
                mixed_ref.at[b, c], mixed_hbm.at[rows, place], sem.at[b, c]
            )
            copy.start()
            copies.append(copy)
    fresh = (half_ref[...] + sums.T[:SUM_ROWS, :]) * (1.0 / length)
    fresh = jnp.where(old_ref[SUM_ROWS:, :] > 0.5, old_ref[:SUM_ROWS, :], fresh)
    for b in range(samples):
        for h in range(heads):
            row = (b * heads + h) * 2
            new_ref[b, h] = fresh[row : row + 2, :]
    copies.append(pltpu.make_async_copy(new_ref, new_hbm, new_sem.at[0]))
    copies[-1].start()
    for copy in copies:
        copy.wait()


VMEM = pl.BlockSpec(memory_space=pltpu.VMEM)
HBM = pl.BlockSpec(memory_space=pltpu.HBM)


def per_device(
    images, w_qkv, b_qkv, q_gain, k_gain, key_basis, value_basis, centers, refresh, w_out
):
    samples, tokens, model = images.shape
    heads, dim, rank = key_basis.shape
    seq = lax.axis_size("seq")
    rows = samples * tokens
    width = heads * dim
    sizes = dict(samples=samples, tokens=tokens, heads=heads, dim=dim)
    log_factor = log2_e / math.sqrt(dim)
    flat = images.reshape(rows, model)
    key_rows = key_basis.transpose(0, 2, 1)
    value_rows = value_basis.transpose(0, 2, 1)
    center_rows = centers.transpose(0, 2, 1, 3)
    cuts = tuple(model * i // 3 for i in range(4))
    shard = (1, tokens + SUM_ROWS, width)
    params = lambda mib: pltpu.CompilerParams(vmem_limit_bytes=mib * 2**20)

    payload, query, qkv = pl.pallas_call(
        functools.partial(project_kernel, **sizes, rank=rank, log_factor=log_factor, cuts=cuts),
        in_specs=[HBM] * 8,
        out_specs=[VMEM] * 3,
        out_shape=[
            jax.ShapeDtypeStruct(shard, bf16),
            jax.ShapeDtypeStruct((tokens, width), bf16),
            jax.ShapeDtypeStruct((rows, 3 * width), f32),
        ],
        scratch_shapes=[
            pltpu.VMEM((rows, model), bf16),
            pltpu.VMEM((model, 3 * width), bf16),
            pltpu.VMEM((3 * heads, dim), f32),
            pltpu.VMEM((1, dim), f32),
            pltpu.VMEM((1, dim), f32),
            pltpu.VMEM((heads, rank, dim), f32),
            pltpu.VMEM((heads, rank, dim), f32),
            pltpu.VMEM((samples, heads, 2, dim), f32),
            pltpu.VMEM((rows, 3 * width), f32),
            pltpu.VMEM((2 * dim, width + dim), bf16),
            pltpu.VMEM((dim, width - dim), bf16),
            pltpu.VMEM((SUM_ROWS, dim), f32),
            pltpu.SemaphoreType.DMA((2, len(cuts) - 1)),
            pltpu.SemaphoreType.DMA((6,)),
        ],
        compiler_params=params(32),
        name="project",
    )(
        *(
            pltpu.with_memory_space_constraint(x, pltpu.HBM)
            for x in (
                flat, w_qkv, b_qkv.reshape(3 * heads, dim), q_gain.reshape(1, -1),
                k_gain.reshape(1, -1), key_rows, value_rows, center_rows,
            )
        )
    )

    def swap(x, mask):
        return lax.ppermute(x, "seq", [(i, i ^ mask) for i in range(seq)])

    far_mask = seq // 2
    bits = [m for m in (2**i for i in range(1, seq.bit_length() - 1)) if m < far_mask]
    held = [(payload, [0])]
    direct = sum(bits[:2])
    for mask in range(2, 2 * direct, 2):
        if mask & ~direct == 0:
            held.append((swap(payload, mask), [mask]))
    for bit in bits[2:]:
        block = jnp.concatenate([a for a, _ in held], axis=0)
        names = [m for _, ms in held for m in ms]
        held.append((swap(block, bit), [m ^ bit for m in names]))

    query_far = swap(query, far_mask)

    near, rel, basis_high, basis_low, old = pl.pallas_call(
        functools.partial(near_kernel, **sizes, rank=rank),
        in_specs=[VMEM, VMEM, pl.BlockSpec(memory_space=pltpu.SMEM), VMEM],
        out_specs=[VMEM] * 5,
        out_shape=[
            jax.ShapeDtypeStruct((rows, width), f32),
            jax.ShapeDtypeStruct((rows, width), f32),
            jax.ShapeDtypeStruct((samples, dim, width), bf16),
            jax.ShapeDtypeStruct((samples, dim, width), bf16),
            jax.ShapeDtypeStruct((2 * SUM_ROWS, dim), f32),
        ],
        compiler_params=params(24),
        cost_estimate=pl.CostEstimate(
            flops=1200 * rows * tokens * width, bytes_accessed=50 * rows * width * 4, transcendentals=0
        ),
        name="near",
    )(qkv, center_rows, refresh, value_rows)

    for i in range(1, len(held)):
        x, _ = lax.optimization_barrier((held[i][0], rel))
        held[i] = (x, held[i][1])
    held.insert(1, (swap(payload, 1), [1]))
    early = [a for a, _ in held]
    held += [(swap(a, 1), [m ^ 1 for m in ms]) for a, ms in held[2:]]
    arrays = [a for a, _ in held]
    names = [m for _, ms in held for m in ms]
    order = tuple(names.index(m) for m in range(len(names)))
    count_early = sum(a.shape[0] for a in early)

    def cost(shards):
        return pl.CostEstimate(
            flops=8 * rows * tokens * shards * width,
            bytes_accessed=shards * 2 * tokens * width,
            transcendentals=0,
        )

    part, part_log = pl.pallas_call(
        functools.partial(early_kernel, **sizes, rank=rank),
        in_specs=[VMEM] * (1 + len(early)),
        out_specs=[VMEM] * 2,
        out_shape=[jax.ShapeDtypeStruct((rows, dim), f32)] * 2,
        compiler_params=params(32),
        cost_estimate=cost(count_early),
        name="early",
    )(query_far, *early)
    back, half = pl.pallas_call(
        functools.partial(
            partner_kernel, **sizes, rank=rank, order=order, late=len(names) - count_early
        ),
        in_specs=[VMEM] * (3 + len(arrays)),
        out_specs=[VMEM] * 2,
        out_shape=[
            jax.ShapeDtypeStruct((rows, dim), bf16),
            jax.ShapeDtypeStruct((SUM_ROWS, dim), f32),
        ],
        compiler_params=params(32),
        cost_estimate=cost(len(names)),
        name="partner",
    )(query_far, part, part_log, *arrays)
    returned = swap(back, far_mask)
    merged, logs = pl.pallas_call(
        functools.partial(own_kernel, **sizes, rank=rank),
        in_specs=[VMEM] * (5 + len(arrays)),
        out_specs=[VMEM] * 2,
        out_shape=[
            jax.ShapeDtypeStruct((rows, width), f32),
            jax.ShapeDtypeStruct((rows, dim), f32),
        ],
        compiler_params=params(32),
        cost_estimate=cost(len(names)),
        name="own",
    )(query, near, rel, old, basis_high, basis_low, *arrays[1:])

    columns = 768
    mixed, new_centers = pl.pallas_call(
        functools.partial(finish_kernel, **sizes, rank=rank, length=tokens * seq),
        in_specs=[VMEM] * 8,
        out_specs=[HBM, HBM],
        out_shape=[
            jax.ShapeDtypeStruct((rows, model), bf16),
            jax.ShapeDtypeStruct((samples, heads, 2, dim), f32),
        ],
        scratch_shapes=[
            pltpu.VMEM((rows, width), bf16),
            pltpu.VMEM((samples, model // columns, tokens, columns), bf16),
            pltpu.VMEM((samples, heads, 2, dim), f32),
            pltpu.SemaphoreType.DMA((samples, model // columns)),
            pltpu.SemaphoreType.DMA((1,)),
        ],
        compiler_params=params(24),
        name="finish",
    )(returned, half, merged, logs, old, basis_high, basis_low, w_out)
    return (mixed.reshape(samples, tokens, model), new_centers.transpose(0, 2, 1, 3))


def solution(mesh):
    return jax.shard_map(
        per_device,
        mesh=mesh,
        in_specs=(
            P("groups", "seq", None),
            P(),
            P(),
            P(),
            P(),
            P(),
            P(),
            P("groups", None, None, None),
            P(),
            P(),
        ),
        out_specs=(P("groups", "seq", None), P("groups", None, None, None)),
        check_vma=False,
    )
```

```python
import functools
import math

import jax
import jax.numpy as jnp
from jax import lax
from jax.experimental import pallas as pl
from jax.experimental.pallas import tpu as pltpu
from jax.sharding import PartitionSpec as P

epsilon = 1e-06
log2_e = math.log2(math.e)
f32 = jnp.float32
bf16 = jnp.bfloat16
SUM_ROWS = 16
NT = (((1,), (1,)), ((), ()))
NN = (((1,), (0,)), ((), ()))


def dot(a, b, dims=NN):
    return lax.dot_general(a, b, dims, preferred_element_type=f32)


def split(x):
    high = x.astype(bf16)
    low = (x - high.astype(f32)).astype(bf16)
    return high, low


def dot3(a, b, dims=NN):
    return dot(a[0], b[0], dims) + (dot(a[0], b[1], dims) + dot(a[1], b[0], dims))


def pieces_of(x, count):
    out = []
    for _ in range(count):
        top = x.astype(bf16)
        out.append(top)
        x = x - top.astype(f32)
    return out


def lane_ids(rows, lanes):
    return lax.broadcasted_iota(jnp.int32, (rows, lanes), 1)


def key_lane(sample, head, rank):
    return head * rank if sample == 0 else (head + 1) * rank


def value_lane(sample, head, rank, heads):
    if head == 0:
        return heads * rank if sample == 0 else 0
    return ((heads - 1) * sample + head - 1) * rank


def free_lane(sample, rank):
    return 2 * rank if sample == 0 else rank


def log_lane(sample, head, piece, rank):
    return free_lane(sample, rank) + 8 * piece + head


def sum_lane(sample, rank):
    return free_lane(sample, rank) + 20


def within(lanes, start, count):
    return (lanes >= start) & (lanes < start + count)


def fill_basis(basis_h, basis_l, vb_ref, samples, heads, dim, rank):
    basis_h[...] = jnp.zeros_like(basis_h)
    basis_l[...] = jnp.zeros_like(basis_l)
    for h in range(heads):
        vh, vl = split(vb_ref[h])
        for b in range(samples):
            at = value_lane(b, h, rank, heads)
            basis_h[b, at : at + rank, h * dim : (h + 1) * dim] = vh
            basis_l[b, at : at + rank, h * dim : (h + 1) * dim] = vl


def project_kernel(
    images_hbm, w_hbm, b_hbm, qg_hbm, kg_hbm, kb_hbm, vb_hbm, centers_hbm,
    payload_ref, query_ref, qkv_ref,
    x_ref, w_ref, b_ref, qg_ref, kg_ref, kb_ref, vb_ref, centers_ref,
    acc_ref, main_ref, tail_ref, sums_ref, big_sem, small_sem,
    *, samples, tokens, heads, dim, rank, log_factor, cuts,
):
    width = heads * dim
    places = [slice(first, last) for first, last in zip(cuts[:-1], cuts[1:])]

    def x_copy(c):
        p = places[c]
        return pltpu.make_async_copy(images_hbm.at[:, p], x_ref.at[:, p], big_sem.at[0, c])

    def w_copy(c):
        p = places[c]
        return pltpu.make_async_copy(w_hbm.at[p, :], w_ref.at[p, :], big_sem.at[1, c])

    small = [
        pltpu.make_async_copy(source, target, small_sem.at[i])
        for i, (source, target) in enumerate(
            [
                (kb_hbm, kb_ref), (vb_hbm, vb_ref), (b_hbm, b_ref),
                (qg_hbm, qg_ref), (kg_hbm, kg_ref), (centers_hbm, centers_ref),
            ]
        )
    ]
    for copy in small:
        copy.start()
    for c in range(len(places)):
        x_copy(c).start()
        w_copy(c).start()
    main_ref[...] = jnp.zeros_like(main_ref)
    tail_ref[...] = jnp.zeros_like(tail_ref)
    sums_ref[...] = jnp.zeros_like(sums_ref)
    half = dim // 2

    def build():
        for copy in small:
            copy.wait()
        for h in range(heads):
            for p, (k, v) in enumerate(zip(split(kb_ref[h]), split(vb_ref[h]))):
                at = p * dim + key_lane(0, h, rank)
                main_ref[at : at + rank, h * dim : (h + 1) * dim] = k
                at = value_lane(0, h, rank, heads)
                if h == 0:
                    main_ref[p * dim + at : p * dim + at + rank, width:] = v
                else:
                    at = p * half + at
                    tail_ref[at : at + rank, (h - 1) * dim : h * dim] = v

    for c, place in enumerate(places):
        if c == len(places) - 1:
            build()
        x_copy(c).wait()
        w_copy(c).wait()
        part = dot(x_ref[:, place], w_ref[place, :])
        if c == 0:
            acc_ref[...] = part
        else:
            acc_ref[...] += part

    def column(at):
        return acc_ref[:, at * dim : (at + 1) * dim] + b_ref[at : at + 1, :]

    def normed(at, gain):
        x = column(at)
        mean_square = jnp.mean(x * x, axis=-1, keepdims=True)
        return x * lax.rsqrt(mean_square + epsilon) * gain

    queries, keys, values = [], [], []
    for h in range(heads):
        q = normed(h, qg_ref[...])
        k = normed(heads + h, kg_ref[...])
        v = column(2 * heads + h)
        queries.append(q)
        keys.append(k)
        values.append(v)
        for b in range(samples):
            rows = slice(b * tokens, (b + 1) * tokens)
            row = (b * heads + h) * 2
            sums_ref[row : row + 1, :] = jnp.sum(k[rows], axis=0, keepdims=True)
            sums_ref[row + 1 : row + 2, :] = jnp.sum(v[rows], axis=0, keepdims=True)
    for p, piece in enumerate(pieces_of(sums_ref[...], 3)):
        payload_ref[0, tokens : tokens + SUM_ROWS, p * dim : (p + 1) * dim] = piece
    def by_sample(j):
        rows = [centers_ref[b, h, j : j + 1, :] for b in range(samples) for h in range(heads)]
        return [
            jnp.concatenate(
                [jnp.broadcast_to(rows[b * heads + h], (tokens, dim)) for b in range(samples)], axis=0
            )
            for h in range(heads)
        ]

    key_centers, value_centers = by_sample(0), by_sample(1)
    shifted = [keys[h] - key_centers[h] for h in range(heads)]
    shifted += [values[h] - value_centers[h] for h in range(heads)]

    def coded(x, columns):
        high, low = split(x)
        both = dot(high, main_ref[:, columns], NT)
        return both[:, :dim] + (both[:, dim:] + dot(low, main_ref[:dim, columns], NT))

    code = coded(jnp.concatenate(shifted[: heads + 1], axis=1), slice(0, width + dim))
    query_code = coded(jnp.concatenate(queries, axis=1), slice(0, width)) * log_factor
    high, low = split(jnp.concatenate(shifted[heads + 1 :], axis=1))
    both = dot(high, tail_ref[...], NT)
    tail = both + pltpu.roll(both, half, 1) + dot(low, tail_ref[...], NT)
    payload_ref[0, :tokens, :dim] = code[:tokens].astype(bf16)
    payload_ref[0, :tokens, dim : 2 * dim] = pltpu.roll(code[tokens:], rank, 1).astype(bf16)
    lanes = lane_ids(tokens, dim)
    last = jnp.where(lanes < half, tail[:tokens], pltpu.roll(tail[tokens:], half, 1))
    payload_ref[0, :tokens, samples * dim :] = last.astype(bf16)
    high_0 = query_code[:tokens].astype(bf16).astype(f32)
    low_0 = query_code[:tokens] - high_0
    query_1 = pltpu.roll(query_code[tokens:], rank, 1)
    high_1 = query_1.astype(bf16).astype(f32)
    low_1 = query_1 - high_1
    turned = pltpu.roll(low_1, half, 1)
    query_ref[:, :dim] = jnp.where(lanes < heads * rank, high_0, turned).astype(bf16)
    query_ref[:, dim : 2 * dim] = jnp.where(lanes < rank, turned, high_1).astype(bf16)
    query_ref[:, 2 * dim :] = jnp.where(lanes < heads * rank, low_0, low_1).astype(bf16)
    for h in range(heads):
        qkv_ref[:, h * dim : (h + 1) * dim] = queries[h] * log_factor
        qkv_ref[:, width + h * dim : width + (h + 1) * dim] = keys[h]
        qkv_ref[:, 2 * width + h * dim : 2 * width + (h + 1) * dim] = values[h]


def near_kernel(
    qkv_ref, centers_ref, refresh_ref, vb_ref, near_ref, rel_ref, basis_h, basis_l, old_ref,
    *, samples, tokens, heads, dim, rank,
):
    width = heads * dim
    fill_basis(basis_h, basis_l, vb_ref, samples, heads, dim, rank)
    old_ref[...] = jnp.zeros_like(old_ref)
    for b in range(samples):
        for h in range(heads):
            for j in range(2):
                row = (b * heads + h) * 2 + j
                keep = jnp.where(refresh_ref[j, h] == 1, 0.0, 1.0)
                old_ref[row : row + 1, :] = centers_ref[b, h, j : j + 1, :]
                old_ref[SUM_ROWS + row : SUM_ROWS + row + 1, :] = jnp.full((1, dim), keep, f32)
    for b in range(samples):
        rows = slice(b * tokens, (b + 1) * tokens)
        for h in range(heads):
            head = slice(h * dim, (h + 1) * dim)
            q = qkv_ref[rows, head]
            k = split(qkv_ref[rows, width + h * dim : width + (h + 1) * dim])
            v = split(qkv_ref[rows, 2 * width + h * dim : 2 * width + (h + 1) * dim])
            scores = dot3(split(q), k, NT)
            row_max = jnp.max(scores, axis=-1, keepdims=True)
            weights = jnp.exp2(scores - row_max)
            row_sum = jnp.sum(weights, axis=-1, keepdims=True)
            near_ref[rows, head] = dot3(split(weights), v) / row_sum
            center = jnp.sum(q * centers_ref[b, h, 0:1, :], axis=-1, keepdims=True)
            rel = row_max + jnp.log(row_sum) * log2_e - center
            rel_ref[rows, head] = jnp.broadcast_to(rel, (tokens, dim))


def query_parts(query_ref, sample, heads, dim, rank):
    lanes = lane_ids(query_ref.shape[0], dim)
    if sample == 0:
        return query_ref[:, :dim].astype(f32), query_ref[:, 2 * dim :].astype(f32)
    first, second = query_ref[:, :dim].astype(f32), query_ref[:, dim : 2 * dim].astype(f32)
    turned = pltpu.roll(jnp.where(lanes < rank, second, first), dim // 2, 1)
    return second, jnp.where(lanes < heads * rank, turned, query_ref[:, 2 * dim :].astype(f32))


def code_attention(query_ref, tiles, *, samples, tokens, heads, dim, rank):
    lanes = lane_ids(tokens, dim)
    scores, values = [], []
    for b in range(samples):
        high, low = query_parts(query_ref, b, heads, dim, rank)
        stacked = []
        for h in range(heads):
            own = within(lanes, key_lane(b, h, rank), rank)
            both = [jnp.where(own, part, 0.0).astype(bf16) for part in (high, low)]
            stacked.append(jnp.concatenate(both, axis=1))
        left = jnp.concatenate(stacked, axis=0)
        codes = [ref[i, :tokens, b * dim : (b + 1) * dim] for ref, i in tiles]
        values.append(jnp.concatenate(codes, axis=0))
        parts = []
        for i in range(0, len(codes), 2):
            some = jnp.concatenate(codes[i : i + 2], axis=0)
            both = dot(left, jnp.concatenate([some, some], axis=1), NT)
            parts += [both[:, j * tokens : (j + 1) * tokens] for j in range(len(codes[i : i + 2]))]
        scores.append(parts)
    rest = jnp.concatenate([ref[i, :tokens, samples * dim :] for ref, i in tiles], axis=0)
    weights, scales, logs = [], [], []
    for b in range(samples):
        best = scores[b][0]
        for part in scores[b][1:]:
            best = jnp.maximum(best, part)
        row_max = jnp.max(best, axis=-1, keepdims=True)
        total = jnp.zeros_like(best)
        parts = []
        for part in scores[b]:
            weight = jnp.exp2(part - row_max).astype(bf16)
            total = total + weight.astype(f32)
            parts.append(weight)
        row_sum = jnp.sum(total, axis=-1, keepdims=True)
        weights.append(jnp.concatenate(parts, axis=1))
        scales.append(1.0 / row_sum)
        log = row_max + jnp.log(row_sum) * log2_e
        logs.append([log[h * tokens : (h + 1) * tokens] for h in range(heads)])
    outs = []
    for b in range(samples):
        results = [dot(weights[b][:tokens], values[b])]
        others = dot(weights[b][tokens:], rest)
        results += [others[h * tokens : (h + 1) * tokens] for h in range(heads - 1)]
        out = jnp.zeros((tokens, dim), f32)
        for h in range(heads):
            part = results[h] * scales[b][h * tokens : (h + 1) * tokens]
            out = jnp.where(within(lanes, value_lane(b, h, rank, heads), rank), part, out)
        outs.append(out)
    return outs, logs


def spread(b, logs, tokens, heads, dim, rank):
    lanes = lane_ids(tokens, dim)
    out = jnp.zeros((tokens, dim), f32)
    for h in range(heads):
        place = within(lanes, value_lane(b, h, rank, heads), rank)
        for p in range(3):
            place = place | (lanes == log_lane(b, h, p, rank))
        out = jnp.where(place, logs[h], out)
    return out


def tree_sum(parts):
    while len(parts) > 1:
        parts = [parts[i] + parts[i + 1] for i in range(0, len(parts), 2)]
    return parts[0]


def tiles_of(refs):
    return [(ref, i) for ref in refs for i in range(ref.shape[0])]


def early_kernel(query_ref, *refs, samples, tokens, heads, dim, rank):
    out_ref, log_ref = refs[-2:]
    tiles = tiles_of(refs[:-2])
    lanes = lane_ids(tokens, dim)
    outs, all_logs = code_attention(
        query_ref, tiles, samples=samples, tokens=tokens, heads=heads, dim=dim, rank=rank
    )
    for b in range(samples):
        rows = slice(b * tokens, (b + 1) * tokens)
        out, logs = outs[b], all_logs[b]
        out_ref[rows, :] = out
        log_ref[rows, :] = spread(b, logs, tokens, heads, dim, rank)


def partner_kernel(
    query_ref, part_ref, part_log_ref, *refs, order, late, samples, tokens, heads, dim, rank
):
    out_ref, half_ref = refs[-2:]
    tiles = tiles_of(refs[:-2])
    parts = []
    for place in order:
        ref, i = tiles[place]
        rows = slice(tokens, tokens + SUM_ROWS)
        pieces = [ref[i, rows, p * dim : (p + 1) * dim].astype(f32) for p in range(3)]
        parts.append(pieces[0] + (pieces[1] + pieces[2]))
    pieces = [piece.astype(f32) for piece in pieces_of(tree_sum(parts), 2)]
    half_ref[...] = pieces[0] + pieces[1]
    empty = jnp.zeros((tokens - SUM_ROWS, dim), f32)
    turned = [jnp.concatenate([piece, empty], axis=0).T for piece in pieces]
    lanes = lane_ids(tokens, dim)
    outs, all_logs = code_attention(
        query_ref, tiles[-late:], samples=samples, tokens=tokens, heads=heads, dim=dim, rank=rank
    )
    for b in range(samples):
        rows = slice(b * tokens, (b + 1) * tokens)
        out, logs = outs[b], all_logs[b]
        before, before_log = part_ref[rows, :], part_log_ref[rows, :]
        log = spread(b, logs, tokens, heads, dim, rank)
        top = jnp.maximum(log, before_log)
        new = jnp.exp2(log - top)
        whole = new + jnp.exp2(before_log - top)
        out = before + (out - before) * (new / whole)
        log = top + jnp.log(whole) * log2_e
        for p, piece in enumerate(pieces_of(log, 3)):
            place = within(lanes, log_lane(b, 0, p, rank), heads)
            out = jnp.where(place, piece.astype(f32), out)
        at = sum_lane(b, rank)
        out = jnp.where(within(lanes, at, 2 * samples * heads), pltpu.roll(turned[b], at, 1), out)
        out_ref[rows, :] = out.astype(bf16)


def own_kernel(
    query_ref, near_ref, rel_ref, old_ref, basis_h, basis_l, *refs,
    samples, tokens, heads, dim, rank,
):
    merged_ref, log_ref = refs[-2:]
    tiles = tiles_of(refs[:-2])
    lanes = lane_ids(tokens, dim)
    outs, all_logs = code_attention(
        query_ref, tiles, samples=samples, tokens=tokens, heads=heads, dim=dim, rank=rank
    )
    for b in range(samples):
        rows = slice(b * tokens, (b + 1) * tokens)
        out, logs = outs[b], all_logs[b]
        far = dot3(split(out), (basis_h[b], basis_l[b]))
        kept = jnp.zeros((tokens, dim), f32)
        for h in range(heads):
            columns = slice(h * dim, (h + 1) * dim)
            near, rel = near_ref[rows, columns], rel_ref[rows, columns]
            top = jnp.maximum(rel, logs[h])
            far_part = jnp.exp2(logs[h] - top)
            whole = jnp.exp2(rel - top) + far_part
            row = (b * heads + h) * 2 + 1
            value = far[:, columns] + old_ref[row : row + 1, :] - near
            merged_ref[rows, columns] = near + value * (far_part / whole)
            log = top + jnp.log(whole) * log2_e
            kept = jnp.where(lanes == log_lane(b, h, 0, rank), log, kept)
        log_ref[rows, :] = kept


def finish_kernel(
    back_ref, half_ref, merged_ref, log_ref, old_ref, basis_h, basis_l, w_ref,
    mixed_hbm, new_hbm, attended_ref, mixed_ref, new_ref, sem, new_sem,
    *, samples, tokens, heads, dim, rank, length,
):
    chunks, columns = mixed_ref.shape[1], mixed_ref.shape[3]
    copies = []
    sums = jnp.zeros((tokens, dim), f32)
    for b in range(samples):
        rows = slice(b * tokens, (b + 1) * tokens)
        codes = back_ref[rows, :]
        extra = codes.astype(f32)
        sums = sums + pltpu.roll(extra, dim - sum_lane(b, rank), 1)
        far_log = extra + (pltpu.roll(extra, dim - 8, 1) + pltpu.roll(extra, dim - 16, 1))
        share = 1.0 / (1.0 + jnp.exp2(log_ref[rows, :] - far_log))
        far = dot(codes, basis_h[b]) + dot(codes, basis_l[b])
        for h in range(heads):
            head = slice(h * dim, (h + 1) * dim)
            at = log_lane(b, h, 0, rank)
            row = (b * heads + h) * 2 + 1
            near = merged_ref[rows, head]
            value = far[:, head] + old_ref[row : row + 1, :] - near
            attended_ref[rows, head] = (near + value * share[:, at : at + 1]).astype(bf16)
        for c in range(chunks):
            place = slice(c * columns, (c + 1) * columns)
            mixed_ref[b, c] = dot(attended_ref[rows, :], w_ref[:, place]).astype(bf16)
            copy = pltpu.make_async_copy(
                mixed_ref.at[b, c], mixed_hbm.at[rows, place], sem.at[b, c]
            )
            copy.start()
            copies.append(copy)
    fresh = (half_ref[...] + sums.T[:SUM_ROWS, :]) * (1.0 / length)
    fresh = jnp.where(old_ref[SUM_ROWS:, :] > 0.5, old_ref[:SUM_ROWS, :], fresh)
    for b in range(samples):
        for h in range(heads):
            row = (b * heads + h) * 2
            new_ref[b, h] = fresh[row : row + 2, :]
    copies.append(pltpu.make_async_copy(new_ref, new_hbm, new_sem.at[0]))
    copies[-1].start()
    for copy in copies:
        copy.wait()


VMEM = pl.BlockSpec(memory_space=pltpu.VMEM)
HBM = pl.BlockSpec(memory_space=pltpu.HBM)


def per_device(
    images, w_qkv, b_qkv, q_gain, k_gain, key_basis, value_basis, centers, refresh, w_out
):
    samples, tokens, model = images.shape
    heads, dim, rank = key_basis.shape
    seq = lax.axis_size("seq")
    rows = samples * tokens
    width = heads * dim
    sizes = dict(samples=samples, tokens=tokens, heads=heads, dim=dim)
    log_factor = log2_e / math.sqrt(dim)
    flat = images.reshape(rows, model)
    key_rows = key_basis.transpose(0, 2, 1)
    value_rows = value_basis.transpose(0, 2, 1)
    center_rows = centers.transpose(0, 2, 1, 3)
    cuts = tuple(model * i // 3 for i in range(4))
    shard = (1, tokens + SUM_ROWS, width)
    params = lambda mib: pltpu.CompilerParams(vmem_limit_bytes=mib * 2**20)

    payload, query, qkv = pl.pallas_call(
        functools.partial(project_kernel, **sizes, rank=rank, log_factor=log_factor, cuts=cuts),
        in_specs=[HBM] * 8,
        out_specs=[VMEM] * 3,
        out_shape=[
            jax.ShapeDtypeStruct(shard, bf16),
            jax.ShapeDtypeStruct((tokens, width), bf16),
            jax.ShapeDtypeStruct((rows, 3 * width), f32),
        ],
        scratch_shapes=[
            pltpu.VMEM((rows, model), bf16),
            pltpu.VMEM((model, 3 * width), bf16),
            pltpu.VMEM((3 * heads, dim), f32),
            pltpu.VMEM((1, dim), f32),
            pltpu.VMEM((1, dim), f32),
            pltpu.VMEM((heads, rank, dim), f32),
            pltpu.VMEM((heads, rank, dim), f32),
            pltpu.VMEM((samples, heads, 2, dim), f32),
            pltpu.VMEM((rows, 3 * width), f32),
            pltpu.VMEM((2 * dim, width + dim), bf16),
            pltpu.VMEM((dim, width - dim), bf16),
            pltpu.VMEM((SUM_ROWS, dim), f32),
            pltpu.SemaphoreType.DMA((2, len(cuts) - 1)),
            pltpu.SemaphoreType.DMA((6,)),
        ],
        compiler_params=params(32),
        name="project",
    )(
        *(
            pltpu.with_memory_space_constraint(x, pltpu.HBM)
            for x in (
                flat, w_qkv, b_qkv.reshape(3 * heads, dim), q_gain.reshape(1, -1),
                k_gain.reshape(1, -1), key_rows, value_rows, center_rows,
            )
        )
    )

    def swap(x, mask):
        return lax.ppermute(x, "seq", [(i, i ^ mask) for i in range(seq)])

    far_mask = seq // 2
    bits = [m for m in (2**i for i in range(1, seq.bit_length() - 1)) if m < far_mask]
    held = [(payload, [0])]
    direct = sum(bits[:2])
    for mask in range(2, 2 * direct, 2):
        if mask & ~direct == 0:
            held.append((swap(payload, mask), [mask]))
    for bit in bits[2:]:
        block = jnp.concatenate([a for a, _ in held], axis=0)
        names = [m for _, ms in held for m in ms]
        held.append((swap(block, bit), [m ^ bit for m in names]))

    query_far = swap(query, far_mask)

    near, rel, basis_high, basis_low, old = pl.pallas_call(
        functools.partial(near_kernel, **sizes, rank=rank),
        in_specs=[VMEM, VMEM, pl.BlockSpec(memory_space=pltpu.SMEM), VMEM],
        out_specs=[VMEM] * 5,
        out_shape=[
            jax.ShapeDtypeStruct((rows, width), f32),
            jax.ShapeDtypeStruct((rows, width), f32),
            jax.ShapeDtypeStruct((samples, dim, width), bf16),
            jax.ShapeDtypeStruct((samples, dim, width), bf16),
            jax.ShapeDtypeStruct((2 * SUM_ROWS, dim), f32),
        ],
        compiler_params=params(24),
        cost_estimate=pl.CostEstimate(
            flops=1200 * rows * tokens * width, bytes_accessed=50 * rows * width * 4, transcendentals=0
        ),
        name="near",
    )(qkv, center_rows, refresh, value_rows)

    for i in (1,):
        x, _ = lax.optimization_barrier((held[i][0], rel))
        held[i] = (x, held[i][1])
    held.insert(1, (swap(payload, 1), [1]))
    early = [a for a, _ in held]
    held += [(swap(a, 1), [m ^ 1 for m in ms]) for a, ms in held[2:]]
    arrays = [a for a, _ in held]
    names = [m for _, ms in held for m in ms]
    order = tuple(names.index(m) for m in range(len(names)))
    count_early = sum(a.shape[0] for a in early)

    def cost(shards):
        return pl.CostEstimate(
            flops=8 * rows * tokens * shards * width,
            bytes_accessed=shards * 2 * tokens * width,
            transcendentals=0,
        )

    part, part_log = pl.pallas_call(
        functools.partial(early_kernel, **sizes, rank=rank),
        in_specs=[VMEM] * (1 + len(early)),
        out_specs=[VMEM] * 2,
        out_shape=[jax.ShapeDtypeStruct((rows, dim), f32)] * 2,
        compiler_params=params(32),
        cost_estimate=cost(count_early),
        name="early",
    )(query_far, *early)
    back, half = pl.pallas_call(
        functools.partial(
            partner_kernel, **sizes, rank=rank, order=order, late=len(names) - count_early
        ),
        in_specs=[VMEM] * (3 + len(arrays)),
        out_specs=[VMEM] * 2,
        out_shape=[
            jax.ShapeDtypeStruct((rows, dim), bf16),
            jax.ShapeDtypeStruct((SUM_ROWS, dim), f32),
        ],
        compiler_params=params(32),
        cost_estimate=cost(len(names)),
        name="partner",
    )(query_far, part, part_log, *arrays)
    returned = swap(back, far_mask)
    merged, logs = pl.pallas_call(
        functools.partial(own_kernel, **sizes, rank=rank),
        in_specs=[VMEM] * (5 + len(arrays)),
        out_specs=[VMEM] * 2,
        out_shape=[
            jax.ShapeDtypeStruct((rows, width), f32),
            jax.ShapeDtypeStruct((rows, dim), f32),
        ],
        compiler_params=params(32),
        cost_estimate=cost(len(names)),
        name="own",
    )(query, near, rel, old, basis_high, basis_low, *arrays[1:])

    columns = 768
    mixed, new_centers = pl.pallas_call(
        functools.partial(finish_kernel, **sizes, rank=rank, length=tokens * seq),
        in_specs=[VMEM] * 8,
        out_specs=[HBM, HBM],
        out_shape=[
            jax.ShapeDtypeStruct((rows, model), bf16),
            jax.ShapeDtypeStruct((samples, heads, 2, dim), f32),
        ],
        scratch_shapes=[
            pltpu.VMEM((rows, width), bf16),
            pltpu.VMEM((samples, model // columns, tokens, columns), bf16),
            pltpu.VMEM((samples, heads, 2, dim), f32),
            pltpu.SemaphoreType.DMA((samples, model // columns)),
            pltpu.SemaphoreType.DMA((1,)),
        ],
        compiler_params=params(24),
        name="finish",
    )(returned, half, merged, logs, old, basis_high, basis_low, w_out)
    return (mixed.reshape(samples, tokens, model), new_centers.transpose(0, 2, 1, 3))


def solution(mesh):
    return jax.shard_map(
        per_device,
        mesh=mesh,
        in_specs=(
            P("groups", "seq", None),
            P(),
            P(),
            P(),
            P(),
            P(),
            P(),
            P("groups", None, None, None),
            P(),
            P(),
        ),
        out_specs=(P("groups", "seq", None), P("groups", None, None, None)),
        check_vma=False,
    )
```

```python
import functools
import math

import jax
import jax.numpy as jnp
from jax import lax
from jax.experimental import pallas as pl
from jax.experimental.pallas import tpu as pltpu
from jax.sharding import PartitionSpec as P

epsilon = 1e-06
log2_e = math.log2(math.e)
f32 = jnp.float32
bf16 = jnp.bfloat16
SUM_ROWS = 16
NT = (((1,), (1,)), ((), ()))
NN = (((1,), (0,)), ((), ()))


def dot(a, b, dims=NN):
    return lax.dot_general(a, b, dims, preferred_element_type=f32)


def split(x):
    high = x.astype(bf16)
    low = (x - high.astype(f32)).astype(bf16)
    return high, low


def dot3(a, b, dims=NN):
    return dot(a[0], b[0], dims) + (dot(a[0], b[1], dims) + dot(a[1], b[0], dims))


def pieces_of(x, count):
    out = []
    for _ in range(count):
        top = x.astype(bf16)
        out.append(top)
        x = x - top.astype(f32)
    return out


def lane_ids(rows, lanes):
    return lax.broadcasted_iota(jnp.int32, (rows, lanes), 1)


def key_lane(sample, head, rank):
    return head * rank if sample == 0 else (head + 1) * rank


def value_lane(sample, head, rank, heads):
    if head == 0:
        return heads * rank if sample == 0 else 0
    return ((heads - 1) * sample + head - 1) * rank


def free_lane(sample, rank):
    return 2 * rank if sample == 0 else rank


def log_lane(sample, head, piece, rank):
    return free_lane(sample, rank) + 8 * piece + head


def sum_lane(sample, rank):
    return free_lane(sample, rank) + 20


def within(lanes, start, count):
    return (lanes >= start) & (lanes < start + count)


def fill_basis(basis_h, basis_l, vb_ref, samples, heads, dim, rank):
    basis_h[...] = jnp.zeros_like(basis_h)
    basis_l[...] = jnp.zeros_like(basis_l)
    for h in range(heads):
        vh, vl = split(vb_ref[h])
        for b in range(samples):
            at = value_lane(b, h, rank, heads)
            basis_h[b, at : at + rank, h * dim : (h + 1) * dim] = vh
            basis_l[b, at : at + rank, h * dim : (h + 1) * dim] = vl


def project_kernel(
    images_hbm, w_hbm, b_hbm, qg_hbm, kg_hbm, kb_hbm, vb_hbm, centers_hbm,
    payload_ref, query_ref, qkv_ref,
    x_ref, w_ref, b_ref, qg_ref, kg_ref, kb_ref, vb_ref, centers_ref,
    acc_ref, main_ref, tail_ref, sums_ref, big_sem, small_sem,
    *, samples, tokens, heads, dim, rank, log_factor, cuts,
):
    width = heads * dim
    places = [slice(first, last) for first, last in zip(cuts[:-1], cuts[1:])]

    def x_copy(c):
        p = places[c]
        return pltpu.make_async_copy(images_hbm.at[:, p], x_ref.at[:, p], big_sem.at[0, c])

    def w_copy(c):
        p = places[c]
        return pltpu.make_async_copy(w_hbm.at[p, :], w_ref.at[p, :], big_sem.at[1, c])

    small = [
        pltpu.make_async_copy(source, target, small_sem.at[i])
        for i, (source, target) in enumerate(
            [
                (kb_hbm, kb_ref), (vb_hbm, vb_ref), (b_hbm, b_ref),
                (qg_hbm, qg_ref), (kg_hbm, kg_ref), (centers_hbm, centers_ref),
            ]
        )
    ]
    for copy in small:
        copy.start()
    for c in range(len(places)):
        x_copy(c).start()
        w_copy(c).start()
    main_ref[...] = jnp.zeros_like(main_ref)
    tail_ref[...] = jnp.zeros_like(tail_ref)
    sums_ref[...] = jnp.zeros_like(sums_ref)
    half = dim // 2

    def build():
        for copy in small:
            copy.wait()
        for h in range(heads):
            for p, (k, v) in enumerate(zip(split(kb_ref[h]), split(vb_ref[h]))):
                at = p * dim + key_lane(0, h, rank)
                main_ref[at : at + rank, h * dim : (h + 1) * dim] = k
                at = value_lane(0, h, rank, heads)
                if h == 0:
                    main_ref[p * dim + at : p * dim + at + rank, width:] = v
                else:
                    at = p * half + at
                    tail_ref[at : at + rank, (h - 1) * dim : h * dim] = v

    for c, place in enumerate(places):
        if c == len(places) - 1:
            build()
        x_copy(c).wait()
        w_copy(c).wait()
        part = dot(x_ref[:, place], w_ref[place, :])
        if c == 0:
            acc_ref[...] = part
        else:
            acc_ref[...] += part

    def column(at):
        return acc_ref[:, at * dim : (at + 1) * dim] + b_ref[at : at + 1, :]

    def normed(at, gain):
        x = column(at)
        mean_square = jnp.mean(x * x, axis=-1, keepdims=True)
        return x * lax.rsqrt(mean_square + epsilon) * gain

    queries, keys, values = [], [], []
    for h in range(heads):
        q = normed(h, qg_ref[...])
        k = normed(heads + h, kg_ref[...])
        v = column(2 * heads + h)
        queries.append(q)
        keys.append(k)
        values.append(v)
        for b in range(samples):
            rows = slice(b * tokens, (b + 1) * tokens)
            row = (b * heads + h) * 2
            sums_ref[row : row + 1, :] = jnp.sum(k[rows], axis=0, keepdims=True)
            sums_ref[row + 1 : row + 2, :] = jnp.sum(v[rows], axis=0, keepdims=True)
    for p, piece in enumerate(pieces_of(sums_ref[...], 3)):
        payload_ref[0, tokens : tokens + SUM_ROWS, p * dim : (p + 1) * dim] = piece
    def by_sample(j):
        rows = [centers_ref[b, h, j : j + 1, :] for b in range(samples) for h in range(heads)]
        return [
            jnp.concatenate(
                [jnp.broadcast_to(rows[b * heads + h], (tokens, dim)) for b in range(samples)], axis=0
            )
            for h in range(heads)
        ]

    key_centers, value_centers = by_sample(0), by_sample(1)
    shifted = [keys[h] - key_centers[h] for h in range(heads)]
    shifted += [values[h] - value_centers[h] for h in range(heads)]

    def coded(x, columns):
        high, low = split(x)
        both = dot(high, main_ref[:, columns], NT)
        return both[:, :dim] + (both[:, dim:] + dot(low, main_ref[:dim, columns], NT))

    code = coded(jnp.concatenate(shifted[: heads + 1], axis=1), slice(0, width + dim))
    query_code = coded(jnp.concatenate(queries, axis=1), slice(0, width)) * log_factor
    high, low = split(jnp.concatenate(shifted[heads + 1 :], axis=1))
    both = dot(high, tail_ref[...], NT)
    tail = both + pltpu.roll(both, half, 1) + dot(low, tail_ref[...], NT)
    payload_ref[0, :tokens, :dim] = code[:tokens].astype(bf16)
    payload_ref[0, :tokens, dim : 2 * dim] = pltpu.roll(code[tokens:], rank, 1).astype(bf16)
    lanes = lane_ids(tokens, dim)
    last = jnp.where(lanes < half, tail[:tokens], pltpu.roll(tail[tokens:], half, 1))
    payload_ref[0, :tokens, samples * dim :] = last.astype(bf16)
    high_0 = query_code[:tokens].astype(bf16).astype(f32)
    low_0 = query_code[:tokens] - high_0
    query_1 = pltpu.roll(query_code[tokens:], rank, 1)
    high_1 = query_1.astype(bf16).astype(f32)
    low_1 = query_1 - high_1
    turned = pltpu.roll(low_1, half, 1)
    query_ref[:, :dim] = jnp.where(lanes < heads * rank, high_0, turned).astype(bf16)
    query_ref[:, dim : 2 * dim] = jnp.where(lanes < rank, turned, high_1).astype(bf16)
    query_ref[:, 2 * dim :] = jnp.where(lanes < heads * rank, low_0, low_1).astype(bf16)
    for h in range(heads):
        qkv_ref[:, h * dim : (h + 1) * dim] = queries[h] * log_factor
        qkv_ref[:, width + h * dim : width + (h + 1) * dim] = keys[h]
        qkv_ref[:, 2 * width + h * dim : 2 * width + (h + 1) * dim] = values[h]


def near_kernel(
    qkv_ref, centers_ref, refresh_ref, vb_ref, near_ref, rel_ref, basis_h, basis_l, old_ref,
    *, samples, tokens, heads, dim, rank,
):
    width = heads * dim
    fill_basis(basis_h, basis_l, vb_ref, samples, heads, dim, rank)
    old_ref[...] = jnp.zeros_like(old_ref)
    for b in range(samples):
        for h in range(heads):
            for j in range(2):
                row = (b * heads + h) * 2 + j
                keep = jnp.where(refresh_ref[j, h] == 1, 0.0, 1.0)
                old_ref[row : row + 1, :] = centers_ref[b, h, j : j + 1, :]
                old_ref[SUM_ROWS + row : SUM_ROWS + row + 1, :] = jnp.full((1, dim), keep, f32)
    for b in range(samples):
        rows = slice(b * tokens, (b + 1) * tokens)
        for h in range(heads):
            head = slice(h * dim, (h + 1) * dim)
            q = qkv_ref[rows, head]
            k = split(qkv_ref[rows, width + h * dim : width + (h + 1) * dim])
            v = split(qkv_ref[rows, 2 * width + h * dim : 2 * width + (h + 1) * dim])
            scores = dot3(split(q), k, NT)
            row_max = jnp.max(scores, axis=-1, keepdims=True)
            weights = jnp.exp2(scores - row_max)
            row_sum = jnp.sum(weights, axis=-1, keepdims=True)
            near_ref[rows, head] = dot3(split(weights), v) / row_sum
            center = jnp.sum(q * centers_ref[b, h, 0:1, :], axis=-1, keepdims=True)
            rel = row_max + jnp.log(row_sum) * log2_e - center
            rel_ref[rows, head] = jnp.broadcast_to(rel, (tokens, dim))


def query_parts(query_ref, sample, heads, dim, rank):
    lanes = lane_ids(query_ref.shape[0], dim)
    if sample == 0:
        return query_ref[:, :dim].astype(f32), query_ref[:, 2 * dim :].astype(f32)
    first, second = query_ref[:, :dim].astype(f32), query_ref[:, dim : 2 * dim].astype(f32)
    turned = pltpu.roll(jnp.where(lanes < rank, second, first), dim // 2, 1)
    return second, jnp.where(lanes < heads * rank, turned, query_ref[:, 2 * dim :].astype(f32))


def code_attention(query_ref, tiles, *, samples, tokens, heads, dim, rank):
    lanes = lane_ids(tokens, dim)
    scores, values = [], []
    for b in range(samples):
        high, low = query_parts(query_ref, b, heads, dim, rank)
        stacked = []
        for h in range(heads):
            own = within(lanes, key_lane(b, h, rank), rank)
            both = [jnp.where(own, part, 0.0).astype(bf16) for part in (high, low)]
            stacked.append(jnp.concatenate(both, axis=1))
        left = jnp.concatenate(stacked, axis=0)
        codes = [ref[i, :tokens, b * dim : (b + 1) * dim] for ref, i in tiles]
        values.append(jnp.concatenate(codes, axis=0))
        parts = []
        for i in range(0, len(codes), 2):
            some = jnp.concatenate(codes[i : i + 2], axis=0)
            both = dot(left, jnp.concatenate([some, some], axis=1), NT)
            parts += [both[:, j * tokens : (j + 1) * tokens] for j in range(len(codes[i : i + 2]))]
        scores.append(parts)
    rest = jnp.concatenate([ref[i, :tokens, samples * dim :] for ref, i in tiles], axis=0)
    weights, scales, logs = [], [], []
    for b in range(samples):
        best = scores[b][0]
        for part in scores[b][1:]:
            best = jnp.maximum(best, part)
        row_max = jnp.max(best, axis=-1, keepdims=True)
        total = jnp.zeros_like(best)
        parts = []
        for part in scores[b]:
            weight = jnp.exp2(part - row_max).astype(bf16)
            total = total + weight.astype(f32)
            parts.append(weight)
        row_sum = jnp.sum(total, axis=-1, keepdims=True)
        weights.append(jnp.concatenate(parts, axis=1))
        scales.append(1.0 / row_sum)
        log = row_max + jnp.log(row_sum) * log2_e
        logs.append([log[h * tokens : (h + 1) * tokens] for h in range(heads)])
    outs = []
    for b in range(samples):
        results = [dot(weights[b][:tokens], values[b])]
        others = dot(weights[b][tokens:], rest)
        results += [others[h * tokens : (h + 1) * tokens] for h in range(heads - 1)]
        out = jnp.zeros((tokens, dim), f32)
        for h in range(heads):
            part = results[h] * scales[b][h * tokens : (h + 1) * tokens]
            out = jnp.where(within(lanes, value_lane(b, h, rank, heads), rank), part, out)
        outs.append(out)
    return outs, logs


def spread(b, logs, tokens, heads, dim, rank):
    lanes = lane_ids(tokens, dim)
    out = jnp.zeros((tokens, dim), f32)
    for h in range(heads):
        place = within(lanes, value_lane(b, h, rank, heads), rank)
        for p in range(3):
            place = place | (lanes == log_lane(b, h, p, rank))
        out = jnp.where(place, logs[h], out)
    return out


def tree_sum(parts):
    while len(parts) > 1:
        parts = [parts[i] + parts[i + 1] for i in range(0, len(parts), 2)]
    return parts[0]


def tiles_of(refs):
    return [(ref, i) for ref in refs for i in range(ref.shape[0])]


def early_kernel(query_ref, *refs, samples, tokens, heads, dim, rank):
    out_ref, log_ref = refs[-2:]
    tiles = tiles_of(refs[:-2])
    lanes = lane_ids(tokens, dim)
    outs, all_logs = code_attention(
        query_ref, tiles, samples=samples, tokens=tokens, heads=heads, dim=dim, rank=rank
    )
    for b in range(samples):
        rows = slice(b * tokens, (b + 1) * tokens)
        out, logs = outs[b], all_logs[b]
        out_ref[rows, :] = out
        log_ref[rows, :] = spread(b, logs, tokens, heads, dim, rank)


def partner_kernel(
    query_ref, part_ref, part_log_ref, *refs, order, late, samples, tokens, heads, dim, rank
):
    out_ref, half_ref = refs[-2:]
    tiles = tiles_of(refs[:-2])
    parts = []
    for place in order:
        ref, i = tiles[place]
        rows = slice(tokens, tokens + SUM_ROWS)
        pieces = [ref[i, rows, p * dim : (p + 1) * dim].astype(f32) for p in range(3)]
        parts.append(pieces[0] + (pieces[1] + pieces[2]))
    pieces = [piece.astype(f32) for piece in pieces_of(tree_sum(parts), 2)]
    half_ref[...] = pieces[0] + pieces[1]
    empty = jnp.zeros((tokens - SUM_ROWS, dim), f32)
    turned = [jnp.concatenate([piece, empty], axis=0).T for piece in pieces]
    lanes = lane_ids(tokens, dim)
    outs, all_logs = code_attention(
        query_ref, tiles[-late:], samples=samples, tokens=tokens, heads=heads, dim=dim, rank=rank
    )
    for b in range(samples):
        rows = slice(b * tokens, (b + 1) * tokens)
        out, logs = outs[b], all_logs[b]
        before, before_log = part_ref[rows, :], part_log_ref[rows, :]
        log = spread(b, logs, tokens, heads, dim, rank)
        top = jnp.maximum(log, before_log)
        new = jnp.exp2(log - top)
        whole = new + jnp.exp2(before_log - top)
        out = before + (out - before) * (new / whole)
        log = top + jnp.log(whole) * log2_e
        for p, piece in enumerate(pieces_of(log, 3)):
            place = within(lanes, log_lane(b, 0, p, rank), heads)
            out = jnp.where(place, piece.astype(f32), out)
        at = sum_lane(b, rank)
        out = jnp.where(within(lanes, at, 2 * samples * heads), pltpu.roll(turned[b], at, 1), out)
        out_ref[rows, :] = out.astype(bf16)


def own_kernel(
    query_ref, near_ref, rel_ref, old_ref, basis_h, basis_l, *refs,
    samples, tokens, heads, dim, rank,
):
    merged_ref, log_ref = refs[-2:]
    tiles = tiles_of(refs[:-2])
    lanes = lane_ids(tokens, dim)
    outs, all_logs = code_attention(
        query_ref, tiles, samples=samples, tokens=tokens, heads=heads, dim=dim, rank=rank
    )
    for b in range(samples):
        rows = slice(b * tokens, (b + 1) * tokens)
        out, logs = outs[b], all_logs[b]
        far = dot3(split(out), (basis_h[b], basis_l[b]))
        kept = jnp.zeros((tokens, dim), f32)
        for h in range(heads):
            columns = slice(h * dim, (h + 1) * dim)
            near, rel = near_ref[rows, columns], rel_ref[rows, columns]
            top = jnp.maximum(rel, logs[h])
            far_part = jnp.exp2(logs[h] - top)
            whole = jnp.exp2(rel - top) + far_part
            row = (b * heads + h) * 2 + 1
            value = far[:, columns] + old_ref[row : row + 1, :] - near
            merged_ref[rows, columns] = near + value * (far_part / whole)
            log = top + jnp.log(whole) * log2_e
            kept = jnp.where(lanes == log_lane(b, h, 0, rank), log, kept)
        log_ref[rows, :] = kept


def finish_kernel(
    back_ref, half_ref, merged_ref, log_ref, old_ref, basis_h, basis_l, w_ref,
    mixed_hbm, new_hbm, attended_ref, mixed_ref, new_ref, sem, new_sem,
    *, samples, tokens, heads, dim, rank, length,
):
    chunks, columns = mixed_ref.shape[0], mixed_ref.shape[2]
    copies = []
    sums = jnp.zeros((tokens, dim), f32)
    for b in range(samples):
        rows = slice(b * tokens, (b + 1) * tokens)
        codes = back_ref[rows, :]
        extra = codes.astype(f32)
        sums = sums + pltpu.roll(extra, dim - sum_lane(b, rank), 1)
        far_log = extra + (pltpu.roll(extra, dim - 8, 1) + pltpu.roll(extra, dim - 16, 1))
        share = 1.0 / (1.0 + jnp.exp2(log_ref[rows, :] - far_log))
        far = dot(codes, basis_h[b]) + dot(codes, basis_l[b])
        for h in range(heads):
            head = slice(h * dim, (h + 1) * dim)
            at = log_lane(b, h, 0, rank)
            row = (b * heads + h) * 2 + 1
            near = merged_ref[rows, head]
            value = far[:, head] + old_ref[row : row + 1, :] - near
            attended_ref[rows, head] = (near + value * share[:, at : at + 1]).astype(bf16)
    for c in range(chunks):
        place = slice(c * columns, (c + 1) * columns)
        mixed_ref[c] = dot(attended_ref[...], w_ref[:, place]).astype(bf16)
        copies.append(pltpu.make_async_copy(mixed_ref.at[c], mixed_hbm.at[:, place], sem.at[c]))
        copies[-1].start()
        if c == 1:
            fresh = (half_ref[...] + sums.T[:SUM_ROWS, :]) * (1.0 / length)
            fresh = jnp.where(old_ref[SUM_ROWS:, :] > 0.5, old_ref[:SUM_ROWS, :], fresh)
            for b in range(samples):
                for h in range(heads):
                    row = (b * heads + h) * 2
                    new_ref[b, h] = fresh[row : row + 2, :]
            copies.append(pltpu.make_async_copy(new_ref, new_hbm, new_sem.at[0]))
            copies[-1].start()
    for copy in copies:
        copy.wait()


VMEM = pl.BlockSpec(memory_space=pltpu.VMEM)
HBM = pl.BlockSpec(memory_space=pltpu.HBM)


def per_device(
    images, w_qkv, b_qkv, q_gain, k_gain, key_basis, value_basis, centers, refresh, w_out
):
    samples, tokens, model = images.shape
    heads, dim, rank = key_basis.shape
    seq = lax.axis_size("seq")
    rows = samples * tokens
    width = heads * dim
    sizes = dict(samples=samples, tokens=tokens, heads=heads, dim=dim)
    log_factor = log2_e / math.sqrt(dim)
    flat = images.reshape(rows, model)
    key_rows = key_basis.transpose(0, 2, 1)
    value_rows = value_basis.transpose(0, 2, 1)
    center_rows = centers.transpose(0, 2, 1, 3)
    cuts = tuple(model * i // 3 for i in range(4))
    shard = (1, tokens + SUM_ROWS, width)
    params = lambda mib: pltpu.CompilerParams(vmem_limit_bytes=mib * 2**20)

    payload, query, qkv = pl.pallas_call(
        functools.partial(project_kernel, **sizes, rank=rank, log_factor=log_factor, cuts=cuts),
        in_specs=[HBM] * 8,
        out_specs=[VMEM] * 3,
        out_shape=[
            jax.ShapeDtypeStruct(shard, bf16),
            jax.ShapeDtypeStruct((tokens, width), bf16),
            jax.ShapeDtypeStruct((rows, 3 * width), f32),
        ],
        scratch_shapes=[
            pltpu.VMEM((rows, model), bf16),
            pltpu.VMEM((model, 3 * width), bf16),
            pltpu.VMEM((3 * heads, dim), f32),
            pltpu.VMEM((1, dim), f32),
            pltpu.VMEM((1, dim), f32),
            pltpu.VMEM((heads, rank, dim), f32),
            pltpu.VMEM((heads, rank, dim), f32),
            pltpu.VMEM((samples, heads, 2, dim), f32),
            pltpu.VMEM((rows, 3 * width), f32),
            pltpu.VMEM((2 * dim, width + dim), bf16),
            pltpu.VMEM((dim, width - dim), bf16),
            pltpu.VMEM((SUM_ROWS, dim), f32),
            pltpu.SemaphoreType.DMA((2, len(cuts) - 1)),
            pltpu.SemaphoreType.DMA((6,)),
        ],
        compiler_params=params(32),
        name="project",
    )(
        *(
            pltpu.with_memory_space_constraint(x, pltpu.HBM)
            for x in (
                flat, w_qkv, b_qkv.reshape(3 * heads, dim), q_gain.reshape(1, -1),
                k_gain.reshape(1, -1), key_rows, value_rows, center_rows,
            )
        )
    )

    def swap(x, mask):
        return lax.ppermute(x, "seq", [(i, i ^ mask) for i in range(seq)])

    far_mask = seq // 2
    bits = [m for m in (2**i for i in range(1, seq.bit_length() - 1)) if m < far_mask]
    held = [(payload, [0])]
    direct = sum(bits[:2])
    for mask in range(2, 2 * direct, 2):
        if mask & ~direct == 0:
            held.append((swap(payload, mask), [mask]))
    for bit in bits[2:]:
        block = jnp.concatenate([a for a, _ in held], axis=0)
        names = [m for _, ms in held for m in ms]
        held.append((swap(block, bit), [m ^ bit for m in names]))

    query_far = swap(query, far_mask)

    near, rel, basis_high, basis_low, old = pl.pallas_call(
        functools.partial(near_kernel, **sizes, rank=rank),
        in_specs=[VMEM, VMEM, pl.BlockSpec(memory_space=pltpu.SMEM), VMEM],
        out_specs=[VMEM] * 5,
        out_shape=[
            jax.ShapeDtypeStruct((rows, width), f32),
            jax.ShapeDtypeStruct((rows, width), f32),
            jax.ShapeDtypeStruct((samples, dim, width), bf16),
            jax.ShapeDtypeStruct((samples, dim, width), bf16),
            jax.ShapeDtypeStruct((2 * SUM_ROWS, dim), f32),
        ],
        compiler_params=params(24),
        cost_estimate=pl.CostEstimate(
            flops=1200 * rows * tokens * width, bytes_accessed=50 * rows * width * 4, transcendentals=0
        ),
        name="near",
    )(qkv, center_rows, refresh, value_rows)

    for i in (1,):
        x, _ = lax.optimization_barrier((held[i][0], rel))
        held[i] = (x, held[i][1])
    held.insert(1, (swap(payload, 1), [1]))
    early = [a for a, _ in held]
    held += [(swap(a, 1), [m ^ 1 for m in ms]) for a, ms in held[2:]]
    arrays = [a for a, _ in held]
    names = [m for _, ms in held for m in ms]
    order = tuple(names.index(m) for m in range(len(names)))
    count_early = sum(a.shape[0] for a in early)

    def cost(shards):
        return pl.CostEstimate(
            flops=8 * rows * tokens * shards * width,
            bytes_accessed=shards * 2 * tokens * width,
            transcendentals=0,
        )

    part, part_log = pl.pallas_call(
        functools.partial(early_kernel, **sizes, rank=rank),
        in_specs=[VMEM] * (1 + len(early)),
        out_specs=[VMEM] * 2,
        out_shape=[jax.ShapeDtypeStruct((rows, dim), f32)] * 2,
        compiler_params=params(32),
        cost_estimate=cost(count_early),
        name="early",
    )(query_far, *early)
    back, half = pl.pallas_call(
        functools.partial(
            partner_kernel, **sizes, rank=rank, order=order, late=len(names) - count_early
        ),
        in_specs=[VMEM] * (3 + len(arrays)),
        out_specs=[VMEM] * 2,
        out_shape=[
            jax.ShapeDtypeStruct((rows, dim), bf16),
            jax.ShapeDtypeStruct((SUM_ROWS, dim), f32),
        ],
        compiler_params=params(32),
        cost_estimate=cost(len(names)),
        name="partner",
    )(query_far, part, part_log, *arrays)
    returned = swap(back, far_mask)
    merged, logs = pl.pallas_call(
        functools.partial(own_kernel, **sizes, rank=rank),
        in_specs=[VMEM] * (5 + len(arrays)),
        out_specs=[VMEM] * 2,
        out_shape=[
            jax.ShapeDtypeStruct((rows, width), f32),
            jax.ShapeDtypeStruct((rows, dim), f32),
        ],
        compiler_params=params(32),
        cost_estimate=cost(len(names)),
        name="own",
    )(query, near, rel, old, basis_high, basis_low, *arrays[1:])

    columns = 512
    mixed, new_centers = pl.pallas_call(
        functools.partial(finish_kernel, **sizes, rank=rank, length=tokens * seq),
        in_specs=[VMEM] * 8,
        out_specs=[HBM, HBM],
        out_shape=[
            jax.ShapeDtypeStruct((rows, model), bf16),
            jax.ShapeDtypeStruct((samples, heads, 2, dim), f32),
        ],
        scratch_shapes=[
            pltpu.VMEM((rows, width), bf16),
            pltpu.VMEM((model // columns, rows, columns), bf16),
            pltpu.VMEM((samples, heads, 2, dim), f32),
            pltpu.SemaphoreType.DMA((model // columns,)),
            pltpu.SemaphoreType.DMA((1,)),
        ],
        compiler_params=params(24),
        name="finish",
    )(returned, half, merged, logs, old, basis_high, basis_low, w_out)
    return (mixed.reshape(samples, tokens, model), new_centers.transpose(0, 2, 1, 3))


def solution(mesh):
    return jax.shard_map(
        per_device,
        mesh=mesh,
        in_specs=(
            P("groups", "seq", None),
            P(),
            P(),
            P(),
            P(),
            P(),
            P(),
            P("groups", None, None, None),
            P(),
            P(),
        ),
        out_specs=(P("groups", "seq", None), P("groups", None, None, None)),
        check_vma=False,
    )
```

```python
import functools
import math

import jax
import jax.numpy as jnp
from jax import lax
from jax.experimental import pallas as pl
from jax.experimental.pallas import tpu as pltpu
from jax.sharding import PartitionSpec as P

epsilon = 1e-06
log2_e = math.log2(math.e)
f32 = jnp.float32
bf16 = jnp.bfloat16
SUM_ROWS = 16
NT = (((1,), (1,)), ((), ()))
NN = (((1,), (0,)), ((), ()))


def dot(a, b, dims=NN):
    return lax.dot_general(a, b, dims, preferred_element_type=f32)


def split(x):
    high = x.astype(bf16)
    low = (x - high.astype(f32)).astype(bf16)
    return high, low


def dot3(a, b, dims=NN):
    return dot(a[0], b[0], dims) + (dot(a[0], b[1], dims) + dot(a[1], b[0], dims))


def pieces_of(x, count):
    out = []
    for _ in range(count):
        top = x.astype(bf16)
        out.append(top)
        x = x - top.astype(f32)
    return out


def lane_ids(rows, lanes):
    return lax.broadcasted_iota(jnp.int32, (rows, lanes), 1)


def key_lane(sample, head, rank):
    return head * rank if sample == 0 else (head + 1) * rank


def value_lane(sample, head, rank, heads):
    if head == 0:
        return heads * rank if sample == 0 else 0
    return ((heads - 1) * sample + head - 1) * rank


def free_lane(sample, rank):
    return 2 * rank if sample == 0 else rank


def log_lane(sample, head, piece, rank):
    return free_lane(sample, rank) + 8 * piece + head


def sum_lane(sample, rank):
    return free_lane(sample, rank) + 20


def within(lanes, start, count):
    return (lanes >= start) & (lanes < start + count)


def fill_basis(basis_h, basis_l, vb_ref, samples, heads, dim, rank):
    basis_h[...] = jnp.zeros_like(basis_h)
    basis_l[...] = jnp.zeros_like(basis_l)
    for h in range(heads):
        vh, vl = split(vb_ref[h])
        for b in range(samples):
            at = value_lane(b, h, rank, heads)
            basis_h[b, at : at + rank, h * dim : (h + 1) * dim] = vh
            basis_l[b, at : at + rank, h * dim : (h + 1) * dim] = vl


def project_kernel(
    images_hbm, w_hbm, b_hbm, qg_hbm, kg_hbm, kb_hbm, vb_hbm, centers_hbm,
    payload_ref, query_ref, qkv_ref,
    x_ref, w_ref, b_ref, qg_ref, kg_ref, kb_ref, vb_ref, centers_ref,
    acc_ref, main_ref, tail_ref, sums_ref, big_sem, small_sem,
    *, samples, tokens, heads, dim, rank, log_factor, cuts,
):
    width = heads * dim
    places = [slice(first, last) for first, last in zip(cuts[:-1], cuts[1:])]

    def x_copy(c):
        p = places[c]
        return pltpu.make_async_copy(images_hbm.at[:, p], x_ref.at[:, p], big_sem.at[0, c])

    def w_copy(c):
        p = places[c]
        return pltpu.make_async_copy(w_hbm.at[p, :], w_ref.at[p, :], big_sem.at[1, c])

    small = [
        pltpu.make_async_copy(source, target, small_sem.at[i])
        for i, (source, target) in enumerate(
            [
                (kb_hbm, kb_ref), (vb_hbm, vb_ref), (b_hbm, b_ref),
                (qg_hbm, qg_ref), (kg_hbm, kg_ref), (centers_hbm, centers_ref),
            ]
        )
    ]
    for copy in small:
        copy.start()
    for c in range(len(places)):
        w_copy(c).start()
        x_copy(c).start()
    main_ref[...] = jnp.zeros_like(main_ref)
    tail_ref[...] = jnp.zeros_like(tail_ref)
    sums_ref[...] = jnp.zeros_like(sums_ref)
    half = dim // 2

    def build():
        for copy in small:
            copy.wait()
        for h in range(heads):
            for p, (k, v) in enumerate(zip(split(kb_ref[h]), split(vb_ref[h]))):
                at = p * dim + key_lane(0, h, rank)
                main_ref[at : at + rank, h * dim : (h + 1) * dim] = k
                at = value_lane(0, h, rank, heads)
                if h == 0:
                    main_ref[p * dim + at : p * dim + at + rank, width:] = v
                else:
                    at = p * half + at
                    tail_ref[at : at + rank, (h - 1) * dim : h * dim] = v

    for c, place in enumerate(places):
        if c == len(places) - 1:
            build()
        x_copy(c).wait()
        w_copy(c).wait()
        part = dot(x_ref[:, place], w_ref[place, :])
        if c == 0:
            acc_ref[...] = part
        else:
            acc_ref[...] += part

    def column(at):
        return acc_ref[:, at * dim : (at + 1) * dim] + b_ref[at : at + 1, :]

    def normed(at, gain):
        x = column(at)
        mean_square = jnp.mean(x * x, axis=-1, keepdims=True)
        return x * lax.rsqrt(mean_square + epsilon) * gain

    queries, keys, values = [], [], []
    for h in range(heads):
        q = normed(h, qg_ref[...])
        k = normed(heads + h, kg_ref[...])
        v = column(2 * heads + h)
        queries.append(q)
        keys.append(k)
        values.append(v)
        for b in range(samples):
            rows = slice(b * tokens, (b + 1) * tokens)
            row = (b * heads + h) * 2
            sums_ref[row : row + 1, :] = jnp.sum(k[rows], axis=0, keepdims=True)
            sums_ref[row + 1 : row + 2, :] = jnp.sum(v[rows], axis=0, keepdims=True)
    for p, piece in enumerate(pieces_of(sums_ref[...], 3)):
        payload_ref[0, tokens : tokens + SUM_ROWS, p * dim : (p + 1) * dim] = piece
    def by_sample(j):
        rows = [centers_ref[b, h, j : j + 1, :] for b in range(samples) for h in range(heads)]
        return [
            jnp.concatenate(
                [jnp.broadcast_to(rows[b * heads + h], (tokens, dim)) for b in range(samples)], axis=0
            )
            for h in range(heads)
        ]

    key_centers, value_centers = by_sample(0), by_sample(1)
    shifted = [keys[h] - key_centers[h] for h in range(heads)]
    shifted += [values[h] - value_centers[h] for h in range(heads)]

    def coded(x, columns):
        high, low = split(x)
        both = dot(high, main_ref[:, columns], NT)
        return both[:, :dim] + (both[:, dim:] + dot(low, main_ref[:dim, columns], NT))

    code = coded(jnp.concatenate(shifted[: heads + 1], axis=1), slice(0, width + dim))
    query_code = coded(jnp.concatenate(queries, axis=1), slice(0, width)) * log_factor
    high, low = split(jnp.concatenate(shifted[heads + 1 :], axis=1))
    both = dot(high, tail_ref[...], NT)
    tail = both + pltpu.roll(both, half, 1) + dot(low, tail_ref[...], NT)
    payload_ref[0, :tokens, :dim] = code[:tokens].astype(bf16)
    payload_ref[0, :tokens, dim : 2 * dim] = pltpu.roll(code[tokens:], rank, 1).astype(bf16)
    lanes = lane_ids(tokens, dim)
    last = jnp.where(lanes < half, tail[:tokens], pltpu.roll(tail[tokens:], half, 1))
    payload_ref[0, :tokens, samples * dim :] = last.astype(bf16)
    high_0 = query_code[:tokens].astype(bf16).astype(f32)
    low_0 = query_code[:tokens] - high_0
    query_1 = pltpu.roll(query_code[tokens:], rank, 1)
    high_1 = query_1.astype(bf16).astype(f32)
    low_1 = query_1 - high_1
    turned = pltpu.roll(low_1, half, 1)
    query_ref[:, :dim] = jnp.where(lanes < heads * rank, high_0, turned).astype(bf16)
    query_ref[:, dim : 2 * dim] = jnp.where(lanes < rank, turned, high_1).astype(bf16)
    query_ref[:, 2 * dim :] = jnp.where(lanes < heads * rank, low_0, low_1).astype(bf16)
    for h in range(heads):
        qkv_ref[:, h * dim : (h + 1) * dim] = queries[h] * log_factor
        qkv_ref[:, width + h * dim : width + (h + 1) * dim] = keys[h]
        qkv_ref[:, 2 * width + h * dim : 2 * width + (h + 1) * dim] = values[h]


def near_kernel(
    qkv_ref, centers_ref, refresh_ref, vb_ref, near_ref, rel_ref, basis_h, basis_l, old_ref,
    *, samples, tokens, heads, dim, rank,
):
    width = heads * dim
    fill_basis(basis_h, basis_l, vb_ref, samples, heads, dim, rank)
    old_ref[...] = jnp.zeros_like(old_ref)
    for b in range(samples):
        for h in range(heads):
            for j in range(2):
                row = (b * heads + h) * 2 + j
                keep = jnp.where(refresh_ref[j, h] == 1, 0.0, 1.0)
                old_ref[row : row + 1, :] = centers_ref[b, h, j : j + 1, :]
                old_ref[SUM_ROWS + row : SUM_ROWS + row + 1, :] = jnp.full((1, dim), keep, f32)
    for b in range(samples):
        rows = slice(b * tokens, (b + 1) * tokens)
        for h in range(heads):
            head = slice(h * dim, (h + 1) * dim)
            q = qkv_ref[rows, head]
            k = split(qkv_ref[rows, width + h * dim : width + (h + 1) * dim])
            v = split(qkv_ref[rows, 2 * width + h * dim : 2 * width + (h + 1) * dim])
            scores = dot3(split(q), k, NT)
            row_max = jnp.max(scores, axis=-1, keepdims=True)
            weights = jnp.exp2(scores - row_max)
            row_sum = jnp.sum(weights, axis=-1, keepdims=True)
            near_ref[rows, head] = dot3(split(weights), v) / row_sum
            center = jnp.sum(q * centers_ref[b, h, 0:1, :], axis=-1, keepdims=True)
            rel = row_max + jnp.log(row_sum) * log2_e - center
            rel_ref[rows, head] = jnp.broadcast_to(rel, (tokens, dim))


def query_parts(query_ref, sample, heads, dim, rank):
    lanes = lane_ids(query_ref.shape[0], dim)
    if sample == 0:
        return query_ref[:, :dim].astype(f32), query_ref[:, 2 * dim :].astype(f32)
    first, second = query_ref[:, :dim].astype(f32), query_ref[:, dim : 2 * dim].astype(f32)
    turned = pltpu.roll(jnp.where(lanes < rank, second, first), dim // 2, 1)
    return second, jnp.where(lanes < heads * rank, turned, query_ref[:, 2 * dim :].astype(f32))


def code_attention(query_ref, tiles, *, samples, tokens, heads, dim, rank):
    lanes = lane_ids(tokens, dim)
    scores, values = [], []
    for b in range(samples):
        high, low = query_parts(query_ref, b, heads, dim, rank)
        stacked = []
        for h in range(heads):
            own = within(lanes, key_lane(b, h, rank), rank)
            both = [jnp.where(own, part, 0.0).astype(bf16) for part in (high, low)]
            stacked.append(jnp.concatenate(both, axis=1))
        left = jnp.concatenate(stacked, axis=0)
        codes = [ref[i, :tokens, b * dim : (b + 1) * dim] for ref, i in tiles]
        values.append(jnp.concatenate(codes, axis=0))
        parts = []
        for i in range(0, len(codes), 2):
            some = jnp.concatenate(codes[i : i + 2], axis=0)
            both = dot(left, jnp.concatenate([some, some], axis=1), NT)
            parts += [both[:, j * tokens : (j + 1) * tokens] for j in range(len(codes[i : i + 2]))]
        scores.append(parts)
    rest = jnp.concatenate([ref[i, :tokens, samples * dim :] for ref, i in tiles], axis=0)
    weights, scales, logs = [], [], []
    for b in range(samples):
        best = scores[b][0]
        for part in scores[b][1:]:
            best = jnp.maximum(best, part)
        row_max = jnp.max(best, axis=-1, keepdims=True)
        total = jnp.zeros_like(best)
        parts = []
        for part in scores[b]:
            weight = jnp.exp2(part - row_max).astype(bf16)
            total = total + weight.astype(f32)
            parts.append(weight)
        row_sum = jnp.sum(total, axis=-1, keepdims=True)
        weights.append(jnp.concatenate(parts, axis=1))
        scales.append(1.0 / row_sum)
        log = row_max + jnp.log(row_sum) * log2_e
        logs.append([log[h * tokens : (h + 1) * tokens] for h in range(heads)])
    outs = []
    for b in range(samples):
        results = [dot(weights[b][:tokens], values[b])]
        others = dot(weights[b][tokens:], rest)
        results += [others[h * tokens : (h + 1) * tokens] for h in range(heads - 1)]
        out = jnp.zeros((tokens, dim), f32)
        for h in range(heads):
            part = results[h] * scales[b][h * tokens : (h + 1) * tokens]
            out = jnp.where(within(lanes, value_lane(b, h, rank, heads), rank), part, out)
        outs.append(out)
    return outs, logs


def spread(b, logs, tokens, heads, dim, rank):
    lanes = lane_ids(tokens, dim)
    out = jnp.zeros((tokens, dim), f32)
    for h in range(heads):
        place = within(lanes, value_lane(b, h, rank, heads), rank)
        for p in range(3):
            place = place | (lanes == log_lane(b, h, p, rank))
        out = jnp.where(place, logs[h], out)
    return out


def tree_sum(parts):
    while len(parts) > 1:
        parts = [parts[i] + parts[i + 1] for i in range(0, len(parts), 2)]
    return parts[0]


def tiles_of(refs):
    return [(ref, i) for ref in refs for i in range(ref.shape[0])]


def early_kernel(query_ref, *refs, samples, tokens, heads, dim, rank):
    out_ref, log_ref = refs[-2:]
    tiles = tiles_of(refs[:-2])
    lanes = lane_ids(tokens, dim)
    outs, all_logs = code_attention(
        query_ref, tiles, samples=samples, tokens=tokens, heads=heads, dim=dim, rank=rank
    )
    for b in range(samples):
        rows = slice(b * tokens, (b + 1) * tokens)
        out, logs = outs[b], all_logs[b]
        out_ref[rows, :] = out
        log_ref[rows, :] = spread(b, logs, tokens, heads, dim, rank)


def partner_kernel(
    query_ref, part_ref, part_log_ref, *refs, order, late, samples, tokens, heads, dim, rank
):
    out_ref, half_ref = refs[-2:]
    tiles = tiles_of(refs[:-2])
    parts = []
    for place in order:
        ref, i = tiles[place]
        rows = slice(tokens, tokens + SUM_ROWS)
        pieces = [ref[i, rows, p * dim : (p + 1) * dim].astype(f32) for p in range(3)]
        parts.append(pieces[0] + (pieces[1] + pieces[2]))
    pieces = [piece.astype(f32) for piece in pieces_of(tree_sum(parts), 2)]
    half_ref[...] = pieces[0] + pieces[1]
    empty = jnp.zeros((tokens - SUM_ROWS, dim), f32)
    turned = [jnp.concatenate([piece, empty], axis=0).T for piece in pieces]
    lanes = lane_ids(tokens, dim)
    outs, all_logs = code_attention(
        query_ref, tiles[-late:], samples=samples, tokens=tokens, heads=heads, dim=dim, rank=rank
    )
    for b in range(samples):
        rows = slice(b * tokens, (b + 1) * tokens)
        out, logs = outs[b], all_logs[b]
        before, before_log = part_ref[rows, :], part_log_ref[rows, :]
        log = spread(b, logs, tokens, heads, dim, rank)
        top = jnp.maximum(log, before_log)
        new = jnp.exp2(log - top)
        whole = new + jnp.exp2(before_log - top)
        out = before + (out - before) * (new / whole)
        log = top + jnp.log(whole) * log2_e
        for p, piece in enumerate(pieces_of(log, 3)):
            place = within(lanes, log_lane(b, 0, p, rank), heads)
            out = jnp.where(place, piece.astype(f32), out)
        at = sum_lane(b, rank)
        out = jnp.where(within(lanes, at, 2 * samples * heads), pltpu.roll(turned[b], at, 1), out)
        out_ref[rows, :] = out.astype(bf16)


def own_kernel(
    query_ref, near_ref, rel_ref, old_ref, basis_h, basis_l, *refs,
    samples, tokens, heads, dim, rank,
):
    merged_ref, log_ref = refs[-2:]
    tiles = tiles_of(refs[:-2])
    lanes = lane_ids(tokens, dim)
    outs, all_logs = code_attention(
        query_ref, tiles, samples=samples, tokens=tokens, heads=heads, dim=dim, rank=rank
    )
    for b in range(samples):
        rows = slice(b * tokens, (b + 1) * tokens)
        out, logs = outs[b], all_logs[b]
        far = dot3(split(out), (basis_h[b], basis_l[b]))
        kept = jnp.zeros((tokens, dim), f32)
        for h in range(heads):
            columns = slice(h * dim, (h + 1) * dim)
            near, rel = near_ref[rows, columns], rel_ref[rows, columns]
            top = jnp.maximum(rel, logs[h])
            far_part = jnp.exp2(logs[h] - top)
            whole = jnp.exp2(rel - top) + far_part
            row = (b * heads + h) * 2 + 1
            value = far[:, columns] + old_ref[row : row + 1, :] - near
            merged_ref[rows, columns] = near + value * (far_part / whole)
            log = top + jnp.log(whole) * log2_e
            kept = jnp.where(lanes == log_lane(b, h, 0, rank), log, kept)
        log_ref[rows, :] = kept


def finish_kernel(
    back_ref, half_ref, merged_ref, log_ref, old_ref, basis_h, basis_l, w_ref,
    mixed_hbm, new_hbm, attended_ref, mixed_ref, new_ref, sem, new_sem,
    *, samples, tokens, heads, dim, rank, length,
):
    chunks, columns = mixed_ref.shape[0], mixed_ref.shape[2]
    copies = []
    sums = jnp.zeros((tokens, dim), f32)
    for b in range(samples):
        rows = slice(b * tokens, (b + 1) * tokens)
        codes = back_ref[rows, :]
        extra = codes.astype(f32)
        sums = sums + pltpu.roll(extra, dim - sum_lane(b, rank), 1)
        far_log = extra + (pltpu.roll(extra, dim - 8, 1) + pltpu.roll(extra, dim - 16, 1))
        share = 1.0 / (1.0 + jnp.exp2(log_ref[rows, :] - far_log))
        far = dot(codes, basis_h[b]) + dot(codes, basis_l[b])
        for h in range(heads):
            head = slice(h * dim, (h + 1) * dim)
            at = log_lane(b, h, 0, rank)
            row = (b * heads + h) * 2 + 1
            near = merged_ref[rows, head]
            value = far[:, head] + old_ref[row : row + 1, :] - near
            attended_ref[rows, head] = (near + value * share[:, at : at + 1]).astype(bf16)
    for c in range(chunks):
        place = slice(c * columns, (c + 1) * columns)
        mixed_ref[c] = dot(attended_ref[...], w_ref[:, place]).astype(bf16)
        copies.append(pltpu.make_async_copy(mixed_ref.at[c], mixed_hbm.at[:, place], sem.at[c]))
        copies[-1].start()
        if c == 1:
            fresh = (half_ref[...] + sums.T[:SUM_ROWS, :]) * (1.0 / length)
            fresh = jnp.where(old_ref[SUM_ROWS:, :] > 0.5, old_ref[:SUM_ROWS, :], fresh)
            for b in range(samples):
                for h in range(heads):
                    row = (b * heads + h) * 2
                    new_ref[b, h] = fresh[row : row + 2, :]
            copies.append(pltpu.make_async_copy(new_ref, new_hbm, new_sem.at[0]))
            copies[-1].start()
    for copy in copies:
        copy.wait()


VMEM = pl.BlockSpec(memory_space=pltpu.VMEM)
HBM = pl.BlockSpec(memory_space=pltpu.HBM)


def per_device(
    images, w_qkv, b_qkv, q_gain, k_gain, key_basis, value_basis, centers, refresh, w_out
):
    samples, tokens, model = images.shape
    heads, dim, rank = key_basis.shape
    seq = lax.axis_size("seq")
    rows = samples * tokens
    width = heads * dim
    sizes = dict(samples=samples, tokens=tokens, heads=heads, dim=dim)
    log_factor = log2_e / math.sqrt(dim)
    flat = images.reshape(rows, model)
    key_rows = key_basis.transpose(0, 2, 1)
    value_rows = value_basis.transpose(0, 2, 1)
    center_rows = centers.transpose(0, 2, 1, 3)
    cuts = tuple(model * i // 4 for i in range(5))
    shard = (1, tokens + SUM_ROWS, width)
    params = lambda mib: pltpu.CompilerParams(vmem_limit_bytes=mib * 2**20)

    payload, query, qkv = pl.pallas_call(
        functools.partial(project_kernel, **sizes, rank=rank, log_factor=log_factor, cuts=cuts),
        in_specs=[HBM] * 8,
        out_specs=[VMEM] * 3,
        out_shape=[
            jax.ShapeDtypeStruct(shard, bf16),
            jax.ShapeDtypeStruct((tokens, width), bf16),
            jax.ShapeDtypeStruct((rows, 3 * width), f32),
        ],
        scratch_shapes=[
            pltpu.VMEM((rows, model), bf16),
            pltpu.VMEM((model, 3 * width), bf16),
            pltpu.VMEM((3 * heads, dim), f32),
            pltpu.VMEM((1, dim), f32),
            pltpu.VMEM((1, dim), f32),
            pltpu.VMEM((heads, rank, dim), f32),
            pltpu.VMEM((heads, rank, dim), f32),
            pltpu.VMEM((samples, heads, 2, dim), f32),
            pltpu.VMEM((rows, 3 * width), f32),
            pltpu.VMEM((2 * dim, width + dim), bf16),
            pltpu.VMEM((dim, width - dim), bf16),
            pltpu.VMEM((SUM_ROWS, dim), f32),
            pltpu.SemaphoreType.DMA((2, len(cuts) - 1)),
            pltpu.SemaphoreType.DMA((6,)),
        ],
        compiler_params=params(32),
        name="project",
    )(
        *(
            pltpu.with_memory_space_constraint(x, pltpu.HBM)
            for x in (
                flat, w_qkv, b_qkv.reshape(3 * heads, dim), q_gain.reshape(1, -1),
                k_gain.reshape(1, -1), key_rows, value_rows, center_rows,
            )
        )
    )

    def swap(x, mask):
        return lax.ppermute(x, "seq", [(i, i ^ mask) for i in range(seq)])

    far_mask = seq // 2
    bits = [m for m in (2**i for i in range(1, seq.bit_length() - 1)) if m < far_mask]
    held = [(payload, [0])]
    direct = sum(bits[:2])
    for mask in range(2, 2 * direct, 2):
        if mask & ~direct == 0:
            held.append((swap(payload, mask), [mask]))
    for bit in bits[2:]:
        block = jnp.concatenate([a for a, _ in held], axis=0)
        names = [m for _, ms in held for m in ms]
        held.append((swap(block, bit), [m ^ bit for m in names]))

    query_far = swap(query, far_mask)

    near, rel, basis_high, basis_low, old = pl.pallas_call(
        functools.partial(near_kernel, **sizes, rank=rank),
        in_specs=[VMEM, VMEM, pl.BlockSpec(memory_space=pltpu.SMEM), VMEM],
        out_specs=[VMEM] * 5,
        out_shape=[
            jax.ShapeDtypeStruct((rows, width), f32),
            jax.ShapeDtypeStruct((rows, width), f32),
            jax.ShapeDtypeStruct((samples, dim, width), bf16),
            jax.ShapeDtypeStruct((samples, dim, width), bf16),
            jax.ShapeDtypeStruct((2 * SUM_ROWS, dim), f32),
        ],
        compiler_params=params(24),
        cost_estimate=pl.CostEstimate(
            flops=1200 * rows * tokens * width, bytes_accessed=50 * rows * width * 4, transcendentals=0
        ),
        name="near",
    )(qkv, center_rows, refresh, value_rows)

    for i in (1,):
        x, _ = lax.optimization_barrier((held[i][0], rel))
        held[i] = (x, held[i][1])
    held.insert(1, (swap(payload, 1), [1]))
    early = [a for a, _ in held]
    held += [(swap(a, 1), [m ^ 1 for m in ms]) for a, ms in held[2:]]
    arrays = [a for a, _ in held]
    names = [m for _, ms in held for m in ms]
    order = tuple(names.index(m) for m in range(len(names)))
    count_early = sum(a.shape[0] for a in early)

    def cost(shards):
        return pl.CostEstimate(
            flops=8 * rows * tokens * shards * width,
            bytes_accessed=shards * 2 * tokens * width,
            transcendentals=0,
        )

    part, part_log = pl.pallas_call(
        functools.partial(early_kernel, **sizes, rank=rank),
        in_specs=[VMEM] * (1 + len(early)),
        out_specs=[VMEM] * 2,
        out_shape=[jax.ShapeDtypeStruct((rows, dim), f32)] * 2,
        compiler_params=params(32),
        cost_estimate=cost(count_early),
        name="early",
    )(query_far, *early)
    back, half = pl.pallas_call(
        functools.partial(
            partner_kernel, **sizes, rank=rank, order=order, late=len(names) - count_early
        ),
        in_specs=[VMEM] * (3 + len(arrays)),
        out_specs=[VMEM] * 2,
        out_shape=[
            jax.ShapeDtypeStruct((rows, dim), bf16),
            jax.ShapeDtypeStruct((SUM_ROWS, dim), f32),
        ],
        compiler_params=params(32),
        cost_estimate=cost(len(names)),
        name="partner",
    )(query_far, part, part_log, *arrays)
    returned = swap(back, far_mask)
    merged, logs = pl.pallas_call(
        functools.partial(own_kernel, **sizes, rank=rank),
        in_specs=[VMEM] * (5 + len(arrays)),
        out_specs=[VMEM] * 2,
        out_shape=[
            jax.ShapeDtypeStruct((rows, width), f32),
            jax.ShapeDtypeStruct((rows, dim), f32),
        ],
        compiler_params=params(32),
        cost_estimate=cost(len(names)),
        name="own",
    )(query, near, rel, old, basis_high, basis_low, *arrays[1:])

    columns = 512
    mixed, new_centers = pl.pallas_call(
        functools.partial(finish_kernel, **sizes, rank=rank, length=tokens * seq),
        in_specs=[VMEM] * 8,
        out_specs=[HBM, HBM],
        out_shape=[
            jax.ShapeDtypeStruct((rows, model), bf16),
            jax.ShapeDtypeStruct((samples, heads, 2, dim), f32),
        ],
        scratch_shapes=[
            pltpu.VMEM((rows, width), bf16),
            pltpu.VMEM((model // columns, rows, columns), bf16),
            pltpu.VMEM((samples, heads, 2, dim), f32),
            pltpu.SemaphoreType.DMA((model // columns,)),
            pltpu.SemaphoreType.DMA((1,)),
        ],
        compiler_params=params(24),
        name="finish",
    )(returned, half, merged, logs, old, basis_high, basis_low, w_out)
    return (mixed.reshape(samples, tokens, model), new_centers.transpose(0, 2, 1, 3))


def solution(mesh):
    return jax.shard_map(
        per_device,
        mesh=mesh,
        in_specs=(
            P("groups", "seq", None),
            P(),
            P(),
            P(),
            P(),
            P(),
            P(),
            P("groups", None, None, None),
            P(),
            P(),
        ),
        out_specs=(P("groups", "seq", None), P("groups", None, None, None)),
        check_vma=False,
    )
```

```python
import functools
import math

import jax
import jax.numpy as jnp
from jax import lax
from jax.experimental import pallas as pl
from jax.experimental.pallas import tpu as pltpu
from jax.sharding import PartitionSpec as P

epsilon = 1e-06
log2_e = math.log2(math.e)
f32 = jnp.float32
bf16 = jnp.bfloat16
SUM_ROWS = 16
NT = (((1,), (1,)), ((), ()))
NN = (((1,), (0,)), ((), ()))


def dot(a, b, dims=NN):
    return lax.dot_general(a, b, dims, preferred_element_type=f32)


def split(x):
    high = x.astype(bf16)
    low = (x - high.astype(f32)).astype(bf16)
    return high, low


def dot3(a, b, dims=NN):
    return dot(a[0], b[0], dims) + (dot(a[0], b[1], dims) + dot(a[1], b[0], dims))


def pieces_of(x, count):
    out = []
    for _ in range(count):
        top = x.astype(bf16)
        out.append(top)
        x = x - top.astype(f32)
    return out


def lane_ids(rows, lanes):
    return lax.broadcasted_iota(jnp.int32, (rows, lanes), 1)


def key_lane(sample, head, rank):
    return head * rank if sample == 0 else (head + 1) * rank


def value_lane(sample, head, rank, heads):
    if head == 0:
        return heads * rank if sample == 0 else 0
    return ((heads - 1) * sample + head - 1) * rank


def free_lane(sample, rank):
    return 2 * rank if sample == 0 else rank


def log_lane(sample, head, piece, rank):
    return free_lane(sample, rank) + 8 * piece + head


def sum_lane(sample, rank):
    return free_lane(sample, rank) + 20


def within(lanes, start, count):
    return (lanes >= start) & (lanes < start + count)


def fill_basis(basis_h, basis_l, vb_ref, samples, heads, dim, rank):
    basis_h[...] = jnp.zeros_like(basis_h)
    basis_l[...] = jnp.zeros_like(basis_l)
    for h in range(heads):
        vh, vl = split(vb_ref[h])
        for b in range(samples):
            at = value_lane(b, h, rank, heads)
            basis_h[b, at : at + rank, h * dim : (h + 1) * dim] = vh
            basis_l[b, at : at + rank, h * dim : (h + 1) * dim] = vl


def project_kernel(
    images_hbm, w_hbm, b_hbm, qg_hbm, kg_hbm, kb_hbm, vb_hbm, centers_hbm,
    payload_ref, query_ref, qkv_ref,
    x_ref, w_ref, b_ref, qg_ref, kg_ref, kb_ref, vb_ref, centers_ref,
    acc_ref, main_ref, tail_ref, sums_ref, big_sem, small_sem,
    *, samples, tokens, heads, dim, rank, log_factor, cuts,
):
    width = heads * dim
    places = [slice(first, last) for first, last in zip(cuts[:-1], cuts[1:])]

    def x_copy(c):
        p = places[c]
        return pltpu.make_async_copy(images_hbm.at[:, p], x_ref.at[:, p], big_sem.at[0, c])

    def w_copy(c):
        p = places[c]
        return pltpu.make_async_copy(w_hbm.at[p, :], w_ref.at[p, :], big_sem.at[1, c])

    small = [
        pltpu.make_async_copy(source, target, small_sem.at[i])
        for i, (source, target) in enumerate(
            [
                (kb_hbm, kb_ref), (vb_hbm, vb_ref), (b_hbm, b_ref),
                (qg_hbm, qg_ref), (kg_hbm, kg_ref), (centers_hbm, centers_ref),
            ]
        )
    ]
    for copy in small:
        copy.start()
    for c in range(len(places)):
        w_copy(c).start()
        x_copy(c).start()
    main_ref[...] = jnp.zeros_like(main_ref)
    tail_ref[...] = jnp.zeros_like(tail_ref)
    sums_ref[...] = jnp.zeros_like(sums_ref)
    half = dim // 2

    def build():
        for copy in small:
            copy.wait()
        for h in range(heads):
            for p, (k, v) in enumerate(zip(split(kb_ref[h]), split(vb_ref[h]))):
                at = p * dim + key_lane(0, h, rank)
                main_ref[at : at + rank, h * dim : (h + 1) * dim] = k
                at = value_lane(0, h, rank, heads)
                if h == 0:
                    main_ref[p * dim + at : p * dim + at + rank, width:] = v
                else:
                    at = p * half + at
                    tail_ref[at : at + rank, (h - 1) * dim : h * dim] = v

    for c, place in enumerate(places):
        if c == len(places) - 1:
            build()
        x_copy(c).wait()
        w_copy(c).wait()
        part = dot(x_ref[:, place], w_ref[place, :])
        if c == 0:
            acc_ref[...] = part
        else:
            acc_ref[...] += part

    def column(at):
        return acc_ref[:, at * dim : (at + 1) * dim] + b_ref[at : at + 1, :]

    def normed(at, gain):
        x = column(at)
        mean_square = jnp.mean(x * x, axis=-1, keepdims=True)
        return x * lax.rsqrt(mean_square + epsilon) * gain

    queries, keys, values = [], [], []
    for h in range(heads):
        q = normed(h, qg_ref[...])
        k = normed(heads + h, kg_ref[...])
        v = column(2 * heads + h)
        queries.append(q)
        keys.append(k)
        values.append(v)
        for b in range(samples):
            rows = slice(b * tokens, (b + 1) * tokens)
            row = (b * heads + h) * 2
            sums_ref[row : row + 1, :] = jnp.sum(k[rows], axis=0, keepdims=True)
            sums_ref[row + 1 : row + 2, :] = jnp.sum(v[rows], axis=0, keepdims=True)
    for p, piece in enumerate(pieces_of(sums_ref[...], 3)):
        payload_ref[0, tokens : tokens + SUM_ROWS, p * dim : (p + 1) * dim] = piece
    def by_sample(j):
        rows = [centers_ref[b, h, j : j + 1, :] for b in range(samples) for h in range(heads)]
        return [
            jnp.concatenate(
                [jnp.broadcast_to(rows[b * heads + h], (tokens, dim)) for b in range(samples)], axis=0
            )
            for h in range(heads)
        ]

    key_centers, value_centers = by_sample(0), by_sample(1)
    shifted = [keys[h] - key_centers[h] for h in range(heads)]
    shifted += [values[h] - value_centers[h] for h in range(heads)]

    def coded(x, columns):
        high, low = split(x)
        both = dot(high, main_ref[:, columns], NT)
        return both[:, :dim] + (both[:, dim:] + dot(low, main_ref[:dim, columns], NT))

    code = coded(jnp.concatenate(shifted[: heads + 1], axis=1), slice(0, width + dim))
    query_code = coded(jnp.concatenate(queries, axis=1), slice(0, width)) * log_factor
    high, low = split(jnp.concatenate(shifted[heads + 1 :], axis=1))
    both = dot(high, tail_ref[...], NT)
    tail = both + pltpu.roll(both, half, 1) + dot(low, tail_ref[...], NT)
    payload_ref[0, :tokens, :dim] = code[:tokens].astype(bf16)
    payload_ref[0, :tokens, dim : 2 * dim] = pltpu.roll(code[tokens:], rank, 1).astype(bf16)
    lanes = lane_ids(tokens, dim)
    last = jnp.where(lanes < half, tail[:tokens], pltpu.roll(tail[tokens:], half, 1))
    payload_ref[0, :tokens, samples * dim :] = last.astype(bf16)
    high_0 = query_code[:tokens].astype(bf16).astype(f32)
    low_0 = query_code[:tokens] - high_0
    query_1 = pltpu.roll(query_code[tokens:], rank, 1)
    high_1 = query_1.astype(bf16).astype(f32)
    low_1 = query_1 - high_1
    turned = pltpu.roll(low_1, half, 1)
    query_ref[:, :dim] = jnp.where(lanes < heads * rank, high_0, turned).astype(bf16)
    query_ref[:, dim : 2 * dim] = jnp.where(lanes < rank, turned, high_1).astype(bf16)
    query_ref[:, 2 * dim :] = jnp.where(lanes < heads * rank, low_0, low_1).astype(bf16)
    for h in range(heads):
        qkv_ref[:, h * dim : (h + 1) * dim] = queries[h] * log_factor
        qkv_ref[:, width + h * dim : width + (h + 1) * dim] = keys[h]
        qkv_ref[:, 2 * width + h * dim : 2 * width + (h + 1) * dim] = values[h]


def near_kernel(
    qkv_ref, centers_ref, refresh_ref, vb_ref, near_ref, rel_ref, basis_h, basis_l, old_ref,
    *, samples, tokens, heads, dim, rank,
):
    width = heads * dim
    fill_basis(basis_h, basis_l, vb_ref, samples, heads, dim, rank)
    old_ref[...] = jnp.zeros_like(old_ref)
    for b in range(samples):
        for h in range(heads):
            for j in range(2):
                row = (b * heads + h) * 2 + j
                keep = jnp.where(refresh_ref[j, h] == 1, 0.0, 1.0)
                old_ref[row : row + 1, :] = centers_ref[b, h, j : j + 1, :]
                old_ref[SUM_ROWS + row : SUM_ROWS + row + 1, :] = jnp.full((1, dim), keep, f32)
    for b in range(samples):
        rows = slice(b * tokens, (b + 1) * tokens)
        for h in range(heads):
            head = slice(h * dim, (h + 1) * dim)
            q = qkv_ref[rows, head]
            k = split(qkv_ref[rows, width + h * dim : width + (h + 1) * dim])
            v = split(qkv_ref[rows, 2 * width + h * dim : 2 * width + (h + 1) * dim])
            scores = dot3(split(q), k, NT)
            row_max = jnp.max(scores, axis=-1, keepdims=True)
            weights = jnp.exp2(scores - row_max)
            row_sum = jnp.sum(weights, axis=-1, keepdims=True)
            near_ref[rows, head] = dot3(split(weights), v) / row_sum
            center = jnp.sum(q * centers_ref[b, h, 0:1, :], axis=-1, keepdims=True)
            rel = row_max + jnp.log(row_sum) * log2_e - center
            rel_ref[rows, head] = jnp.broadcast_to(rel, (tokens, dim))


def query_parts(query_ref, sample, heads, dim, rank):
    lanes = lane_ids(query_ref.shape[0], dim)
    if sample == 0:
        return query_ref[:, :dim].astype(f32), query_ref[:, 2 * dim :].astype(f32)
    first, second = query_ref[:, :dim].astype(f32), query_ref[:, dim : 2 * dim].astype(f32)
    turned = pltpu.roll(jnp.where(lanes < rank, second, first), dim // 2, 1)
    return second, jnp.where(lanes < heads * rank, turned, query_ref[:, 2 * dim :].astype(f32))


def code_attention(query_ref, tiles, *, samples, tokens, heads, dim, rank):
    lanes = lane_ids(tokens, dim)
    scores, values = [], []
    for b in range(samples):
        high, low = query_parts(query_ref, b, heads, dim, rank)
        stacked = []
        for h in range(heads):
            own = within(lanes, key_lane(b, h, rank), rank)
            both = [jnp.where(own, part, 0.0).astype(bf16) for part in (high, low)]
            stacked.append(jnp.concatenate(both, axis=1))
        left = jnp.concatenate(stacked, axis=0)
        codes = [ref[i, :tokens, b * dim : (b + 1) * dim] for ref, i in tiles]
        values.append(jnp.concatenate(codes, axis=0))
        parts = []
        for i in range(0, len(codes), 2):
            some = jnp.concatenate(codes[i : i + 2], axis=0)
            both = dot(left, jnp.concatenate([some, some], axis=1), NT)
            parts += [both[:, j * tokens : (j + 1) * tokens] for j in range(len(codes[i : i + 2]))]
        scores.append(parts)
    rest = jnp.concatenate([ref[i, :tokens, samples * dim :] for ref, i in tiles], axis=0)
    weights, scales, logs = [], [], []
    for b in range(samples):
        best = scores[b][0]
        for part in scores[b][1:]:
            best = jnp.maximum(best, part)
        row_max = jnp.max(best, axis=-1, keepdims=True)
        total = jnp.zeros_like(best)
        parts = []
        for part in scores[b]:
            weight = jnp.exp2(part - row_max).astype(bf16)
            total = total + weight.astype(f32)
            parts.append(weight)
        row_sum = jnp.sum(total, axis=-1, keepdims=True)
        weights.append(jnp.concatenate(parts, axis=1))
        scales.append(1.0 / row_sum)
        log = row_max + jnp.log(row_sum) * log2_e
        logs.append([log[h * tokens : (h + 1) * tokens] for h in range(heads)])
    outs = []
    for b in range(samples):
        results = [dot(weights[b][:tokens], values[b])]
        others = dot(weights[b][tokens:], rest)
        results += [others[h * tokens : (h + 1) * tokens] for h in range(heads - 1)]
        out = jnp.zeros((tokens, dim), f32)
        for h in range(heads):
            part = results[h] * scales[b][h * tokens : (h + 1) * tokens]
            out = jnp.where(within(lanes, value_lane(b, h, rank, heads), rank), part, out)
        outs.append(out)
    return outs, logs


def spread(b, logs, tokens, heads, dim, rank):
    lanes = lane_ids(tokens, dim)
    out = jnp.zeros((tokens, dim), f32)
    for h in range(heads):
        place = within(lanes, value_lane(b, h, rank, heads), rank)
        for p in range(3):
            place = place | (lanes == log_lane(b, h, p, rank))
        out = jnp.where(place, logs[h], out)
    return out


def tree_sum(parts):
    while len(parts) > 1:
        parts = [parts[i] + parts[i + 1] for i in range(0, len(parts), 2)]
    return parts[0]


def tiles_of(refs):
    return [(ref, i) for ref in refs for i in range(ref.shape[0])]


def early_kernel(query_ref, *refs, samples, tokens, heads, dim, rank):
    out_ref, log_ref = refs[-2:]
    tiles = tiles_of(refs[:-2])
    lanes = lane_ids(tokens, dim)
    outs, all_logs = code_attention(
        query_ref, tiles, samples=samples, tokens=tokens, heads=heads, dim=dim, rank=rank
    )
    for b in range(samples):
        rows = slice(b * tokens, (b + 1) * tokens)
        out, logs = outs[b], all_logs[b]
        out_ref[rows, :] = out
        log_ref[rows, :] = spread(b, logs, tokens, heads, dim, rank)


def partner_kernel(
    query_ref, part_ref, part_log_ref, *refs, order, late, samples, tokens, heads, dim, rank
):
    out_ref, half_ref = refs[-2:]
    tiles = tiles_of(refs[:-2])
    parts = []
    for place in order:
        ref, i = tiles[place]
        rows = slice(tokens, tokens + SUM_ROWS)
        pieces = [ref[i, rows, p * dim : (p + 1) * dim].astype(f32) for p in range(3)]
        parts.append(pieces[0] + (pieces[1] + pieces[2]))
    pieces = [piece.astype(f32) for piece in pieces_of(tree_sum(parts), 2)]
    half_ref[...] = pieces[0] + pieces[1]
    empty = jnp.zeros((tokens - SUM_ROWS, dim), f32)
    turned = [jnp.concatenate([piece, empty], axis=0).T for piece in pieces]
    lanes = lane_ids(tokens, dim)
    outs, all_logs = code_attention(
        query_ref, tiles[-late:], samples=samples, tokens=tokens, heads=heads, dim=dim, rank=rank
    )
    for b in range(samples):
        rows = slice(b * tokens, (b + 1) * tokens)
        out, logs = outs[b], all_logs[b]
        before, before_log = part_ref[rows, :], part_log_ref[rows, :]
        log = spread(b, logs, tokens, heads, dim, rank)
        top = jnp.maximum(log, before_log)
        new = jnp.exp2(log - top)
        whole = new + jnp.exp2(before_log - top)
        out = before + (out - before) * (new / whole)
        log = top + jnp.log(whole) * log2_e
        for p, piece in enumerate(pieces_of(log, 3)):
            place = within(lanes, log_lane(b, 0, p, rank), heads)
            out = jnp.where(place, piece.astype(f32), out)
        at = sum_lane(b, rank)
        out = jnp.where(within(lanes, at, 2 * samples * heads), pltpu.roll(turned[b], at, 1), out)
        out_ref[rows, :] = out.astype(bf16)


def own_kernel(
    query_ref, near_ref, rel_ref, old_ref, basis_h, basis_l, *refs,
    samples, tokens, heads, dim, rank,
):
    merged_ref, log_ref = refs[-2:]
    tiles = tiles_of(refs[:-2])
    lanes = lane_ids(tokens, dim)
    outs, all_logs = code_attention(
        query_ref, tiles, samples=samples, tokens=tokens, heads=heads, dim=dim, rank=rank
    )
    for b in range(samples):
        rows = slice(b * tokens, (b + 1) * tokens)
        out, logs = outs[b], all_logs[b]
        far = dot3(split(out), (basis_h[b], basis_l[b]))
        kept = jnp.zeros((tokens, dim), f32)
        for h in range(heads):
            columns = slice(h * dim, (h + 1) * dim)
            near, rel = near_ref[rows, columns], rel_ref[rows, columns]
            top = jnp.maximum(rel, logs[h])
            far_part = jnp.exp2(logs[h] - top)
            whole = jnp.exp2(rel - top) + far_part
            row = (b * heads + h) * 2 + 1
            value = far[:, columns] + old_ref[row : row + 1, :] - near
            merged_ref[rows, columns] = near + value * (far_part / whole)
            log = top + jnp.log(whole) * log2_e
            kept = jnp.where(lanes == log_lane(b, h, 0, rank), log, kept)
        log_ref[rows, :] = kept


def finish_kernel(
    back_ref, half_ref, merged_ref, log_ref, old_ref, basis_h, basis_l, w_ref,
    mixed_hbm, new_hbm, attended_ref, mixed_ref, new_ref, sem, new_sem,
    *, samples, tokens, heads, dim, rank, length,
):
    chunks, columns = mixed_ref.shape[0], mixed_ref.shape[2]
    copies = []
    sums = jnp.zeros((tokens, dim), f32)
    for b in range(samples):
        rows = slice(b * tokens, (b + 1) * tokens)
        codes = back_ref[rows, :]
        extra = codes.astype(f32)
        sums = sums + pltpu.roll(extra, dim - sum_lane(b, rank), 1)
        far_log = extra + (pltpu.roll(extra, dim - 8, 1) + pltpu.roll(extra, dim - 16, 1))
        share = 1.0 / (1.0 + jnp.exp2(log_ref[rows, :] - far_log))
        far = dot(codes, basis_h[b]) + dot(codes, basis_l[b])
        for h in range(heads):
            head = slice(h * dim, (h + 1) * dim)
            at = log_lane(b, h, 0, rank)
            row = (b * heads + h) * 2 + 1
            near = merged_ref[rows, head]
            value = far[:, head] + old_ref[row : row + 1, :] - near
            attended_ref[rows, head] = (near + value * share[:, at : at + 1]).astype(bf16)
    for c in range(chunks):
        place = slice(c * columns, (c + 1) * columns)
        mixed_ref[c] = dot(attended_ref[...], w_ref[:, place]).astype(bf16)
        copies.append(pltpu.make_async_copy(mixed_ref.at[c], mixed_hbm.at[:, place], sem.at[c]))
        copies[-1].start()
        if c == 1:
            fresh = (half_ref[...] + sums.T[:SUM_ROWS, :]) * (1.0 / length)
            fresh = jnp.where(old_ref[SUM_ROWS:, :] > 0.5, old_ref[:SUM_ROWS, :], fresh)
            for b in range(samples):
                for h in range(heads):
                    row = (b * heads + h) * 2
                    new_ref[b, h] = fresh[row : row + 2, :]
            copies.append(pltpu.make_async_copy(new_ref, new_hbm, new_sem.at[0]))
            copies[-1].start()
    for copy in copies:
        copy.wait()


VMEM = pl.BlockSpec(memory_space=pltpu.VMEM)
HBM = pl.BlockSpec(memory_space=pltpu.HBM)


def per_device(
    images, w_qkv, b_qkv, q_gain, k_gain, key_basis, value_basis, centers, refresh, w_out
):
    samples, tokens, model = images.shape
    heads, dim, rank = key_basis.shape
    seq = lax.axis_size("seq")
    rows = samples * tokens
    width = heads * dim
    sizes = dict(samples=samples, tokens=tokens, heads=heads, dim=dim)
    log_factor = log2_e / math.sqrt(dim)
    flat = images.reshape(rows, model)
    key_rows = key_basis.transpose(0, 2, 1)
    value_rows = value_basis.transpose(0, 2, 1)
    center_rows = centers.transpose(0, 2, 1, 3)
    cuts = tuple(model * i // 4 for i in range(5))
    shard = (1, tokens + SUM_ROWS, width)
    params = lambda mib: pltpu.CompilerParams(vmem_limit_bytes=mib * 2**20)

    payload, query, qkv = pl.pallas_call(
        functools.partial(project_kernel, **sizes, rank=rank, log_factor=log_factor, cuts=cuts),
        in_specs=[HBM] * 8,
        out_specs=[VMEM] * 3,
        out_shape=[
            jax.ShapeDtypeStruct(shard, bf16),
            jax.ShapeDtypeStruct((tokens, width), bf16),
            jax.ShapeDtypeStruct((rows, 3 * width), f32),
        ],
        scratch_shapes=[
            pltpu.VMEM((rows, model), bf16),
            pltpu.VMEM((model, 3 * width), bf16),
            pltpu.VMEM((3 * heads, dim), f32),
            pltpu.VMEM((1, dim), f32),
            pltpu.VMEM((1, dim), f32),
            pltpu.VMEM((heads, rank, dim), f32),
            pltpu.VMEM((heads, rank, dim), f32),
            pltpu.VMEM((samples, heads, 2, dim), f32),
            pltpu.VMEM((rows, 3 * width), f32),
            pltpu.VMEM((2 * dim, width + dim), bf16),
            pltpu.VMEM((dim, width - dim), bf16),
            pltpu.VMEM((SUM_ROWS, dim), f32),
            pltpu.SemaphoreType.DMA((2, len(cuts) - 1)),
            pltpu.SemaphoreType.DMA((6,)),
        ],
        compiler_params=params(32),
        name="project",
    )(
        *(
            pltpu.with_memory_space_constraint(x, pltpu.HBM)
            for x in (
                flat, w_qkv, b_qkv.reshape(3 * heads, dim), q_gain.reshape(1, -1),
                k_gain.reshape(1, -1), key_rows, value_rows, center_rows,
            )
        )
    )

    def swap(x, mask):
        return lax.ppermute(x, "seq", [(i, i ^ mask) for i in range(seq)])

    far_mask = seq // 2
    bits = [m for m in (2**i for i in range(1, seq.bit_length() - 1)) if m < far_mask]
    held = [(payload, [0])]
    direct = sum(bits[:2])
    for mask in range(2, 2 * direct, 2):
        if mask & ~direct == 0:
            held.append((swap(payload, mask), [mask]))
    for bit in bits[2:]:
        block = jnp.concatenate([a for a, _ in held], axis=0)
        names = [m for _, ms in held for m in ms]
        held.append((swap(block, bit), [m ^ bit for m in names]))

    query_far = swap(query, far_mask)

    near, rel, basis_high, basis_low, old = pl.pallas_call(
        functools.partial(near_kernel, **sizes, rank=rank),
        in_specs=[VMEM, VMEM, pl.BlockSpec(memory_space=pltpu.SMEM), VMEM],
        out_specs=[VMEM] * 5,
        out_shape=[
            jax.ShapeDtypeStruct((rows, width), f32),
            jax.ShapeDtypeStruct((rows, width), f32),
            jax.ShapeDtypeStruct((samples, dim, width), bf16),
            jax.ShapeDtypeStruct((samples, dim, width), bf16),
            jax.ShapeDtypeStruct((2 * SUM_ROWS, dim), f32),
        ],
        compiler_params=params(24),
        cost_estimate=pl.CostEstimate(
            flops=1200 * rows * tokens * width, bytes_accessed=50 * rows * width * 4, transcendentals=0
        ),
        name="near",
    )(qkv, center_rows, refresh, value_rows)

    for i in (1,):
        x, _ = lax.optimization_barrier((held[i][0], rel))
        held[i] = (x, held[i][1])
    early = [a for a, _ in held]
    held += [(swap(a, 1), [m ^ 1 for m in ms]) for a, ms in held]
    arrays = [a for a, _ in held]
    names = [m for _, ms in held for m in ms]
    order = tuple(names.index(m) for m in range(len(names)))
    count_early = sum(a.shape[0] for a in early)

    def cost(shards):
        return pl.CostEstimate(
            flops=8 * rows * tokens * shards * width,
            bytes_accessed=shards * 2 * tokens * width,
            transcendentals=0,
        )

    part, part_log = pl.pallas_call(
        functools.partial(early_kernel, **sizes, rank=rank),
        in_specs=[VMEM] * (1 + len(early)),
        out_specs=[VMEM] * 2,
        out_shape=[jax.ShapeDtypeStruct((rows, dim), f32)] * 2,
        compiler_params=params(32),
        cost_estimate=cost(count_early),
        name="early",
    )(query_far, *early)
    back, half = pl.pallas_call(
        functools.partial(
            partner_kernel, **sizes, rank=rank, order=order, late=len(names) - count_early
        ),
        in_specs=[VMEM] * (3 + len(arrays)),
        out_specs=[VMEM] * 2,
        out_shape=[
            jax.ShapeDtypeStruct((rows, dim), bf16),
            jax.ShapeDtypeStruct((SUM_ROWS, dim), f32),
        ],
        compiler_params=params(32),
        cost_estimate=cost(len(names)),
        name="partner",
    )(query_far, part, part_log, *arrays)
    returned = swap(back, far_mask)
    merged, logs = pl.pallas_call(
        functools.partial(own_kernel, **sizes, rank=rank),
        in_specs=[VMEM] * (5 + len(arrays)),
        out_specs=[VMEM] * 2,
        out_shape=[
            jax.ShapeDtypeStruct((rows, width), f32),
            jax.ShapeDtypeStruct((rows, dim), f32),
        ],
        compiler_params=params(32),
        cost_estimate=cost(len(names)),
        name="own",
    )(query, near, rel, old, basis_high, basis_low, *arrays[1:])

    columns = 512
    mixed, new_centers = pl.pallas_call(
        functools.partial(finish_kernel, **sizes, rank=rank, length=tokens * seq),
        in_specs=[VMEM] * 8,
        out_specs=[HBM, HBM],
        out_shape=[
            jax.ShapeDtypeStruct((rows, model), bf16),
            jax.ShapeDtypeStruct((samples, heads, 2, dim), f32),
        ],
        scratch_shapes=[
            pltpu.VMEM((rows, width), bf16),
            pltpu.VMEM((model // columns, rows, columns), bf16),
            pltpu.VMEM((samples, heads, 2, dim), f32),
            pltpu.SemaphoreType.DMA((model // columns,)),
            pltpu.SemaphoreType.DMA((1,)),
        ],
        compiler_params=params(24),
        name="finish",
    )(returned, half, merged, logs, old, basis_high, basis_low, w_out)
    return (mixed.reshape(samples, tokens, model), new_centers.transpose(0, 2, 1, 3))


def solution(mesh):
    return jax.shard_map(
        per_device,
        mesh=mesh,
        in_specs=(
            P("groups", "seq", None),
            P(),
            P(),
            P(),
            P(),
            P(),
            P(),
            P("groups", None, None, None),
            P(),
            P(),
        ),
        out_specs=(P("groups", "seq", None), P("groups", None, None, None)),
        check_vma=False,
    )
```

```python
import functools
import math

import jax
import jax.numpy as jnp
from jax import lax
from jax.experimental import pallas as pl
from jax.experimental.pallas import tpu as pltpu
from jax.sharding import PartitionSpec as P

epsilon = 1e-06
log2_e = math.log2(math.e)
f32 = jnp.float32
bf16 = jnp.bfloat16
SUM_ROWS = 8
EXTRA_ROWS = 16
NT = (((1,), (1,)), ((), ()))
NN = (((1,), (0,)), ((), ()))


def dot(a, b, dims=NN):
    return lax.dot_general(a, b, dims, preferred_element_type=f32)


def split(x):
    high = x.astype(bf16)
    low = (x - high.astype(f32)).astype(bf16)
    return high, low


def dot3(a, b, dims=NN):
    return dot(a[0], b[0], dims) + (dot(a[0], b[1], dims) + dot(a[1], b[0], dims))


def pieces_of(x, count):
    out = []
    for _ in range(count):
        top = x.astype(bf16)
        out.append(top)
        x = x - top.astype(f32)
    return out


def lane_ids(rows, lanes):
    return lax.broadcasted_iota(jnp.int32, (rows, lanes), 1)


def key_lane(sample, head, rank):
    return head * rank if sample == 0 else (head + 1) * rank


def value_lane(sample, head, rank, heads):
    if head == 0:
        return heads * rank if sample == 0 else 0
    return ((heads - 1) * sample + head - 1) * rank


def free_lane(sample, rank):
    return 2 * rank if sample == 0 else rank


def log_lane(sample, head, piece, rank):
    return free_lane(sample, rank) + 8 * piece + head


def return_lane(head, rank, heads):
    return {heads - 1: 0, 0: rank, 1: 2 * rank}[head]


def center_row(sample, head, kind):
    return head * SUM_ROWS + sample * 2 + kind


def within(lanes, start, count):
    return (lanes >= start) & (lanes < start + count)


def fill_basis(basis_h, basis_l, vb_ref, samples, heads, dim, rank):
    basis_h[...] = jnp.zeros_like(basis_h)
    basis_l[...] = jnp.zeros_like(basis_l)
    for h in range(heads):
        vh, vl = split(vb_ref[h])
        for b in range(samples):
            at = value_lane(b, h, rank, heads)
            basis_h[b, at : at + rank, h * dim : (h + 1) * dim] = vh
            basis_l[b, at : at + rank, h * dim : (h + 1) * dim] = vl
        at = return_lane(h, rank, heads)
        basis_h[samples, at : at + rank, h * dim : (h + 1) * dim] = vh
        basis_l[samples, at : at + rank, h * dim : (h + 1) * dim] = vl


def project_kernel(
    images_hbm, w_hbm, b_hbm, qg_hbm, kg_hbm, kb_hbm, vb_hbm, centers_hbm,
    payload_ref, query_ref, qkv_ref,
    x_ref, w_ref, b_ref, qg_ref, kg_ref, kb_ref, vb_ref, centers_ref,
    acc_ref, main_ref, tail_ref, sums_ref, big_sem, small_sem,
    *, samples, tokens, heads, dim, rank, log_factor, cuts,
):
    width = heads * dim
    places = [slice(first, last) for first, last in zip(cuts[:-1], cuts[1:])]

    def x_copy(c):
        p = places[c]
        return pltpu.make_async_copy(images_hbm.at[:, p], x_ref.at[:, p], big_sem.at[0, c])

    def w_copy(c):
        p = places[c]
        return pltpu.make_async_copy(w_hbm.at[p, :], w_ref.at[p, :], big_sem.at[1, c])

    small = [
        pltpu.make_async_copy(source, target, small_sem.at[i])
        for i, (source, target) in enumerate(
            [
                (kb_hbm, kb_ref), (vb_hbm, vb_ref), (b_hbm, b_ref),
                (qg_hbm, qg_ref), (kg_hbm, kg_ref), (centers_hbm, centers_ref),
            ]
        )
    ]
    for copy in small:
        copy.start()
    for c in range(len(places)):
        w_copy(c).start()
        x_copy(c).start()
    main_ref[...] = jnp.zeros_like(main_ref)
    tail_ref[...] = jnp.zeros_like(tail_ref)
    half = dim // 2

    def build():
        for copy in small:
            copy.wait()
        for h in range(heads):
            for p, (k, v) in enumerate(zip(split(kb_ref[h]), split(vb_ref[h]))):
                at = p * dim + key_lane(0, h, rank)
                main_ref[at : at + rank, h * dim : (h + 1) * dim] = k
                at = value_lane(0, h, rank, heads)
                if h == 0:
                    main_ref[p * dim + at : p * dim + at + rank, width:] = v
                else:
                    at = p * half + at
                    tail_ref[at : at + rank, (h - 1) * dim : h * dim] = v

    for c, place in enumerate(places):
        if c == len(places) - 1:
            build()
        x_copy(c).wait()
        w_copy(c).wait()
        part = dot(x_ref[:, place], w_ref[place, :])
        if c == 0:
            acc_ref[...] = part
        else:
            acc_ref[...] += part

    def column(at):
        return acc_ref[:, at * dim : (at + 1) * dim] + b_ref[at : at + 1, :]

    def normed(at, gain):
        x = column(at)
        mean_square = jnp.mean(x * x, axis=-1, keepdims=True)
        return x * lax.rsqrt(mean_square + epsilon) * gain

    queries, keys, values = [], [], []
    for h in range(heads):
        q = normed(h, qg_ref[...])
        k = normed(heads + h, kg_ref[...])
        v = column(2 * heads + h)
        queries.append(q)
        keys.append(k)
        values.append(v)
        for b in range(samples):
            rows = slice(b * tokens, (b + 1) * tokens)
            for row, x in enumerate((k, v)):
                total = jnp.sum(x[rows], axis=0, keepdims=True)
                for again in range(2):
                    at = again * 4 + b * 2 + row
                    sums_ref[at : at + 1, h * dim : (h + 1) * dim] = total
    total = sums_ref[...]
    top = total.astype(bf16).astype(f32)
    first = lax.broadcasted_iota(jnp.int32, total.shape, 0) < 4
    total = jnp.where(first, top, total - top)
    empty = jnp.zeros((EXTRA_ROWS - SUM_ROWS, width), f32)
    payload_ref[0, tokens:, :] = jnp.concatenate([total, empty], axis=0).astype(bf16)
    def by_sample(j):
        rows = [centers_ref[b, h, j : j + 1, :] for b in range(samples) for h in range(heads)]
        return [
            jnp.concatenate(
                [jnp.broadcast_to(rows[b * heads + h], (tokens, dim)) for b in range(samples)], axis=0
            )
            for h in range(heads)
        ]

    key_centers, value_centers = by_sample(0), by_sample(1)
    shifted = [keys[h] - key_centers[h] for h in range(heads)]
    shifted += [values[h] - value_centers[h] for h in range(heads)]

    def coded(x, columns):
        high, low = split(x)
        both = dot(high, main_ref[:, columns], NT)
        return both[:, :dim] + (both[:, dim:] + dot(low, main_ref[:dim, columns], NT))

    code = coded(jnp.concatenate(shifted[: heads + 1], axis=1), slice(0, width + dim))
    query_code = coded(jnp.concatenate(queries, axis=1), slice(0, width)) * log_factor
    high, low = split(jnp.concatenate(shifted[heads + 1 :], axis=1))
    both = dot(high, tail_ref[...], NT)
    tail = both + pltpu.roll(both, half, 1) + dot(low, tail_ref[...], NT)
    payload_ref[0, :tokens, :dim] = code[:tokens].astype(bf16)
    payload_ref[0, :tokens, dim : 2 * dim] = pltpu.roll(code[tokens:], rank, 1).astype(bf16)
    lanes = lane_ids(tokens, dim)
    last = jnp.where(lanes < half, tail[:tokens], pltpu.roll(tail[tokens:], half, 1))
    payload_ref[0, :tokens, samples * dim :] = last.astype(bf16)
    high_0 = query_code[:tokens].astype(bf16).astype(f32)
    low_0 = query_code[:tokens] - high_0
    query_1 = pltpu.roll(query_code[tokens:], rank, 1)
    high_1 = query_1.astype(bf16).astype(f32)
    low_1 = query_1 - high_1
    turned = pltpu.roll(low_1, half, 1)
    query_ref[:, :dim] = jnp.where(lanes < heads * rank, high_0, turned).astype(bf16)
    query_ref[:, dim : 2 * dim] = jnp.where(lanes < rank, turned, high_1).astype(bf16)
    query_ref[:, 2 * dim :] = jnp.where(lanes < heads * rank, low_0, low_1).astype(bf16)
    for h in range(heads):
        qkv_ref[:, h * dim : (h + 1) * dim] = queries[h] * log_factor
        qkv_ref[:, width + h * dim : width + (h + 1) * dim] = keys[h]
        qkv_ref[:, 2 * width + h * dim : 2 * width + (h + 1) * dim] = values[h]


def near_kernel(
    qkv_ref, centers_ref, refresh_ref, vb_ref, near_ref, rel_ref, basis_h, basis_l, old_ref,
    *, samples, tokens, heads, dim, rank,
):
    width = heads * dim
    fill_basis(basis_h, basis_l, vb_ref, samples, heads, dim, rank)
    old_ref[...] = jnp.zeros_like(old_ref)
    for b in range(samples):
        for h in range(heads):
            for j in range(2):
                row = center_row(b, h, j)
                keep = jnp.where(refresh_ref[j, h] == 1, 0.0, 1.0)
                old_ref[row : row + 1, :] = centers_ref[b, h, j : j + 1, :]
                row += heads * SUM_ROWS
                old_ref[row : row + 1, :] = jnp.full((1, dim), keep, f32)
    for b in range(samples):
        rows = slice(b * tokens, (b + 1) * tokens)
        for h in range(heads):
            head = slice(h * dim, (h + 1) * dim)
            q = qkv_ref[rows, head]
            k = split(qkv_ref[rows, width + h * dim : width + (h + 1) * dim])
            v = split(qkv_ref[rows, 2 * width + h * dim : 2 * width + (h + 1) * dim])
            scores = dot3(split(q), k, NT)
            row_max = jnp.max(scores, axis=-1, keepdims=True)
            weights = jnp.exp2(scores - row_max)
            row_sum = jnp.sum(weights, axis=-1, keepdims=True)
            near_ref[rows, head] = dot3(split(weights), v) / row_sum
            center = jnp.sum(q * centers_ref[b, h, 0:1, :], axis=-1, keepdims=True)
            rel = row_max + jnp.log(row_sum) * log2_e - center
            rel_ref[rows, head] = jnp.broadcast_to(rel, (tokens, dim))


def query_parts(query_ref, sample, heads, dim, rank):
    lanes = lane_ids(query_ref.shape[0], dim)
    if sample == 0:
        return query_ref[:, :dim].astype(f32), query_ref[:, 2 * dim :].astype(f32)
    first, second = query_ref[:, :dim].astype(f32), query_ref[:, dim : 2 * dim].astype(f32)
    turned = pltpu.roll(jnp.where(lanes < rank, second, first), dim // 2, 1)
    return second, jnp.where(lanes < heads * rank, turned, query_ref[:, 2 * dim :].astype(f32))


def code_attention(query_ref, tiles, *, samples, tokens, heads, dim, rank):
    lanes = lane_ids(tokens, dim)
    scores, values = [], []
    for b in range(samples):
        high, low = query_parts(query_ref, b, heads, dim, rank)
        stacked = []
        for h in range(heads):
            own = within(lanes, key_lane(b, h, rank), rank)
            both = [jnp.where(own, part, 0.0).astype(bf16) for part in (high, low)]
            stacked.append(jnp.concatenate(both, axis=1))
        left = jnp.concatenate(stacked, axis=0)
        codes = [ref[i, :tokens, b * dim : (b + 1) * dim] for ref, i in tiles]
        values.append(jnp.concatenate(codes, axis=0))
        parts = []
        for i in range(0, len(codes), 2):
            some = jnp.concatenate(codes[i : i + 2], axis=0)
            both = dot(left, jnp.concatenate([some, some], axis=1), NT)
            parts += [both[:, j * tokens : (j + 1) * tokens] for j in range(len(codes[i : i + 2]))]
        scores.append(parts)
    rest = jnp.concatenate([ref[i, :tokens, samples * dim :] for ref, i in tiles], axis=0)
    weights, scales, logs = [], [], []
    for b in range(samples):
        best = scores[b][0]
        for part in scores[b][1:]:
            best = jnp.maximum(best, part)
        row_max = jnp.max(best, axis=-1, keepdims=True)
        total = jnp.zeros_like(best)
        parts = []
        for part in scores[b]:
            weight = jnp.exp2(part - row_max).astype(bf16)
            total = total + weight.astype(f32)
            parts.append(weight)
        row_sum = jnp.sum(total, axis=-1, keepdims=True)
        weights.append(jnp.concatenate(parts, axis=1))
        scales.append(1.0 / row_sum)
        log = row_max + jnp.log(row_sum) * log2_e
        logs.append([log[h * tokens : (h + 1) * tokens] for h in range(heads)])
    outs = []
    for b in range(samples):
        results = [dot(weights[b][:tokens], values[b])]
        others = dot(weights[b][tokens:], rest)
        results += [others[h * tokens : (h + 1) * tokens] for h in range(heads - 1)]
        out = jnp.zeros((tokens, dim), f32)
        for h in range(heads):
            part = results[h] * scales[b][h * tokens : (h + 1) * tokens]
            out = jnp.where(within(lanes, value_lane(b, h, rank, heads), rank), part, out)
        outs.append(out)
    return outs, logs


def spread(b, logs, tokens, heads, dim, rank):
    lanes = lane_ids(tokens, dim)
    out = jnp.zeros((tokens, dim), f32)
    for h in range(heads):
        place = within(lanes, value_lane(b, h, rank, heads), rank)
        for p in range(3):
            place = place | (lanes == log_lane(b, h, p, rank))
        out = jnp.where(place, logs[h], out)
    return out


def tree_sum(parts):
    while len(parts) > 1:
        parts = [parts[i] + parts[i + 1] for i in range(0, len(parts), 2)]
    return parts[0]


def tiles_of(refs):
    return [(ref, i) for ref in refs for i in range(ref.shape[0])]


def early_kernel(query_ref, *refs, samples, tokens, heads, dim, rank):
    out_ref, log_ref = refs[-2:]
    tiles = tiles_of(refs[:-2])
    lanes = lane_ids(tokens, dim)
    outs, all_logs = code_attention(
        query_ref, tiles, samples=samples, tokens=tokens, heads=heads, dim=dim, rank=rank
    )
    for b in range(samples):
        rows = slice(b * tokens, (b + 1) * tokens)
        out, logs = outs[b], all_logs[b]
        out_ref[rows, :] = out
        log_ref[rows, :] = spread(b, logs, tokens, heads, dim, rank)


def partner_kernel(
    query_ref, part_ref, part_log_ref, *refs, order, late, samples, tokens, heads, dim, rank
):
    out_ref, half_ref = refs[-2:]
    tiles = tiles_of(refs[:-2])
    end = tokens + SUM_ROWS
    parts = [tiles[place][0][tiles[place][1], tokens:end, :].astype(f32) for place in order]
    total = tree_sum(parts)
    total = total + pltpu.roll(total, 4, 0)
    total = jnp.concatenate([total[:, h * dim : (h + 1) * dim] for h in range(heads)], axis=0)
    top = total.astype(bf16).astype(f32)
    rest = (total - top).astype(bf16).astype(f32)
    half_ref[...] = top + rest
    in_eight = lax.broadcasted_iota(jnp.int32, total.shape, 0) % SUM_ROWS
    sums = jnp.where(in_eight < 4, top, rest)
    lanes = lane_ids(tokens, dim)
    outs, all_logs = code_attention(
        query_ref, tiles[-late:], samples=samples, tokens=tokens, heads=heads, dim=dim, rank=rank
    )
    kept = []
    for b in range(samples):
        rows = slice(b * tokens, (b + 1) * tokens)
        before, before_log = part_ref[rows, :], part_log_ref[rows, :]
        log = spread(b, all_logs[b], tokens, heads, dim, rank)
        top = jnp.maximum(log, before_log)
        new = jnp.exp2(log - top)
        whole = new + jnp.exp2(before_log - top)
        outs[b] = before + (outs[b] - before) * (new / whole)
        log = top + jnp.log(whole) * log2_e
        tile = jnp.zeros_like(log)
        for p, piece in enumerate(pieces_of(log, 3)):
            place = within(lanes, log_lane(b, 0, p, rank), heads)
            tile = jnp.where(place, piece.astype(f32), tile)
        kept.append(tile)
    first = free_lane(0, rank)
    out_ref[:tokens, :] = jnp.where(within(lanes, first, rank), outs[1], outs[0]).astype(bf16)
    folded = pltpu.roll(outs[1], rank, 1)
    middle = tokens // 2
    back = pltpu.roll(folded[middle:], dim // 2, 1)
    folded = jnp.where(lanes[:middle] < dim // 2, folded[:middle], back)
    out_ref[tokens : tokens + middle, :] = folded.astype(bf16)
    logs = kept[0] + pltpu.roll(kept[1], first + 4 - free_lane(1, rank), 1)
    logs = logs.T[first : first + 3 * SUM_ROWS, :]
    out_ref[tokens + middle :, :] = jnp.concatenate([logs, sums], axis=0).astype(bf16)


def own_kernel(
    query_ref, near_ref, rel_ref, old_ref, basis_h, basis_l, *refs,
    samples, tokens, heads, dim, rank,
):
    merged_ref, log_ref = refs[-2:]
    tiles = tiles_of(refs[:-2])
    lanes = lane_ids(tokens, dim)
    kept = jnp.zeros((tokens, dim), f32)
    outs, all_logs = code_attention(
        query_ref, tiles, samples=samples, tokens=tokens, heads=heads, dim=dim, rank=rank
    )
    for b in range(samples):
        rows = slice(b * tokens, (b + 1) * tokens)
        out, logs = outs[b], all_logs[b]
        far = dot3(split(out), (basis_h[b], basis_l[b]))
        for h in range(heads):
            columns = slice(h * dim, (h + 1) * dim)
            near, rel = near_ref[rows, columns], rel_ref[rows, columns]
            top = jnp.maximum(rel, logs[h])
            far_part = jnp.exp2(logs[h] - top)
            whole = jnp.exp2(rel - top) + far_part
            row = center_row(b, h, 1)
            value = far[:, columns] + old_ref[row : row + 1, :] - near
            merged_ref[rows, columns] = near + value * (far_part / whole)
            log = top + jnp.log(whole) * log2_e
            kept = jnp.where(lanes == 4 * b + h, log, kept)
    log_ref[...] = kept


def finish_kernel(
    back_ref, half_ref, merged_ref, log_ref, old_ref, basis_h, basis_l, w_ref,
    mixed_hbm, new_hbm, attended_ref, mixed_ref, new_ref, sem, new_sem,
    *, samples, tokens, heads, dim, rank, length,
):
    chunks, columns = mixed_ref.shape[0], mixed_ref.shape[2]
    copies = []
    middle = tokens // 2
    count = heads * SUM_ROWS
    lanes = lane_ids(tokens, dim)
    extra = back_ref[tokens + middle :, :].astype(f32)
    empty = jnp.zeros((tokens - 3 * SUM_ROWS, dim), f32)
    far_log = jnp.concatenate([extra[: 3 * SUM_ROWS], empty], axis=0).T
    far_log = far_log + (pltpu.roll(far_log, dim - 8, 1) + pltpu.roll(far_log, dim - 16, 1))
    share = 1.0 / (1.0 + jnp.exp2(log_ref[...] - far_log))
    straight = back_ref[:tokens, :]
    folded = back_ref[tokens : tokens + middle, :].astype(f32)
    folded = jnp.concatenate([folded, pltpu.roll(folded, dim // 2, 1)], axis=0)
    own_lanes = within(lanes, free_lane(0, rank), rank)
    second = jnp.where(own_lanes, straight.astype(f32), folded).astype(bf16)
    for b, (codes, place) in enumerate(((straight, 0), (second, samples))):
        rows = slice(b * tokens, (b + 1) * tokens)
        far = dot(codes, basis_h[place]) + dot(codes, basis_l[place])
        for h in range(heads):
            head = slice(h * dim, (h + 1) * dim)
            at = 4 * b + h
            row = center_row(b, h, 1)
            near = merged_ref[rows, head]
            value = far[:, head] + old_ref[row : row + 1, :] - near
            attended_ref[rows, head] = (near + value * share[:, at : at + 1]).astype(bf16)
    for c in range(chunks):
        place = slice(c * columns, (c + 1) * columns)
        mixed_ref[c] = dot(attended_ref[...], w_ref[:, place]).astype(bf16)
        copies.append(pltpu.make_async_copy(mixed_ref.at[c], mixed_hbm.at[:, place], sem.at[c]))
        copies[-1].start()
        if c == 1:
            sums = extra[3 * SUM_ROWS :]
            sums = sums + pltpu.roll(sums, 4, 0)
            fresh = (half_ref[...] + sums) * (1.0 / length)
            fresh = jnp.where(old_ref[count:, :] > 0.5, old_ref[:count, :], fresh)
            for b in range(samples):
                for h in range(heads):
                    row = center_row(b, h, 0)
                    new_ref[b, h] = fresh[row : row + 2, :]
            copies.append(pltpu.make_async_copy(new_ref, new_hbm, new_sem.at[0]))
            copies[-1].start()
    for copy in copies:
        copy.wait()


VMEM = pl.BlockSpec(memory_space=pltpu.VMEM)
HBM = pl.BlockSpec(memory_space=pltpu.HBM)


def per_device(
    images, w_qkv, b_qkv, q_gain, k_gain, key_basis, value_basis, centers, refresh, w_out
):
    samples, tokens, model = images.shape
    heads, dim, rank = key_basis.shape
    seq = lax.axis_size("seq")
    rows = samples * tokens
    width = heads * dim
    sizes = dict(samples=samples, tokens=tokens, heads=heads, dim=dim)
    log_factor = log2_e / math.sqrt(dim)
    flat = images.reshape(rows, model)
    key_rows = key_basis.transpose(0, 2, 1)
    value_rows = value_basis.transpose(0, 2, 1)
    center_rows = centers.transpose(0, 2, 1, 3)
    cuts = tuple(model * i // 4 for i in range(5))
    shard = (1, tokens + EXTRA_ROWS, width)
    params = lambda mib: pltpu.CompilerParams(vmem_limit_bytes=mib * 2**20)

    payload, query, qkv = pl.pallas_call(
        functools.partial(project_kernel, **sizes, rank=rank, log_factor=log_factor, cuts=cuts),
        in_specs=[HBM] * 8,
        out_specs=[VMEM] * 3,
        out_shape=[
            jax.ShapeDtypeStruct(shard, bf16),
            jax.ShapeDtypeStruct((tokens, width), bf16),
            jax.ShapeDtypeStruct((rows, 3 * width), f32),
        ],
        scratch_shapes=[
            pltpu.VMEM((rows, model), bf16),
            pltpu.VMEM((model, 3 * width), bf16),
            pltpu.VMEM((3 * heads, dim), f32),
            pltpu.VMEM((1, dim), f32),
            pltpu.VMEM((1, dim), f32),
            pltpu.VMEM((heads, rank, dim), f32),
            pltpu.VMEM((heads, rank, dim), f32),
            pltpu.VMEM((samples, heads, 2, dim), f32),
            pltpu.VMEM((rows, 3 * width), f32),
            pltpu.VMEM((2 * dim, width + dim), bf16),
            pltpu.VMEM((dim, width - dim), bf16),
            pltpu.VMEM((SUM_ROWS, width), f32),
            pltpu.SemaphoreType.DMA((2, len(cuts) - 1)),
            pltpu.SemaphoreType.DMA((6,)),
        ],
        compiler_params=params(32),
        name="project",
    )(
        *(
            pltpu.with_memory_space_constraint(x, pltpu.HBM)
            for x in (
                flat, w_qkv, b_qkv.reshape(3 * heads, dim), q_gain.reshape(1, -1),
                k_gain.reshape(1, -1), key_rows, value_rows, center_rows,
            )
        )
    )

    def swap(x, mask):
        return lax.ppermute(x, "seq", [(i, i ^ mask) for i in range(seq)])

    far_mask = seq // 2
    bits = [m for m in (2**i for i in range(1, seq.bit_length() - 1)) if m < far_mask]
    held = [(payload, [0])]
    direct = sum(bits[:2])
    for mask in range(2, 2 * direct, 2):
        if mask & ~direct == 0:
            held.append((swap(payload, mask), [mask]))
    for bit in bits[2:]:
        block = jnp.concatenate([a for a, _ in held], axis=0)
        names = [m for _, ms in held for m in ms]
        held.append((swap(block, bit), [m ^ bit for m in names]))

    query_far = swap(query, far_mask)

    near, rel, basis_high, basis_low, old = pl.pallas_call(
        functools.partial(near_kernel, **sizes, rank=rank),
        in_specs=[VMEM, VMEM, pl.BlockSpec(memory_space=pltpu.SMEM), VMEM],
        out_specs=[VMEM] * 5,
        out_shape=[
            jax.ShapeDtypeStruct((rows, width), f32),
            jax.ShapeDtypeStruct((rows, width), f32),
            jax.ShapeDtypeStruct((samples + 1, dim, width), bf16),
            jax.ShapeDtypeStruct((samples + 1, dim, width), bf16),
            jax.ShapeDtypeStruct((2 * heads * SUM_ROWS, dim), f32),
        ],
        compiler_params=params(24),
        cost_estimate=pl.CostEstimate(
            flops=1200 * rows * tokens * width, bytes_accessed=50 * rows * width * 4, transcendentals=0
        ),
        name="near",
    )(qkv, center_rows, refresh, value_rows)

    for i in (1,):
        x, _ = lax.optimization_barrier((held[i][0], rel))
        held[i] = (x, held[i][1])
    early = [a for a, _ in held]
    held += [(swap(a, 1), [m ^ 1 for m in ms]) for a, ms in held]
    arrays = [a for a, _ in held]
    names = [m for _, ms in held for m in ms]
    order = tuple(names.index(m) for m in range(len(names)))
    count_early = sum(a.shape[0] for a in early)

    def cost(shards):
        return pl.CostEstimate(
            flops=8 * rows * tokens * shards * width,
            bytes_accessed=shards * 2 * tokens * width,
            transcendentals=0,
        )

    part, part_log = pl.pallas_call(
        functools.partial(early_kernel, **sizes, rank=rank),
        in_specs=[VMEM] * (1 + len(early)),
        out_specs=[VMEM] * 2,
        out_shape=[jax.ShapeDtypeStruct((rows, dim), f32)] * 2,
        compiler_params=params(32),
        cost_estimate=cost(count_early),
        name="early",
    )(query_far, *early)
    back, half = pl.pallas_call(
        functools.partial(
            partner_kernel, **sizes, rank=rank, order=order, late=len(names) - count_early
        ),
        in_specs=[VMEM] * (3 + len(arrays)),
        out_specs=[VMEM] * 2,
        out_shape=[
            jax.ShapeDtypeStruct((tokens + tokens // 2 + (3 + heads) * SUM_ROWS, dim), bf16),
            jax.ShapeDtypeStruct((heads * SUM_ROWS, dim), f32),
        ],
        compiler_params=params(32),
        cost_estimate=cost(len(names)),
        name="partner",
    )(query_far, part, part_log, *arrays)
    returned = swap(back, far_mask)
    merged, logs = pl.pallas_call(
        functools.partial(own_kernel, **sizes, rank=rank),
        in_specs=[VMEM] * (5 + len(arrays)),
        out_specs=[VMEM] * 2,
        out_shape=[
            jax.ShapeDtypeStruct((rows, width), f32),
            jax.ShapeDtypeStruct((tokens, dim), f32),
        ],
        compiler_params=params(32),
        cost_estimate=cost(len(names)),
        name="own",
    )(query, near, rel, old, basis_high, basis_low, *arrays[1:])

    columns = 512
    mixed, new_centers = pl.pallas_call(
        functools.partial(finish_kernel, **sizes, rank=rank, length=tokens * seq),
        in_specs=[VMEM] * 8,
        out_specs=[HBM, HBM],
        out_shape=[
            jax.ShapeDtypeStruct((rows, model), bf16),
            jax.ShapeDtypeStruct((samples, heads, 2, dim), f32),
        ],
        scratch_shapes=[
            pltpu.VMEM((rows, width), bf16),
            pltpu.VMEM((model // columns, rows, columns), bf16),
            pltpu.VMEM((samples, heads, 2, dim), f32),
            pltpu.SemaphoreType.DMA((model // columns,)),
            pltpu.SemaphoreType.DMA((1,)),
        ],
        compiler_params=params(24),
        name="finish",
    )(returned, half, merged, logs, old, basis_high, basis_low, w_out)
    return (mixed.reshape(samples, tokens, model), new_centers.transpose(0, 2, 1, 3))


def solution(mesh):
    return jax.shard_map(
        per_device,
        mesh=mesh,
        in_specs=(
            P("groups", "seq", None),
            P(),
            P(),
            P(),
            P(),
            P(),
            P(),
            P("groups", None, None, None),
            P(),
            P(),
        ),
        out_specs=(P("groups", "seq", None), P("groups", None, None, None)),
        check_vma=False,
    )
```

```python
import functools
import math

import jax
import jax.numpy as jnp
from jax import lax
from jax.experimental import pallas as pl
from jax.experimental.pallas import tpu as pltpu
from jax.sharding import PartitionSpec as P

epsilon = 1e-06
log2_e = math.log2(math.e)
f32 = jnp.float32
bf16 = jnp.bfloat16
SUM_ROWS = 16
NT = (((1,), (1,)), ((), ()))
NN = (((1,), (0,)), ((), ()))


def dot(a, b, dims=NN):
    return lax.dot_general(a, b, dims, preferred_element_type=f32)


def split(x):
    high = x.astype(bf16)
    low = (x - high.astype(f32)).astype(bf16)
    return high, low


def dot3(a, b, dims=NN):
    return dot(a[0], b[0], dims) + (dot(a[0], b[1], dims) + dot(a[1], b[0], dims))


def pieces_of(x, count):
    out = []
    for _ in range(count):
        top = x.astype(bf16)
        out.append(top)
        x = x - top.astype(f32)
    return out


def lane_ids(rows, lanes):
    return lax.broadcasted_iota(jnp.int32, (rows, lanes), 1)


def key_lane(sample, head, rank):
    return head * rank if sample == 0 else (head + 1) * rank


def value_lane(sample, head, rank, heads):
    if head == 0:
        return heads * rank if sample == 0 else 0
    return ((heads - 1) * sample + head - 1) * rank


def free_lane(sample, rank):
    return 2 * rank if sample == 0 else rank


def log_lane(sample, head, piece, rank):
    return free_lane(sample, rank) + 8 * piece + head


def sum_lane(sample, rank):
    return free_lane(sample, rank) + 20


def within(lanes, start, count):
    return (lanes >= start) & (lanes < start + count)


def fill_basis(basis_h, basis_l, vb_ref, samples, heads, dim, rank):
    basis_h[...] = jnp.zeros_like(basis_h)
    basis_l[...] = jnp.zeros_like(basis_l)
    for h in range(heads):
        vh, vl = split(vb_ref[h])
        for b in range(samples):
            at = value_lane(b, h, rank, heads)
            basis_h[b, at : at + rank, h * dim : (h + 1) * dim] = vh
            basis_l[b, at : at + rank, h * dim : (h + 1) * dim] = vl


def project_kernel(
    images_hbm, w_hbm, b_hbm, qg_hbm, kg_hbm, kb_hbm, vb_hbm, centers_hbm,
    payload_ref, query_ref, qkv_ref,
    x_ref, w_ref, b_ref, qg_ref, kg_ref, kb_ref, vb_ref, centers_ref,
    acc_ref, main_ref, tail_ref, sums_ref, big_sem, small_sem,
    *, samples, tokens, heads, dim, rank, log_factor, cuts,
):
    width = heads * dim
    places = [slice(first, last) for first, last in zip(cuts[:-1], cuts[1:])]

    def x_copy(c):
        p = places[c]
        return pltpu.make_async_copy(images_hbm.at[:, p], x_ref.at[:, p], big_sem.at[0, c])

    def w_copy(c):
        p = places[c]
        return pltpu.make_async_copy(w_hbm.at[p, :], w_ref.at[p, :], big_sem.at[1, c])

    small = [
        pltpu.make_async_copy(source, target, small_sem.at[i])
        for i, (source, target) in enumerate(
            [
                (kb_hbm, kb_ref), (vb_hbm, vb_ref), (b_hbm, b_ref),
                (qg_hbm, qg_ref), (kg_hbm, kg_ref), (centers_hbm, centers_ref),
            ]
        )
    ]
    for copy in small:
        copy.start()
    for c in range(len(places)):
        w_copy(c).start()
        x_copy(c).start()
    main_ref[...] = jnp.zeros_like(main_ref)
    tail_ref[...] = jnp.zeros_like(tail_ref)
    sums_ref[...] = jnp.zeros_like(sums_ref)
    half = dim // 2

    def build():
        for copy in small:
            copy.wait()
        for h in range(heads):
            for p, (k, v) in enumerate(zip(split(kb_ref[h]), split(vb_ref[h]))):
                at = p * dim + key_lane(0, h, rank)
                main_ref[at : at + rank, h * dim : (h + 1) * dim] = k
                at = value_lane(0, h, rank, heads)
                if h == 0:
                    main_ref[p * dim + at : p * dim + at + rank, width:] = v
                else:
                    at = p * half + at
                    tail_ref[at : at + rank, (h - 1) * dim : h * dim] = v

    for c, place in enumerate(places):
        if c == len(places) - 1:
            build()
        x_copy(c).wait()
        w_copy(c).wait()
        part = dot(x_ref[:, place], w_ref[place, :])
        if c == 0:
            acc_ref[...] = part
        else:
            acc_ref[...] += part

    def column(at):
        return acc_ref[:, at * dim : (at + 1) * dim] + b_ref[at : at + 1, :]

    def normed(at, gain):
        x = column(at)
        mean_square = jnp.mean(x * x, axis=-1, keepdims=True)
        return x * lax.rsqrt(mean_square + epsilon) * gain

    queries, keys, values = [], [], []
    for h in range(heads):
        q = normed(h, qg_ref[...])
        k = normed(heads + h, kg_ref[...])
        v = column(2 * heads + h)
        queries.append(q)
        keys.append(k)
        values.append(v)
        for b in range(samples):
            rows = slice(b * tokens, (b + 1) * tokens)
            row = (b * heads + h) * 2
            sums_ref[row : row + 1, :] = jnp.sum(k[rows], axis=0, keepdims=True)
            sums_ref[row + 1 : row + 2, :] = jnp.sum(v[rows], axis=0, keepdims=True)
    for p, piece in enumerate(pieces_of(sums_ref[...], 3)):
        payload_ref[0, tokens : tokens + SUM_ROWS, p * dim : (p + 1) * dim] = piece
    def by_sample(j):
        rows = [centers_ref[b, h, j : j + 1, :] for b in range(samples) for h in range(heads)]
        return [
            jnp.concatenate(
                [jnp.broadcast_to(rows[b * heads + h], (tokens, dim)) for b in range(samples)], axis=0
            )
            for h in range(heads)
        ]

    key_centers, value_centers = by_sample(0), by_sample(1)
    shifted = [keys[h] - key_centers[h] for h in range(heads)]
    shifted += [values[h] - value_centers[h] for h in range(heads)]

    def coded(x, columns):
        high, low = split(x)
        both = dot(high, main_ref[:, columns], NT)
        return both[:, :dim] + (both[:, dim:] + dot(low, main_ref[:dim, columns], NT))

    code = coded(jnp.concatenate(shifted[: heads + 1], axis=1), slice(0, width + dim))
    query_code = coded(jnp.concatenate(queries, axis=1), slice(0, width)) * log_factor
    high, low = split(jnp.concatenate(shifted[heads + 1 :], axis=1))
    both = dot(high, tail_ref[...], NT)
    tail = both + pltpu.roll(both, half, 1) + dot(low, tail_ref[...], NT)
    payload_ref[0, :tokens, :dim] = code[:tokens].astype(bf16)
    payload_ref[0, :tokens, dim : 2 * dim] = pltpu.roll(code[tokens:], rank, 1).astype(bf16)
    lanes = lane_ids(tokens, dim)
    last = jnp.where(lanes < half, tail[:tokens], pltpu.roll(tail[tokens:], half, 1))
    payload_ref[0, :tokens, samples * dim :] = last.astype(bf16)
    high_0 = query_code[:tokens].astype(bf16).astype(f32)
    low_0 = query_code[:tokens] - high_0
    query_1 = pltpu.roll(query_code[tokens:], rank, 1)
    high_1 = query_1.astype(bf16).astype(f32)
    low_1 = query_1 - high_1
    turned = pltpu.roll(low_1, half, 1)
    query_ref[:, :dim] = jnp.where(lanes < heads * rank, high_0, turned).astype(bf16)
    query_ref[:, dim : 2 * dim] = jnp.where(lanes < rank, turned, high_1).astype(bf16)
    query_ref[:, 2 * dim :] = jnp.where(lanes < heads * rank, low_0, low_1).astype(bf16)
    for h in range(heads):
        qkv_ref[:, h * dim : (h + 1) * dim] = queries[h] * log_factor
        qkv_ref[:, width + h * dim : width + (h + 1) * dim] = keys[h]
        qkv_ref[:, 2 * width + h * dim : 2 * width + (h + 1) * dim] = values[h]


def near_kernel(
    qkv_ref, centers_ref, refresh_ref, vb_ref, near_ref, rel_ref, basis_h, basis_l, old_ref,
    *, samples, tokens, heads, dim, rank,
):
    width = heads * dim
    fill_basis(basis_h, basis_l, vb_ref, samples, heads, dim, rank)
    old_ref[...] = jnp.zeros_like(old_ref)
    for b in range(samples):
        for h in range(heads):
            for j in range(2):
                row = (b * heads + h) * 2 + j
                keep = jnp.where(refresh_ref[j, h] == 1, 0.0, 1.0)
                old_ref[row : row + 1, :] = centers_ref[b, h, j : j + 1, :]
                old_ref[SUM_ROWS + row : SUM_ROWS + row + 1, :] = jnp.full((1, dim), keep, f32)
    for b in range(samples):
        rows = slice(b * tokens, (b + 1) * tokens)
        for h in range(heads):
            head = slice(h * dim, (h + 1) * dim)
            q = qkv_ref[rows, head]
            k = split(qkv_ref[rows, width + h * dim : width + (h + 1) * dim])
            v = split(qkv_ref[rows, 2 * width + h * dim : 2 * width + (h + 1) * dim])
            scores = dot3(split(q), k, NT)
            row_max = jnp.max(scores, axis=-1, keepdims=True)
            weights = jnp.exp2(scores - row_max)
            row_sum = jnp.sum(weights, axis=-1, keepdims=True)
            near_ref[rows, head] = dot3(split(weights), v) / row_sum
            center = jnp.sum(q * centers_ref[b, h, 0:1, :], axis=-1, keepdims=True)
            rel = row_max + jnp.log(row_sum) * log2_e - center
            rel_ref[rows, head] = jnp.broadcast_to(rel, (tokens, dim))


def query_parts(query_ref, sample, heads, dim, rank):
    lanes = lane_ids(query_ref.shape[0], dim)
    if sample == 0:
        return query_ref[:, :dim].astype(f32), query_ref[:, 2 * dim :].astype(f32)
    first, second = query_ref[:, :dim].astype(f32), query_ref[:, dim : 2 * dim].astype(f32)
    turned = pltpu.roll(jnp.where(lanes < rank, second, first), dim // 2, 1)
    return second, jnp.where(lanes < heads * rank, turned, query_ref[:, 2 * dim :].astype(f32))


def code_attention(query_ref, tiles, *, samples, tokens, heads, dim, rank):
    lanes = lane_ids(tokens, dim)
    scores, values = [], []
    for b in range(samples):
        high, low = query_parts(query_ref, b, heads, dim, rank)
        stacked = []
        for h in range(heads):
            own = within(lanes, key_lane(b, h, rank), rank)
            both = [jnp.where(own, part, 0.0).astype(bf16) for part in (high, low)]
            stacked.append(jnp.concatenate(both, axis=1))
        left = jnp.concatenate(stacked, axis=0)
        codes = [ref[i, :tokens, b * dim : (b + 1) * dim] for ref, i in tiles]
        values.append(jnp.concatenate(codes, axis=0))
        parts = []
        for i in range(0, len(codes), 2):
            some = jnp.concatenate(codes[i : i + 2], axis=0)
            both = dot(left, jnp.concatenate([some, some], axis=1), NT)
            parts += [both[:, j * tokens : (j + 1) * tokens] for j in range(len(codes[i : i + 2]))]
        scores.append(parts)
    rest = jnp.concatenate([ref[i, :tokens, samples * dim :] for ref, i in tiles], axis=0)
    weights, scales, logs = [], [], []
    for b in range(samples):
        best = scores[b][0]
        for part in scores[b][1:]:
            best = jnp.maximum(best, part)
        row_max = jnp.max(best, axis=-1, keepdims=True)
        total = jnp.zeros_like(best)
        parts = []
        for part in scores[b]:
            weight = jnp.exp2(part - row_max).astype(bf16)
            total = total + weight.astype(f32)
            parts.append(weight)
        row_sum = jnp.sum(total, axis=-1, keepdims=True)
        weights.append(jnp.concatenate(parts, axis=1))
        scales.append(1.0 / row_sum)
        log = row_max + jnp.log(row_sum) * log2_e
        logs.append([log[h * tokens : (h + 1) * tokens] for h in range(heads)])
    outs = []
    for b in range(samples):
        results = [dot(weights[b][:tokens], values[b])]
        others = dot(weights[b][tokens:], rest)
        results += [others[h * tokens : (h + 1) * tokens] for h in range(heads - 1)]
        out = jnp.zeros((tokens, dim), f32)
        for h in range(heads):
            part = results[h] * scales[b][h * tokens : (h + 1) * tokens]
            out = jnp.where(within(lanes, value_lane(b, h, rank, heads), rank), part, out)
        outs.append(out)
    return outs, logs


def spread(b, logs, tokens, heads, dim, rank):
    lanes = lane_ids(tokens, dim)
    out = jnp.zeros((tokens, dim), f32)
    for h in range(heads):
        place = within(lanes, value_lane(b, h, rank, heads), rank)
        for p in range(3):
            place = place | (lanes == log_lane(b, h, p, rank))
        out = jnp.where(place, logs[h], out)
    return out


def tree_sum(parts):
    while len(parts) > 1:
        parts = [parts[i] + parts[i + 1] for i in range(0, len(parts), 2)]
    return parts[0]


def tiles_of(refs):
    return [(ref, i) for ref in refs for i in range(ref.shape[0])]


def early_kernel(query_ref, *refs, samples, tokens, heads, dim, rank):
    out_ref, log_ref = refs[-2:]
    tiles = tiles_of(refs[:-2])
    lanes = lane_ids(tokens, dim)
    outs, all_logs = code_attention(
        query_ref, tiles, samples=samples, tokens=tokens, heads=heads, dim=dim, rank=rank
    )
    for b in range(samples):
        rows = slice(b * tokens, (b + 1) * tokens)
        out, logs = outs[b], all_logs[b]
        out_ref[rows, :] = out
        log_ref[rows, :] = spread(b, logs, tokens, heads, dim, rank)


def partner_kernel(
    query_ref, part_ref, part_log_ref, *refs, order, late, samples, tokens, heads, dim, rank
):
    out_ref, half_ref = refs[-2:]
    tiles = tiles_of(refs[:-2])
    parts = []
    for place in order:
        ref, i = tiles[place]
        rows = slice(tokens, tokens + SUM_ROWS)
        pieces = [ref[i, rows, p * dim : (p + 1) * dim].astype(f32) for p in range(3)]
        parts.append(pieces[0] + (pieces[1] + pieces[2]))
    pieces = [piece.astype(f32) for piece in pieces_of(tree_sum(parts), 2)]
    half_ref[...] = pieces[0] + pieces[1]
    empty = jnp.zeros((tokens - SUM_ROWS, dim), f32)
    turned = [jnp.concatenate([piece, empty], axis=0).T for piece in pieces]
    lanes = lane_ids(tokens, dim)
    outs, all_logs = code_attention(
        query_ref, tiles[-late:], samples=samples, tokens=tokens, heads=heads, dim=dim, rank=rank
    )
    for b in range(samples):
        rows = slice(b * tokens, (b + 1) * tokens)
        out, logs = outs[b], all_logs[b]
        before, before_log = part_ref[rows, :], part_log_ref[rows, :]
        log = spread(b, logs, tokens, heads, dim, rank)
        top = jnp.maximum(log, before_log)
        new = jnp.exp2(log - top)
        whole = new + jnp.exp2(before_log - top)
        out = before + (out - before) * (new / whole)
        log = top + jnp.log(whole) * log2_e
        for p, piece in enumerate(pieces_of(log, 3)):
            place = within(lanes, log_lane(b, 0, p, rank), heads)
            out = jnp.where(place, piece.astype(f32), out)
        at = sum_lane(b, rank)
        out = jnp.where(within(lanes, at, 2 * samples * heads), pltpu.roll(turned[b], at, 1), out)
        out_ref[rows, :] = out.astype(bf16)


def own_kernel(
    query_ref, near_ref, rel_ref, old_ref, basis_h, basis_l, *refs,
    samples, tokens, heads, dim, rank,
):
    merged_ref, log_ref = refs[-2:]
    tiles = tiles_of(refs[:-2])
    lanes = lane_ids(tokens, dim)
    outs, all_logs = code_attention(
        query_ref, tiles, samples=samples, tokens=tokens, heads=heads, dim=dim, rank=rank
    )
    for b in range(samples):
        rows = slice(b * tokens, (b + 1) * tokens)
        out, logs = outs[b], all_logs[b]
        far = dot3(split(out), (basis_h[b], basis_l[b]))
        kept = jnp.zeros((tokens, dim), f32)
        for h in range(heads):
            columns = slice(h * dim, (h + 1) * dim)
            near, rel = near_ref[rows, columns], rel_ref[rows, columns]
            top = jnp.maximum(rel, logs[h])
            far_part = jnp.exp2(logs[h] - top)
            whole = jnp.exp2(rel - top) + far_part
            row = (b * heads + h) * 2 + 1
            value = far[:, columns] + old_ref[row : row + 1, :] - near
            merged_ref[rows, columns] = near + value * (far_part / whole)
            log = top + jnp.log(whole) * log2_e
            kept = jnp.where(lanes == log_lane(b, h, 0, rank), log, kept)
        log_ref[rows, :] = kept


def finish_kernel(
    back_ref, half_ref, merged_ref, log_ref, old_ref, basis_h, basis_l, w_ref,
    mixed_hbm, new_hbm, attended_ref, mixed_ref, new_ref, sem, new_sem,
    *, samples, tokens, heads, dim, rank, length,
):
    chunks, columns = mixed_ref.shape[0], mixed_ref.shape[2]
    copies = []
    sums = jnp.zeros((tokens, dim), f32)
    for b in range(samples):
        rows = slice(b * tokens, (b + 1) * tokens)
        codes = back_ref[rows, :]
        extra = codes.astype(f32)
        sums = sums + pltpu.roll(extra, dim - sum_lane(b, rank), 1)
        far_log = extra + (pltpu.roll(extra, dim - 8, 1) + pltpu.roll(extra, dim - 16, 1))
        share = 1.0 / (1.0 + jnp.exp2(log_ref[rows, :] - far_log))
        far = dot(codes, basis_h[b]) + dot(codes, basis_l[b])
        for h in range(heads):
            head = slice(h * dim, (h + 1) * dim)
            at = log_lane(b, h, 0, rank)
            row = (b * heads + h) * 2 + 1
            near = merged_ref[rows, head]
            value = far[:, head] + old_ref[row : row + 1, :] - near
            attended_ref[rows, head] = (near + value * share[:, at : at + 1]).astype(bf16)
    for c in range(chunks):
        place = slice(c * columns, (c + 1) * columns)
        mixed_ref[c] = dot(attended_ref[...], w_ref[:, place]).astype(bf16)
        copies.append(pltpu.make_async_copy(mixed_ref.at[c], mixed_hbm.at[:, place], sem.at[c]))
        copies[-1].start()
        if c == 1:
            fresh = (half_ref[...] + sums.T[:SUM_ROWS, :]) * (1.0 / length)
            fresh = jnp.where(old_ref[SUM_ROWS:, :] > 0.5, old_ref[:SUM_ROWS, :], fresh)
            for b in range(samples):
                for h in range(heads):
                    row = (b * heads + h) * 2
                    new_ref[b, h] = fresh[row : row + 2, :]
            copies.append(pltpu.make_async_copy(new_ref, new_hbm, new_sem.at[0]))
            copies[-1].start()
    for copy in copies:
        copy.wait()


VMEM = pl.BlockSpec(memory_space=pltpu.VMEM)
HBM = pl.BlockSpec(memory_space=pltpu.HBM)


def per_device(
    images, w_qkv, b_qkv, q_gain, k_gain, key_basis, value_basis, centers, refresh, w_out
):
    samples, tokens, model = images.shape
    heads, dim, rank = key_basis.shape
    seq = lax.axis_size("seq")
    rows = samples * tokens
    width = heads * dim
    sizes = dict(samples=samples, tokens=tokens, heads=heads, dim=dim)
    log_factor = log2_e / math.sqrt(dim)
    flat = images.reshape(rows, model)
    key_rows = key_basis.transpose(0, 2, 1)
    value_rows = value_basis.transpose(0, 2, 1)
    center_rows = centers.transpose(0, 2, 1, 3)
    cuts = tuple(model * i // 4 for i in range(5))
    shard = (1, tokens + SUM_ROWS, width)
    params = lambda mib: pltpu.CompilerParams(vmem_limit_bytes=mib * 2**20)

    payload, query, qkv = pl.pallas_call(
        functools.partial(project_kernel, **sizes, rank=rank, log_factor=log_factor, cuts=cuts),
        in_specs=[HBM] * 8,
        out_specs=[VMEM] * 3,
        out_shape=[
            jax.ShapeDtypeStruct(shard, bf16),
            jax.ShapeDtypeStruct((tokens, width), bf16),
            jax.ShapeDtypeStruct((rows, 3 * width), f32),
        ],
        scratch_shapes=[
            pltpu.VMEM((rows, model), bf16),
            pltpu.VMEM((model, 3 * width), bf16),
            pltpu.VMEM((3 * heads, dim), f32),
            pltpu.VMEM((1, dim), f32),
            pltpu.VMEM((1, dim), f32),
            pltpu.VMEM((heads, rank, dim), f32),
            pltpu.VMEM((heads, rank, dim), f32),
            pltpu.VMEM((samples, heads, 2, dim), f32),
            pltpu.VMEM((rows, 3 * width), f32),
            pltpu.VMEM((2 * dim, width + dim), bf16),
            pltpu.VMEM((dim, width - dim), bf16),
            pltpu.VMEM((SUM_ROWS, dim), f32),
            pltpu.SemaphoreType.DMA((2, len(cuts) - 1)),
            pltpu.SemaphoreType.DMA((6,)),
        ],
        compiler_params=params(32),
        name="project",
    )(
        *(
            pltpu.with_memory_space_constraint(x, pltpu.HBM)
            for x in (
                flat, w_qkv, b_qkv.reshape(3 * heads, dim), q_gain.reshape(1, -1),
                k_gain.reshape(1, -1), key_rows, value_rows, center_rows,
            )
        )
    )

    def swap(x, mask):
        return lax.ppermute(x, "seq", [(i, i ^ mask) for i in range(seq)])

    far_mask = seq // 2
    bits = [m for m in (2**i for i in range(1, seq.bit_length() - 1)) if m < far_mask]
    held = [(payload, [0])]
    direct = sum(bits[:2])
    for mask in range(2, 2 * direct, 2):
        if mask & ~direct == 0:
            held.append((swap(payload, mask), [mask]))
    for bit in bits[2:]:
        block = jnp.concatenate([a for a, _ in held], axis=0)
        names = [m for _, ms in held for m in ms]
        held.append((swap(block, bit), [m ^ bit for m in names]))

    query_far = swap(query, far_mask)

    near, rel, basis_high, basis_low, old = pl.pallas_call(
        functools.partial(near_kernel, **sizes, rank=rank),
        in_specs=[VMEM, VMEM, pl.BlockSpec(memory_space=pltpu.SMEM), VMEM],
        out_specs=[VMEM] * 5,
        out_shape=[
            jax.ShapeDtypeStruct((rows, width), f32),
            jax.ShapeDtypeStruct((rows, width), f32),
            jax.ShapeDtypeStruct((samples, dim, width), bf16),
            jax.ShapeDtypeStruct((samples, dim, width), bf16),
            jax.ShapeDtypeStruct((2 * SUM_ROWS, dim), f32),
        ],
        compiler_params=params(24),
        cost_estimate=pl.CostEstimate(
            flops=1200 * rows * tokens * width, bytes_accessed=50 * rows * width * 4, transcendentals=0
        ),
        name="near",
    )(qkv, center_rows, refresh, value_rows)

    for i in (1,):
        x, _ = lax.optimization_barrier((held[i][0], rel))
        held[i] = (x, held[i][1])
    early = [a for a, _ in held]
    held += [(swap(a, 1), [m ^ 1 for m in ms]) for a, ms in held]
    arrays = [a for a, _ in held]
    names = [m for _, ms in held for m in ms]
    order = tuple(names.index(m) for m in range(len(names)))
    count_early = sum(a.shape[0] for a in early)

    def cost(shards):
        return pl.CostEstimate(
            flops=8 * rows * tokens * shards * width,
            bytes_accessed=shards * 2 * tokens * width,
            transcendentals=0,
        )

    part, part_log = pl.pallas_call(
        functools.partial(early_kernel, **sizes, rank=rank),
        in_specs=[VMEM] * (1 + len(early)),
        out_specs=[VMEM] * 2,
        out_shape=[jax.ShapeDtypeStruct((rows, dim), f32)] * 2,
        compiler_params=params(32),
        cost_estimate=cost(count_early),
        name="early",
    )(query_far, *early)
    back, half = pl.pallas_call(
        functools.partial(
            partner_kernel, **sizes, rank=rank, order=order, late=len(names) - count_early
        ),
        in_specs=[VMEM] * (3 + len(arrays)),
        out_specs=[VMEM] * 2,
        out_shape=[
            jax.ShapeDtypeStruct((rows, dim), bf16),
            jax.ShapeDtypeStruct((SUM_ROWS, dim), f32),
        ],
        compiler_params=params(32),
        cost_estimate=cost(len(names)),
        name="partner",
    )(query_far, part, part_log, *arrays)
    returned = swap(back, far_mask)
    merged, logs = pl.pallas_call(
        functools.partial(own_kernel, **sizes, rank=rank),
        in_specs=[VMEM] * (5 + len(arrays)),
        out_specs=[VMEM] * 2,
        out_shape=[
            jax.ShapeDtypeStruct((rows, width), f32),
            jax.ShapeDtypeStruct((rows, dim), f32),
        ],
        compiler_params=params(32),
        cost_estimate=cost(len(names)),
        name="own",
    )(query, near, rel, old, basis_high, basis_low, *arrays[1:])

    columns = 384
    mixed, new_centers = pl.pallas_call(
        functools.partial(finish_kernel, **sizes, rank=rank, length=tokens * seq),
        in_specs=[VMEM] * 8,
        out_specs=[HBM, HBM],
        out_shape=[
            jax.ShapeDtypeStruct((rows, model), bf16),
            jax.ShapeDtypeStruct((samples, heads, 2, dim), f32),
        ],
        scratch_shapes=[
            pltpu.VMEM((rows, width), bf16),
            pltpu.VMEM((model // columns, rows, columns), bf16),
            pltpu.VMEM((samples, heads, 2, dim), f32),
            pltpu.SemaphoreType.DMA((model // columns,)),
            pltpu.SemaphoreType.DMA((1,)),
        ],
        compiler_params=params(24),
        name="finish",
    )(returned, half, merged, logs, old, basis_high, basis_low, w_out)
    return (mixed.reshape(samples, tokens, model), new_centers.transpose(0, 2, 1, 3))


def solution(mesh):
    return jax.shard_map(
        per_device,
        mesh=mesh,
        in_specs=(
            P("groups", "seq", None),
            P(),
            P(),
            P(),
            P(),
            P(),
            P(),
            P("groups", None, None, None),
            P(),
            P(),
        ),
        out_specs=(P("groups", "seq", None), P("groups", None, None, None)),
        check_vma=False,
    )
```
